256 devices in a mesh: frame: 4 (over y_lo, core), slab: 64 (over x, y_hi, z).
Axes of the slice: x: 4, y: 4 (y_hi: 2, y_lo: 2; y = y_hi * 2 + y_lo), z: 8, core: 2. Of those that a mesh axis runs over, the one named last changes fastest.
Arguments:
- element_data: bfloat16 [1024, 4, 4096], P('slab', 'frame'), may hold values from -6 to 6
- migration: bfloat16 [2048, 1024], replicated, may hold values from -0.1875 to 0.1875
- column_gain: float32 [2048], replicated, may hold values from 0.3 to 3
- depth_gain: float32 [4096], P('slab'), may hold values from 0.3 to 3
- coarse_shift: int32 [3, 4, 4, 8, 256], P(None, 'frame', None, None, 'slab'), may hold values from -8 to 8
- reference_frame: int32 [4], replicated, may hold values from 0 to 3, each once
Outputs:
- scores: float32 [7, 4, 4, 8, 256], P(None, 'frame', None, None, 'slab')
- displacement: float32 [3, 4, 4, 8, 256], P(None, 'frame', None, None, 'slab')
The draws below stay inside these ranges and needn't reach their ends.
Inputs may be any that keep to these rules, and one draw needn't show every extreme that they name: `reference_frame`: each frame index appears exactly once; the first entry names the reference frame, which serves all blocks.
All inputs are finite; a program needn't handle non-finite values.
Results may differ from the reference program's by a relative error of at most 0.0039.
Values may be sent and summed in bfloat16 or wider, within the bound.
A program may use at most 64 MiB of HBM per device.

```python
import math
import jax
import jax.numpy as jnp
from jax import lax

ELEM = 1024
LX = 32
LY = 64
KX = 8
KY = 8
KZ = 16
CMAX = 8
FRAMES = 4
DEPTH = 4096
BX = 4
BY = 8
BZ = 256


def place_ends(drawn, key, least, high):
    longest = drawn.shape.index(max(drawn.shape))
    spots = []
    for shift in (0, 1):
        where = [jax.random.randint(jax.random.fold_in(key, axis), (), 0, length) for axis, length in enumerate(drawn.shape)]
        where[longest] = (where[longest] + shift) % drawn.shape[longest]
        spots.append(tuple(where))
    return drawn.at[spots[0]].set(least).at[spots[1]].set(high)


def steps_of(own_key, dims, split, smallest, largest):
    def one(position, parts):
        draws = jax.random.uniform(jax.random.fold_in(jax.random.fold_in(own_key, 6), position), (parts,), jnp.float32, smallest / len(split), largest / len(split))
        return jnp.repeat(jnp.exp(draws), dims[position] // parts).reshape((-1,) + (1,) * (len(dims) - position - 1))

    level = one(*split[0])
    for cut in split[1:]:
        level = level * one(*cut)
    return level


def scatter_about(stream_key, shape, scale, limit, shards=(), kind=jnp.bfloat16):
    entries = scale * jax.random.normal(stream_key, shape, jnp.float32)
    if shards:
        entries = entries * steps_of(stream_key, shape, shards, -0.22, 0.18)
    return jnp.clip(entries, -limit, limit).astype(kind)


def setup_inputs(seed: int = 0) -> dict:
    key_of = jax.random.split(jax.random.key(seed), 7)
    return {
        "element_data": scatter_about(key_of[0], (ELEM, FRAMES, DEPTH), 1.0, 6.0, ((0, 64), (1, 4))),
        "migration": scatter_about(key_of[1], (LX * LY, ELEM), ELEM ** -0.5, 0.1875),
        "column_gain": jnp.clip(jnp.exp(jax.random.uniform(key_of[2], (LX * LY,), jnp.float32, math.log(0.3), math.log(3.0))), 0.3, 3.0),
        "depth_gain": jnp.clip(jnp.exp(math.log(3.0) - 2.3025851 * jax.random.uniform(key_of[3], (DEPTH,), jnp.float32) ** steps_of(key_of[3], (DEPTH,), ((0, 64),), -0.2, 0.2)), 0.3, 3.0),
        "coarse_shift": place_ends(jax.random.randint(key_of[4], (3, FRAMES, BX, BY, BZ), -CMAX, CMAX + 1), jax.random.fold_in(key_of[4], 1), -CMAX, CMAX).astype(jnp.int32),
        "reference_frame": jax.random.permutation(key_of[5], FRAMES).astype(jnp.int32),
    }


epsilon = 1e-05
shift_table = ((0, 0, 0), (-1, 0, 0), (1, 0, 0), (0, -1, 0), (0, 1, 0), (0, 0, -1), (0, 0, 1))

def block_scores(kernels, padded, starts):
    kernel_shape = kernels.shape[1:]
    box_shape = (kernel_shape[0] + 2, kernel_shape[1] + 2, kernel_shape[2] + 2)

    def take_box(first, second, third):
        return lax.dynamic_slice(padded, (first - 1, second - 1, third - 1), box_shape)
    boxes = jax.vmap(take_box)(starts[0], starts[1], starts[2])
    cell_count = kernel_shape[0] * kernel_shape[1] * kernel_shape[2]
    kernel_float = kernels.astype(jnp.float32)
    kernel_power = lax.optimization_barrier(jnp.mean(kernel_float * kernel_float, axis=(1, 2, 3)))
    results = []
    for shift_step in shift_table:
        low = [1 + shift_step[dimension] for dimension in range(3)]
        window = boxes[:, low[0]:low[0] + kernel_shape[0], low[1]:low[1] + kernel_shape[1], low[2]:low[2] + kernel_shape[2]].astype(jnp.float32)
        cross_mean = lax.optimization_barrier(jnp.mean(kernel_float * window, axis=(1, 2, 3)))
        window_power = lax.optimization_barrier(jnp.mean(window * window, axis=(1, 2, 3)))
        results.append(math.sqrt(cell_count) * cross_mean / jnp.sqrt((kernel_power + epsilon) * (window_power + epsilon)))
    return jnp.stack(results)

def refine(scores, shifts):
    refined = []
    for dimension in range(3):
        lower_score = scores[1 + 2 * dimension]
        upper_score = scores[2 + 2 * dimension]
        curvature = jnp.maximum(2.0 * scores[0] - lower_score - upper_score, 1.0)
        refined.append(shifts[dimension].astype(jnp.float32) + (upper_score - lower_score) / (2.0 * curvature))
    return jnp.stack(refined)

def reference(element_data, migration, column_gain, depth_gain, coarse_shift, reference_frame):

    def imaging(frame_number):
        samples = lax.dynamic_index_in_dim(element_data, frame_number, 1, keepdims=False)
        raw_image = jnp.dot(migration, samples, preferred_element_type=jnp.float32)
        return (raw_image * column_gain[:, None] * depth_gain[None, :]).astype(jnp.bfloat16)
    margin = CMAX + 1
    volume = imaging(reference_frame[0]).reshape(LX, LY, DEPTH)
    padded = jnp.pad(volume, margin)
    kernel_shape = (KX, KY, KZ)
    block_shape = (BX, BY, BZ)
    block_index = [lax.broadcasted_iota(jnp.int32, block_shape, dimension).reshape(-1) for dimension in range(3)]

    def per_frame(frame_number):
        image = imaging(frame_number)
        arranged = image.reshape(BX, KX, BY, KY, BZ, KZ).transpose(0, 2, 4, 1, 3, 5).reshape(-1, KX, KY, KZ)
        shifts = lax.dynamic_index_in_dim(coarse_shift, frame_number, 1, keepdims=False).reshape(3, -1)
        starts = [(block_index[dimension] * kernel_shape[dimension] + shifts[dimension] + margin).astype(jnp.int32) for dimension in range(3)]
        scores = block_scores(arranged, padded, starts)
        return (scores, refine(scores, shifts))
    scores, displacement = lax.map(per_frame, jnp.arange(FRAMES, dtype=jnp.int32))
    scores = scores.transpose(1, 0, 2).reshape(7, FRAMES, BX, BY, BZ)
    displacement = displacement.transpose(1, 0, 2).reshape(3, FRAMES, BX, BY, BZ)
    return (scores, displacement)
```

```python
import functools

import jax
import jax.numpy as jnp
from jax import lax
from jax.experimental import pallas as pl
from jax.experimental.pallas import tpu as pltpu
from jax.sharding import PartitionSpec as P

LX, LY = 32, 64
KX, KY, KZ = 8, 8, 16
MARGIN = 9
YPAD = 16
GROUP = 32
BLOCKS = 4
EPS = 1e-5
CELLS = KX * KY * KZ
ROWS = 256


def expand_gain(gain_ref, wide_ref):
    for i in range(gain_ref.shape[0]):
        row = jnp.broadcast_to(gain_ref[i : i + 1, :], (128, 128))
        wide_ref[pl.ds(i * 128, 128), :] = jnp.transpose(row)


def clear(volume_ref):
    def one(i, carry):
        volume_ref[i] = jnp.zeros(volume_ref.shape[1:], volume_ref.dtype)
        return carry

    lax.fori_loop(0, volume_ref.shape[0], one, 0)


def make_images(migration_ref, samples_ref, gain_ref, depth_ref, image_ref, volume_ref):
    planes = ROWS // LY

    def one(i, carry):
        rows = pl.ds(pl.multiple_of(i * ROWS, ROWS), ROWS)
        raw = jnp.dot(migration_ref[rows, :], samples_ref[...], preferred_element_type=jnp.float32)
        gain = gain_ref[rows, :]
        own = (raw[:, :128] * gain * depth_ref[0:1, :]).astype(jnp.bfloat16)
        image_ref[rows, :] = own.astype(jnp.float32)
        ref = (raw[:, 128:] * gain * depth_ref[1:2, :]).astype(jnp.bfloat16)
        ref = ref.astype(jnp.float32)
        for j in range(planes):
            volume_ref[MARGIN + i * planes + j, YPAD : YPAD + LY, :] = ref[j * LY : (j + 1) * LY]
        return carry

    lax.fori_loop(0, LX * LY // ROWS, one, 0)


def correlate(image_ref, volume_ref, shift_ref, parts_ref):
    lane = lax.broadcasted_iota(jnp.int32, (8, 128), 1)
    inside = lane % GROUP
    first = lane < GROUP
    third = lane < 3 * GROUP
    half = lane < 2 * GROUP
    center_mask = (inside >= 1) & (inside < 1 + KZ)
    before_mask = inside < KZ
    after_mask = (inside >= 2) & (inside < 2 + KZ)

    def one(g, carry):
        bx = g // 8
        by = g % 8
        xs, ys, turns = [], [], []
        for b in range(BLOCKS):
            xs.append(bx * KX + shift_ref[0, bx, b, by] + MARGIN)
            ys.append(by * KY + shift_ref[1, bx, b, by] + YPAD)
            turns.append((GROUP * b + 1 - MARGIN - KZ * b + 128 - shift_ref[2, bx, b, by]) % 128)

        def aligned(p, q):
            turned = [
                pltpu.roll(volume_ref[xs[b] + p, pl.ds(ys[b] + q, 8), :], turns[b], 1)
                for b in range(BLOCKS)
            ]
            return jnp.where(
                half,
                jnp.where(first, turned[0], turned[1]),
                jnp.where(third, turned[2], turned[3]),
            )

        def kernel_plane(p):
            row = pl.multiple_of((bx * KX + p) * LY + by * KY, 8)
            return image_ref[pl.ds(row, 8), :]

        zero = jnp.zeros((8, 128), jnp.float32)
        cross = [zero] * 7
        core, xm, xp, ym, yp, own = zero, zero, zero, zero, zero, zero
        for p in range(-1, KX + 1):
            window = aligned(p, 0)
            power = window * window
            if 0 <= p < KX:
                kernel = kernel_plane(p)
                own = own + kernel * kernel
                cross[0] += kernel * window
                cross[5] += pltpu.roll(kernel, 127, 1) * window
                cross[6] += pltpu.roll(kernel, 1, 1) * window
                low, high = aligned(p, -1), aligned(p, 1)
                cross[3] += kernel * low
                cross[4] += kernel * high
                ym = ym + low * low
                yp = yp + high * high
                core = core + power
            if p < KX - 1:
                cross[1] += kernel_plane(p + 1) * window
                xm = xm + power
            if p > 0:
                cross[2] += kernel_plane(p - 1) * window
                xp = xp + power
        slots = cross + [own]
        for value, mask in (
            (core, center_mask),
            (xm, center_mask),
            (xp, center_mask),
            (ym, center_mask),
            (yp, center_mask),
            (core, before_mask),
            (core, after_mask),
        ):
            slots.append(jnp.where(mask, value, 0.0))
        slots.append(own)
        for k, value in enumerate(slots):
            parts_ref[pl.ds(pl.multiple_of(k * 256 + g * 8, 8), 8), :] = value
        return carry

    lax.fori_loop(0, 32, one, 0)


def finish(parts_ref, coarse_ref, scores_ref, moved_ref):
    total = parts_ref[pl.ds(0, 512, stride=8), :]
    for s in range(1, 8):
        total = total + parts_ref[pl.ds(s, 512, stride=8), :]
    picked = lax.broadcasted_iota(jnp.int32, (8, 128), 1) // GROUP
    picked = (picked == lax.broadcasted_iota(jnp.int32, (8, 128), 0)).astype(jnp.float32)
    sums = lax.dot_general(
        picked,
        total,
        (((1,), (1,)), ((), ())),
        precision=lax.Precision.HIGHEST,
        preferred_element_type=jnp.float32,
    ) * (1.0 / CELLS)
    tiles = [sums[:, 128 * i : 128 * (i + 1)] for i in range(4)]
    lane = lax.broadcasted_iota(jnp.int32, (8, 128), 1)
    own = jnp.where(lane >= 3 * GROUP, tiles[3], 0.0)
    own = own + pltpu.roll(own, 64, 1)
    own = own + pltpu.roll(own, 32, 1) + EPS
    scored = [
        CELLS**0.5 * tiles[i] / jnp.sqrt(own * (tiles[2 + i] + EPS)) for i in range(2)
    ]
    scores = [
        scored[k // 4] if k % 4 == 0 else pltpu.roll(scored[k // 4], 128 - GROUP * (k % 4), 1)
        for k in range(7)
    ]

    def tile(value, bx):
        value = value if bx == 0 else pltpu.roll(value, 128 - 8 * bx, 1)
        return value[:BLOCKS, :8]

    for k in range(7):
        for bx in range(4):
            scores_ref[k, bx] = tile(scores[k], bx)
    for a in range(3):
        low, high = scores[1 + 2 * a], scores[2 + 2 * a]
        curvature = jnp.maximum(2.0 * scores[0] - low - high, 1.0)
        step = (high - low) / (2.0 * curvature)
        for bx in range(4):
            moved_ref[a, bx] = coarse_ref[a, bx].astype(jnp.float32) + tile(step, bx)


def local_kernel(
    shift_ref, migration_ref, samples_ref, column_ref, depth_ref, coarse_ref,
    scores_ref, moved_ref, gain_ref, image_ref, volume_ref, parts_ref,
):
    expand_gain(column_ref, gain_ref)
    clear(volume_ref)
    make_images(migration_ref, samples_ref, gain_ref, depth_ref, image_ref, volume_ref)
    correlate(image_ref, volume_ref, shift_ref, parts_ref)
    finish(parts_ref, coarse_ref, scores_ref, moved_ref)


def local_stage(migration, samples, column_gain, depth_rows, coarse):
    vmem = pl.BlockSpec(memory_space=pltpu.VMEM)
    smem = pl.BlockSpec(memory_space=pltpu.SMEM)
    return pl.pallas_call(
        local_kernel,
        out_shape=(
            jax.ShapeDtypeStruct((7, 4, 4, 8), jnp.float32),
            jax.ShapeDtypeStruct((3, 4, 4, 8), jnp.float32),
        ),
        in_specs=[smem, vmem, vmem, vmem, vmem, vmem],
        out_specs=(vmem, vmem),
        scratch_shapes=[
            pltpu.VMEM((LX * LY, 128), jnp.float32),
            pltpu.VMEM((LX * LY, 128), jnp.float32),
            pltpu.VMEM((LX + 2 * MARGIN, LY + 2 * YPAD, 128), jnp.float32),
            pltpu.VMEM((16 * 32 * 8, 128), jnp.float32),
        ],
        compiler_params=pltpu.CompilerParams(vmem_limit_bytes=40 * 2**20),
    )(coarse, migration, samples, column_gain.reshape(16, 128), depth_rows, coarse)


def with_sides(array):
    n = lax.axis_size("slab")
    up = [(i, i + 1) for i in range(n - 1)]
    down = [(i + 1, i) for i in range(n - 1)]
    before = lax.ppermute(array[:, -MARGIN:], "slab", up)
    after = lax.ppermute(array[:, :MARGIN], "slab", down)
    return jnp.concatenate([before, array, after], axis=1)


def per_device(element_data, migration, column_gain, depth_gain, coarse_shift, reference_frame):
    elements, _, depth = element_data.shape
    data = element_data.reshape(elements, depth)
    chosen = lax.axis_index("frame") == reference_frame[0]
    own = lax.all_to_all(data, "slab", split_axis=1, concat_axis=0, tiled=True)
    shared = lax.psum(jnp.where(chosen, own, 0).astype(jnp.bfloat16), "frame")
    shared = with_sides(shared)

    def spread(columns):
        groups = [
            jnp.pad(columns[:, KZ * b : KZ * (b + 1)], ((0, 0), (1, GROUP - KZ - 1)))
            for b in range(BLOCKS)
        ]
        return jnp.concatenate(groups, axis=1)

    def fill(columns):
        return jnp.pad(columns, ((0, 0), (0, 128 - columns.shape[1])))

    samples = jnp.concatenate([spread(own), fill(shared)], axis=1)
    gains = depth_gain[None, :]
    depth_rows = jnp.concatenate([spread(gains), fill(with_sides(gains))], axis=0)
    coarse = coarse_shift[:, 0].transpose(0, 1, 3, 2)
    scores, moved = local_stage(migration, samples, column_gain, depth_rows, coarse)
    return scores.transpose(0, 1, 3, 2)[:, None], moved.transpose(0, 1, 3, 2)[:, None]


def solution(mesh):
    placed = (
        P("slab", "frame", None),
        P(),
        P(),
        P("slab"),
        P(None, "frame", None, None, "slab"),
        P(),
    )
    return jax.shard_map(
        per_device,
        mesh=mesh,
        in_specs=placed,
        out_specs=(P(None, "frame", None, None, "slab"), P(None, "frame", None, None, "slab")),
        check_vma=False,
    )
```

```python
import functools

import jax
import jax.numpy as jnp
from jax import lax
from jax.experimental import pallas as pl
from jax.experimental.pallas import tpu as pltpu
from jax.sharding import PartitionSpec as P

LX, LY = 32, 64
KX, KY, KZ = 8, 8, 16
MARGIN = 9
YPAD = 16
GROUP = 32
BLOCKS = 4
EPS = 1e-5
CELLS = KX * KY * KZ
ROWS = 256
ELEMENTS = 16
MESH = pl.DeviceIdType.MESH


def expand_gain(gain_ref, wide_ref):
    for i in range(gain_ref.shape[0]):
        row = jnp.broadcast_to(gain_ref[i : i + 1, :], (128, 128))
        wide_ref[pl.ds(i * 128, 128), :] = jnp.transpose(row)


def clear(volume_ref):
    def one(i, carry):
        volume_ref[i] = jnp.zeros(volume_ref.shape[1:], volume_ref.dtype)
        return carry

    lax.fori_loop(0, volume_ref.shape[0], one, 0)


def correlate(image_ref, volume_ref, shift_ref, parts_ref):
    lane = lax.broadcasted_iota(jnp.int32, (8, 128), 1)
    inside = lane % GROUP
    first = lane < GROUP
    third = lane < 3 * GROUP
    half = lane < 2 * GROUP
    center_mask = (inside >= 1) & (inside < 1 + KZ)
    before_mask = inside < KZ
    after_mask = (inside >= 2) & (inside < 2 + KZ)

    def one(g, carry):
        bx = g // 8
        by = g % 8
        xs, ys, turns = [], [], []
        for b in range(BLOCKS):
            xs.append(bx * KX + shift_ref[0, bx, b, by] + MARGIN)
            ys.append(by * KY + shift_ref[1, bx, b, by] + YPAD)
            turns.append((GROUP * b + 1 - MARGIN - KZ * b + 128 - shift_ref[2, bx, b, by]) % 128)

        def aligned(p, q):
            turned = [
                pltpu.roll(volume_ref[xs[b] + p, pl.ds(ys[b] + q, 8), :], turns[b], 1)
                for b in range(BLOCKS)
            ]
            return jnp.where(
                half,
                jnp.where(first, turned[0], turned[1]),
                jnp.where(third, turned[2], turned[3]),
            )

        def kernel_plane(p):
            row = pl.multiple_of((bx * KX + p) * LY + by * KY, 8)
            return image_ref[pl.ds(row, 8), :]

        zero = jnp.zeros((8, 128), jnp.float32)
        cross = [zero] * 7
        core, xm, xp, ym, yp, own = zero, zero, zero, zero, zero, zero
        for p in range(-1, KX + 1):
            window = aligned(p, 0)
            power = window * window
            if 0 <= p < KX:
                kernel = kernel_plane(p)
                own = own + kernel * kernel
                cross[0] += kernel * window
                cross[5] += pltpu.roll(kernel, 127, 1) * window
                cross[6] += pltpu.roll(kernel, 1, 1) * window
                low, high = aligned(p, -1), aligned(p, 1)
                cross[3] += kernel * low
                cross[4] += kernel * high
                ym = ym + low * low
                yp = yp + high * high
                core = core + power
            if p < KX - 1:
                cross[1] += kernel_plane(p + 1) * window
                xm = xm + power
            if p > 0:
                cross[2] += kernel_plane(p - 1) * window
                xp = xp + power
        slots = cross + [own]
        for value, mask in (
            (core, center_mask),
            (xm, center_mask),
            (xp, center_mask),
            (ym, center_mask),
            (yp, center_mask),
            (core, before_mask),
            (core, after_mask),
        ):
            slots.append(jnp.where(mask, value, 0.0))
        slots.append(own)
        for k, value in enumerate(slots):
            parts_ref[pl.ds(pl.multiple_of(k * 256 + g * 8, 8), 8), :] = value
        return carry

    lax.fori_loop(0, 32, one, 0)


def finish(parts_ref, coarse_ref, scores_ref, moved_ref):
    total = parts_ref[pl.ds(0, 512, stride=8), :]
    for s in range(1, 8):
        total = total + parts_ref[pl.ds(s, 512, stride=8), :]
    picked = lax.broadcasted_iota(jnp.int32, (8, 128), 1) // GROUP
    picked = (picked == lax.broadcasted_iota(jnp.int32, (8, 128), 0)).astype(jnp.float32)
    sums = lax.dot_general(
        picked,
        total,
        (((1,), (1,)), ((), ())),
        precision=lax.Precision.HIGHEST,
        preferred_element_type=jnp.float32,
    ) * (1.0 / CELLS)
    tiles = [sums[:, 128 * i : 128 * (i + 1)] for i in range(4)]
    lane = lax.broadcasted_iota(jnp.int32, (8, 128), 1)
    own = jnp.where(lane >= 3 * GROUP, tiles[3], 0.0)
    own = own + pltpu.roll(own, 64, 1)
    own = own + pltpu.roll(own, 32, 1) + EPS
    scored = [
        CELLS**0.5 * tiles[i] / jnp.sqrt(own * (tiles[2 + i] + EPS)) for i in range(2)
    ]
    scores = [
        scored[k // 4] if k % 4 == 0 else pltpu.roll(scored[k // 4], 128 - GROUP * (k % 4), 1)
        for k in range(7)
    ]

    def tile(value, bx):
        value = value if bx == 0 else pltpu.roll(value, 128 - 8 * bx, 1)
        return value[:BLOCKS, :8]

    for k in range(7):
        for bx in range(4):
            scores_ref[k, bx] = tile(scores[k], bx)
    for a in range(3):
        low, high = scores[1 + 2 * a], scores[2 + 2 * a]
        curvature = jnp.maximum(2.0 * scores[0] - low - high, 1.0)
        step = (high - low) / (2.0 * curvature)
        for bx in range(4):
            moved_ref[a, bx] = coarse_ref[a, bx].astype(jnp.float32) + tile(step, bx)


def scaled(migration_ref, samples, gain_ref, depth_row, i):
    rows = pl.ds(pl.multiple_of(i * ROWS, ROWS), ROWS)
    raw = jnp.dot(migration_ref[rows, :], samples, preferred_element_type=jnp.float32)
    return (raw * gain_ref[rows, :] * depth_row).astype(jnp.bfloat16).astype(jnp.float32)


def make_image(migration_ref, samples_ref, gain_ref, depth_ref, image_ref):
    def one(i, carry):
        rows = pl.ds(pl.multiple_of(i * ROWS, ROWS), ROWS)
        image_ref[rows, :] = scaled(migration_ref, samples_ref[...], gain_ref, depth_ref[0:1, :], i)
        return carry

    lax.fori_loop(0, LX * LY // ROWS, one, 0)


def make_volume(migration_ref, samples_ref, gain_ref, depth_ref, volume_ref):
    planes = ROWS // LY

    def one(i, carry):
        samples = samples_ref[...].reshape(-1, 128)
        ref = scaled(migration_ref, samples, gain_ref, depth_ref[1:2, :], i)
        for j in range(planes):
            volume_ref[MARGIN + i * planes + j, YPAD : YPAD + LY, :] = ref[j * LY : (j + 1) * LY]
        return carry

    lax.fori_loop(0, LX * LY // ROWS, one, 0)


def place_of(column):
    return GROUP * (column // KZ) + 1 + column % KZ


def spread_depth(gains_ref, depth_ref):
    lane = lax.broadcasted_iota(jnp.int32, (8, 128), 1)
    left, here, right = [jnp.broadcast_to(gains_ref[i], (8, 128)) for i in range(3)]
    row = jnp.zeros((8, 128), jnp.float32)
    for b in range(BLOCKS):
        turned = pltpu.roll(here, (GROUP * b + 1 - KZ * b) % 128, 1)
        start = GROUP * b + 1
        row = jnp.where((lane >= start) & (lane < start + KZ), turned, row)
    sides = jnp.where(lane < MARGIN, pltpu.roll(left, 128 - 64 + MARGIN, 1), 0.0)
    sides = jnp.where((lane >= MARGIN) & (lane < MARGIN + 64), pltpu.roll(here, MARGIN, 1), sides)
    sides = jnp.where(
        (lane >= MARGIN + 64) & (lane < 2 * MARGIN + 64), pltpu.roll(right, MARGIN + 64, 1), sides
    )
    depth_ref[0:1, :] = row[0:1]
    depth_ref[1:2, :] = sides[0:1]


def pack_own(data_ref, send_ref):
    low = lax.broadcasted_iota(jnp.int32, (8, 128), 1) < 64
    for t in range(send_ref.shape[0] // 2):
        tile = data_ref[:, 128 * (t + 1) : 128 * (t + 2)].astype(jnp.float32)
        first, second = tile[:8], tile[8:]
        even = jnp.where(low, first, pltpu.roll(second, 64, 1))
        odd = jnp.where(low, pltpu.roll(first, 64, 1), second)
        send_ref[2 * t] = even.astype(jnp.bfloat16)
        send_ref[2 * t + 1] = odd.astype(jnp.bfloat16)


def unpack_own(recv_ref, samples_ref):
    row = lax.broadcasted_iota(jnp.int32, (128, 128), 0)
    lane = lax.broadcasted_iota(jnp.int32, (128, 128), 1)
    packed = recv_ref[...].astype(jnp.float32).reshape(-1, 128).astype(jnp.bfloat16)
    halves = []
    for start in (0, 64):
        column = row - start
        picked = (lane == place_of(column)) & (column >= 0) & (column < 64)
        picked = picked.astype(jnp.float32).astype(jnp.bfloat16)
        half = jnp.dot(packed, picked, preferred_element_type=jnp.float32)
        halves.append(half.reshape(-1, 8, 128))
    samples = jnp.concatenate(halves, axis=1).reshape(-1, 128)
    samples_ref[...] = samples.astype(jnp.bfloat16)


def pack_reference(quarters_ref, chosen, send_ref):
    lane = lax.broadcasted_iota(jnp.int32, (ELEMENTS, 128), 1)
    tiles = quarters_ref.shape[2] // 128
    parts = [quarters_ref[chosen, :, 128 * t : 128 * (t + 1)].astype(jnp.float32) for t in range(tiles)]
    for m in range(tiles - 2):
        for half in (0, 1):
            turn = MARGIN + 64 * half
            here, after = parts[m + half], parts[m + half + 1]
            window = jnp.where(lane < turn, pltpu.roll(here, turn, 1), pltpu.roll(after, turn, 1))
            send_ref[2 * m + half] = window.astype(jnp.bfloat16)


def fused_kernel(
    slabs, frames,
    shift_ref, chosen_ref, data_hbm, migration_hbm, column_ref, gains_in_ref, coarse_ref,
    scores_ref, moved_ref,
    data_ref, migration_ref, own_send, own_recv, quarters_ref, ref_send, ref_recv,
    gains_ref, gain_ref, depth_ref, samples_ref, image_ref, volume_ref, parts_ref,
    local_sems, own_sems, quarter_send_sems, quarter_recv_sems, ref_sems, gain_send_sems, gain_recv_sems,
):
    frame = lax.axis_index("frame")
    slab = lax.axis_index("slab")
    share = slabs // frames
    source = slab // share
    same = jnp.where(source == frame, 1, 0)

    gains_ref[...] = jnp.zeros(gains_ref.shape, gains_ref.dtype)
    gains_ref[1, :, :64] = gains_in_ref[...]
    barrier = pltpu.get_barrier_semaphore()

    def greet(target_frame, target_slab):
        pl.semaphore_signal(
            barrier, inc=1, device_id={"frame": target_frame, "slab": target_slab}, device_id_type=MESH
        )

    def greet_own(i, carry):
        greet(frame, (slab + 1 + i) % slabs)
        return carry

    def greet_source(i, carry):
        other = (slab + i) % slabs

        @pl.when((other != slab) | (source != frame))
        def _():
            greet(source, other)

        return carry

    for i in range(1, frames):
        greet((frame + i) % frames, slab)
    lax.fori_loop(0, slabs - 1, greet_own, 0)
    lax.fori_loop(0, slabs, greet_source, 0)

    data_ref[:, :128] = jnp.zeros((ELEMENTS, 128), data_ref.dtype)
    data_ref[:, -128:] = jnp.zeros((ELEMENTS, 128), data_ref.dtype)
    width = data_hbm.shape[1]
    load_data = pltpu.make_async_copy(data_hbm, data_ref.at[:, pl.ds(128, width)], local_sems.at[0])
    load_data.start()
    load_migration = pltpu.make_async_copy(migration_hbm, migration_ref, local_sems.at[1])
    load_migration.start()

    load_data.wait()
    pl.semaphore_wait(barrier, (frames - 1) + (slabs - 1) + slabs - same)

    quarter = width // frames

    def quarter_of(i):
        return data_ref.at[:, pl.ds(pl.multiple_of(i * quarter, 128), quarter + 256)]

    quarter_copies = []
    for i in range(1, frames):
        other = (frame + i) % frames
        copy = pltpu.make_async_remote_copy(
            src_ref=quarter_of(other),
            dst_ref=quarters_ref.at[frame],
            send_sem=quarter_send_sems.at[i - 1],
            recv_sem=quarter_recv_sems.at[i - 1],
            device_id={"frame": other},
            device_id_type=MESH,
        )
        copy.start()
        quarter_copies.append(copy)
    keep_quarter = pltpu.make_async_copy(quarter_of(frame), quarters_ref.at[frame], local_sems.at[2])
    keep_quarter.start()

    pack_own(data_ref, own_send)

    def send_own(i, carry):
        other = (slab + 1 + i) % slabs
        pltpu.make_async_remote_copy(
            src_ref=own_send.at[other],
            dst_ref=own_recv.at[slab],
            send_sem=own_sems.at[0],
            recv_sem=own_sems.at[1],
            device_id={"slab": other},
            device_id_type=MESH,
        ).start()
        return carry

    lax.fori_loop(0, slabs - 1, send_own, 0)
    pltpu.make_async_copy(own_send.at[slab], own_recv.at[slab], own_sems.at[1]).start()

    def gain_copy(way, other):
        return pltpu.make_async_remote_copy(
            src_ref=gains_ref.at[1],
            dst_ref=gains_ref.at[1 - way],
            send_sem=gain_send_sems.at[max(way, 0)],
            recv_sem=gain_recv_sems.at[max(way, 0)],
            device_id={"slab": other},
            device_id_type=MESH,
        )

    to_next = gain_copy(1, (slab + 1) % slabs)
    to_previous = gain_copy(-1, (slab + slabs - 1) % slabs)
    has_next = slab < slabs - 1
    has_previous = slab > 0
    pl.when(has_next)(to_next.start)
    pl.when(has_previous)(to_previous.start)

    for copy in quarter_copies:
        copy.wait_recv()
    keep_quarter.wait()
    pack_reference(quarters_ref, chosen_ref[0], ref_send)

    def send_reference(i, carry):
        place = (slab + i // frames) % share
        to_frame = (frame + i) % frames
        to_slab = frame * share + place
        here = (to_frame == frame) & (to_slab == slab)

        @pl.when(jnp.logical_not(here))
        def _():
            pltpu.make_async_remote_copy(
                src_ref=ref_send.at[place],
                dst_ref=ref_recv.at[slab],
                send_sem=ref_sems.at[0],
                recv_sem=ref_sems.at[1],
                device_id={"frame": to_frame, "slab": to_slab},
                device_id_type=MESH,
            ).start()

        return carry

    lax.fori_loop(0, slabs, send_reference, 0)

    @pl.when(source == frame)
    def _():
        pltpu.make_async_copy(ref_send.at[slab % share], ref_recv.at[slab], ref_sems.at[1]).start()

    expand_gain(column_ref, gain_ref)
    clear(volume_ref)
    pl.when(has_previous)(to_next.wait_recv)
    pl.when(has_next)(to_previous.wait_recv)
    spread_depth(gains_ref, depth_ref)
    load_migration.wait()
    pltpu.make_async_copy(own_recv, own_recv, own_sems.at[1]).wait()
    unpack_own(own_recv, samples_ref)
    make_image(migration_ref, samples_ref, gain_ref, depth_ref, image_ref)
    pltpu.make_async_copy(ref_recv, ref_recv, ref_sems.at[1]).wait()
    make_volume(migration_ref, ref_recv, gain_ref, depth_ref, volume_ref)
    correlate(image_ref, volume_ref, shift_ref, parts_ref)
    finish(parts_ref, coarse_ref, scores_ref, moved_ref)

    for copy in quarter_copies:
        copy.wait_send()
    pl.when(has_next)(to_next.wait_send)
    pl.when(has_previous)(to_previous.wait_send)
    most = pl.ds(0, slabs - 1)
    pltpu.make_async_copy(own_recv.at[most], own_recv.at[most], own_sems.at[0]).wait()

    @pl.when(source == frame)
    def _():
        pltpu.make_async_copy(ref_recv.at[most], ref_recv.at[most], ref_sems.at[0]).wait()

    @pl.when(source != frame)
    def _():
        pltpu.make_async_copy(ref_recv, ref_recv, ref_sems.at[0]).wait()


def per_device(slabs, frames, element_data, migration, column_gain, depth_gain, coarse_shift, reference_frame):
    elements, _, depth = element_data.shape
    data = element_data.reshape(elements, depth)
    coarse = coarse_shift[:, 0].transpose(0, 1, 3, 2)
    vmem = pl.BlockSpec(memory_space=pltpu.VMEM)
    smem = pl.BlockSpec(memory_space=pltpu.SMEM)
    hbm = pl.BlockSpec(memory_space=pl.ANY)
    bf16, f32 = jnp.bfloat16, jnp.float32
    scores, moved = pl.pallas_call(
        functools.partial(fused_kernel, slabs, frames),
        out_shape=(
            jax.ShapeDtypeStruct((7, 4, 4, 8), f32),
            jax.ShapeDtypeStruct((3, 4, 4, 8), f32),
        ),
        in_specs=[smem, smem, hbm, hbm, vmem, vmem, vmem],
        out_specs=(vmem, vmem),
        scratch_shapes=[
            pltpu.VMEM((elements, depth + 256), bf16),
            pltpu.VMEM(migration.shape, bf16),
            pltpu.VMEM((slabs, 8, 128), bf16),
            pltpu.VMEM((slabs, 8, 128), bf16),
            pltpu.VMEM((frames, elements, depth // frames + 256), bf16),
            pltpu.VMEM((slabs // frames, elements, 128), bf16),
            pltpu.VMEM((slabs, elements, 128), bf16),
            pltpu.VMEM((3, 1, 128), f32),
            pltpu.VMEM((LX * LY, 128), f32),
            pltpu.VMEM((8, 128), f32),
            pltpu.VMEM((slabs * elements, 128), bf16),
            pltpu.VMEM((LX * LY, 128), f32),
            pltpu.VMEM((LX + 2 * MARGIN, LY + 2 * YPAD, 128), f32),
            pltpu.VMEM((16 * 32 * 8, 128), f32),
            pltpu.SemaphoreType.DMA((3,)),
            pltpu.SemaphoreType.DMA((2,)),
            pltpu.SemaphoreType.DMA((frames - 1,)),
            pltpu.SemaphoreType.DMA((frames - 1,)),
            pltpu.SemaphoreType.DMA((2,)),
            pltpu.SemaphoreType.DMA((2,)),
            pltpu.SemaphoreType.DMA((2,)),
        ],
        compiler_params=pltpu.CompilerParams(
            collective_id=0, has_side_effects=True, vmem_limit_bytes=48 * 2**20
        ),
    )(coarse, reference_frame, data, migration, column_gain.reshape(16, 128), depth_gain.reshape(1, -1), coarse)
    return scores.transpose(0, 1, 3, 2)[:, None], moved.transpose(0, 1, 3, 2)[:, None]


def solution(mesh):
    placed = (
        P("slab", "frame", None),
        P(),
        P(),
        P("slab"),
        P(None, "frame", None, None, "slab"),
        P(),
    )
    return jax.shard_map(
        functools.partial(per_device, mesh.shape["slab"], mesh.shape["frame"]),
        mesh=mesh,
        in_specs=placed,
        out_specs=(P(None, "frame", None, None, "slab"), P(None, "frame", None, None, "slab")),
        check_vma=False,
    )
```

```python
import functools

import jax
import jax.numpy as jnp
from jax import lax
from jax.experimental import pallas as pl
from jax.experimental.pallas import tpu as pltpu
from jax.sharding import PartitionSpec as P

LX, LY = 32, 64
KX, KY, KZ = 8, 8, 16
MARGIN = 9
YPAD = 16
GROUP = 32
BLOCKS = 4
EPS = 1e-5
CELLS = KX * KY * KZ
ROWS = 256
ELEMENTS = 16
MESH = pl.DeviceIdType.MESH


def expand_gain(gain_ref, wide_ref):
    for i in range(gain_ref.shape[0]):
        row = jnp.broadcast_to(gain_ref[i : i + 1, :], (128, 128))
        wide_ref[pl.ds(i * 128, 128), :] = jnp.transpose(row)


def clear(volume_ref):
    def one(i, carry):
        volume_ref[i] = jnp.zeros(volume_ref.shape[1:], volume_ref.dtype)
        return carry

    lax.fori_loop(0, volume_ref.shape[0], one, 0)


def correlate(image_ref, volume_ref, shift_ref, parts_ref):
    lane = lax.broadcasted_iota(jnp.int32, (8, 128), 1)
    inside = lane % GROUP
    first = lane < GROUP
    third = lane < 3 * GROUP
    half = lane < 2 * GROUP
    center_mask = (inside >= 1) & (inside < 1 + KZ)
    before_mask = inside < KZ
    after_mask = (inside >= 2) & (inside < 2 + KZ)

    def one(g, carry):
        bx = g // 8
        by = g % 8
        xs, ys, turns = [], [], []
        for b in range(BLOCKS):
            xs.append(bx * KX + shift_ref[0, bx, b, by] + MARGIN)
            ys.append(by * KY + shift_ref[1, bx, b, by] + YPAD)
            turns.append((GROUP * b + 1 - MARGIN - KZ * b + 128 - shift_ref[2, bx, b, by]) % 128)

        def aligned(p, q):
            turned = [
                pltpu.roll(volume_ref[xs[b] + p, pl.ds(ys[b] + q, 8), :], turns[b], 1)
                for b in range(BLOCKS)
            ]
            return jnp.where(
                half,
                jnp.where(first, turned[0], turned[1]),
                jnp.where(third, turned[2], turned[3]),
            )

        def kernel_plane(p):
            row = pl.multiple_of((bx * KX + p) * LY + by * KY, 8)
            return image_ref[pl.ds(row, 8), :]

        zero = jnp.zeros((8, 128), jnp.float32)
        cross = [zero] * 7
        core, xm, xp, ym, yp, own = zero, zero, zero, zero, zero, zero
        for p in range(-1, KX + 1):
            window = aligned(p, 0)
            power = window * window
            if 0 <= p < KX:
                kernel = kernel_plane(p)
                own = own + kernel * kernel
                cross[0] += kernel * window
                cross[5] += pltpu.roll(kernel, 127, 1) * window
                cross[6] += pltpu.roll(kernel, 1, 1) * window
                low, high = aligned(p, -1), aligned(p, 1)
                cross[3] += kernel * low
                cross[4] += kernel * high
                ym = ym + low * low
                yp = yp + high * high
                core = core + power
            if p < KX - 1:
                cross[1] += kernel_plane(p + 1) * window
                xm = xm + power
            if p > 0:
                cross[2] += kernel_plane(p - 1) * window
                xp = xp + power
        slots = cross + [own]
        for value, mask in (
            (core, center_mask),
            (xm, center_mask),
            (xp, center_mask),
            (ym, center_mask),
            (yp, center_mask),
            (core, before_mask),
            (core, after_mask),
        ):
            slots.append(jnp.where(mask, value, 0.0))
        slots.append(own)
        for k, value in enumerate(slots):
            parts_ref[pl.ds(pl.multiple_of(k * 256 + g * 8, 8), 8), :] = value
        return carry

    lax.fori_loop(0, 32, one, 0)


def finish(parts_ref, coarse_ref, scores_ref, moved_ref):
    total = parts_ref[pl.ds(0, 512, stride=8), :]
    for s in range(1, 8):
        total = total + parts_ref[pl.ds(s, 512, stride=8), :]
    picked = lax.broadcasted_iota(jnp.int32, (8, 128), 1) // GROUP
    picked = (picked == lax.broadcasted_iota(jnp.int32, (8, 128), 0)).astype(jnp.float32)
    sums = lax.dot_general(
        picked,
        total,
        (((1,), (1,)), ((), ())),
        precision=lax.Precision.HIGHEST,
        preferred_element_type=jnp.float32,
    ) * (1.0 / CELLS)
    tiles = [sums[:, 128 * i : 128 * (i + 1)] for i in range(4)]
    lane = lax.broadcasted_iota(jnp.int32, (8, 128), 1)
    own = jnp.where(lane >= 3 * GROUP, tiles[3], 0.0)
    own = own + pltpu.roll(own, 64, 1)
    own = own + pltpu.roll(own, 32, 1) + EPS
    scored = [
        CELLS**0.5 * tiles[i] / jnp.sqrt(own * (tiles[2 + i] + EPS)) for i in range(2)
    ]
    scores = [
        scored[k // 4] if k % 4 == 0 else pltpu.roll(scored[k // 4], 128 - GROUP * (k % 4), 1)
        for k in range(7)
    ]

    def tile(value, bx):
        value = value if bx == 0 else pltpu.roll(value, 128 - 8 * bx, 1)
        return value[:BLOCKS, :8]

    for k in range(7):
        for bx in range(4):
            scores_ref[k, bx] = tile(scores[k], bx)
    for a in range(3):
        low, high = scores[1 + 2 * a], scores[2 + 2 * a]
        curvature = jnp.maximum(2.0 * scores[0] - low - high, 1.0)
        step = (high - low) / (2.0 * curvature)
        for bx in range(4):
            moved_ref[a, bx] = coarse_ref[a, bx].astype(jnp.float32) + tile(step, bx)


def scaled(migration_ref, samples, gain_ref, depth_row, i):
    rows = pl.ds(pl.multiple_of(i * ROWS, ROWS), ROWS)
    raw = jnp.dot(migration_ref[rows, :], samples, preferred_element_type=jnp.float32)
    return (raw * gain_ref[rows, :] * depth_row).astype(jnp.bfloat16).astype(jnp.float32)


def make_image(migration_ref, samples_ref, gain_ref, depth_ref, image_ref):
    def one(i, carry):
        rows = pl.ds(pl.multiple_of(i * ROWS, ROWS), ROWS)
        image_ref[rows, :] = scaled(migration_ref, samples_ref[...], gain_ref, depth_ref[0:1, :], i)
        return carry

    lax.fori_loop(0, LX * LY // ROWS, one, 0)


def make_volume(migration_ref, samples_ref, gain_ref, depth_ref, volume_ref):
    planes = ROWS // LY

    def one(i, carry):
        samples = samples_ref[...].reshape(-1, 128)
        ref = scaled(migration_ref, samples, gain_ref, depth_ref[1:2, :], i)
        for j in range(planes):
            volume_ref[MARGIN + i * planes + j, YPAD : YPAD + LY, :] = ref[j * LY : (j + 1) * LY]
        return carry

    lax.fori_loop(0, LX * LY // ROWS, one, 0)


def place_of(column):
    return GROUP * (column // KZ) + 1 + column % KZ


def spread_depth(gains_ref, depth_ref):
    lane = lax.broadcasted_iota(jnp.int32, (8, 128), 1)
    left, here, right = [jnp.broadcast_to(gains_ref[i], (8, 128)) for i in range(3)]
    row = jnp.zeros((8, 128), jnp.float32)
    for b in range(BLOCKS):
        turned = pltpu.roll(here, (GROUP * b + 1 - KZ * b) % 128, 1)
        start = GROUP * b + 1
        row = jnp.where((lane >= start) & (lane < start + KZ), turned, row)
    sides = jnp.where(lane < MARGIN, pltpu.roll(left, 128 - 64 + MARGIN, 1), 0.0)
    sides = jnp.where((lane >= MARGIN) & (lane < MARGIN + 64), pltpu.roll(here, MARGIN, 1), sides)
    sides = jnp.where(
        (lane >= MARGIN + 64) & (lane < 2 * MARGIN + 64), pltpu.roll(right, MARGIN + 64, 1), sides
    )
    depth_ref[0:1, :] = row[0:1]
    depth_ref[1:2, :] = sides[0:1]


def pack_own(data_ref, send_ref):
    low = lax.broadcasted_iota(jnp.int32, (8, 128), 1) < 64
    for t in range(send_ref.shape[0] // 2):
        tile = data_ref[:, 128 * (t + 1) : 128 * (t + 2)].astype(jnp.float32)
        first, second = tile[:8], tile[8:]
        even = jnp.where(low, first, pltpu.roll(second, 64, 1))
        odd = jnp.where(low, pltpu.roll(first, 64, 1), second)
        send_ref[2 * t] = even.astype(jnp.bfloat16)
        send_ref[2 * t + 1] = odd.astype(jnp.bfloat16)


def unpack_own(recv_ref, samples_ref):
    row = lax.broadcasted_iota(jnp.int32, (128, 128), 0)
    lane = lax.broadcasted_iota(jnp.int32, (128, 128), 1)
    packed = recv_ref[...].astype(jnp.float32).reshape(-1, 128).astype(jnp.bfloat16)
    halves = []
    for start in (0, 64):
        column = row - start
        picked = (lane == place_of(column)) & (column >= 0) & (column < 64)
        picked = picked.astype(jnp.float32).astype(jnp.bfloat16)
        half = jnp.dot(packed, picked, preferred_element_type=jnp.float32)
        halves.append(half.reshape(-1, 8, 128))
    samples = jnp.concatenate(halves, axis=1).reshape(-1, 128)
    samples_ref[...] = samples.astype(jnp.bfloat16)


def pack_reference(quarters_ref, chosen, send_ref):
    lane = lax.broadcasted_iota(jnp.int32, (ELEMENTS, 128), 1)
    tiles = quarters_ref.shape[2] // 128
    parts = [quarters_ref[chosen, :, 128 * t : 128 * (t + 1)].astype(jnp.float32) for t in range(tiles)]
    for m in range(tiles - 2):
        for half in (0, 1):
            turn = MARGIN + 64 * half
            here, after = parts[m + half], parts[m + half + 1]
            window = jnp.where(lane < turn, pltpu.roll(here, turn, 1), pltpu.roll(after, turn, 1))
            send_ref[2 * m + half] = window.astype(jnp.bfloat16)


def fused_kernel(
    slabs, frames,
    shift_hbm, chosen_hbm, data_hbm, migration_hbm, column_hbm, gains_hbm,
    scores_ref, moved_ref,
    shift_ref, chosen_ref, coarse_ref, column_ref, gains_in_ref,
    data_ref, migration_ref, own_send, own_recv, quarters_ref, ref_send, ref_recv,
    gains_ref, gain_ref, depth_ref, samples_ref, image_ref, volume_ref, parts_ref,
    local_sems, own_sems, quarter_send_sems, quarter_recv_sems, ref_sems, gain_send_sems, gain_recv_sems,
):
    frame = lax.axis_index("frame")
    slab = lax.axis_index("slab")
    share = slabs // frames
    source = slab // share
    same = jnp.where(source == frame, 1, 0)

    width = data_hbm.shape[1]
    loads = [
        pltpu.make_async_copy(start, end, local_sems.at[i])
        for i, (start, end) in enumerate(
            (
                (data_hbm, data_ref.at[:, pl.ds(128, width)]),
                (gains_hbm, gains_in_ref),
                (chosen_hbm, chosen_ref),
                (migration_hbm, migration_ref),
                (column_hbm, column_ref),
                (shift_hbm, shift_ref),
                (shift_hbm, coarse_ref),
            )
        )
    ]
    for copy in loads:
        copy.start()
    gains_ref[...] = jnp.zeros(gains_ref.shape, gains_ref.dtype)
    barrier = pltpu.get_barrier_semaphore()

    def greet(target_frame, target_slab):
        pl.semaphore_signal(
            barrier, inc=1, device_id={"frame": target_frame, "slab": target_slab}, device_id_type=MESH
        )

    def greet_own(i, carry):
        greet(frame, (slab + 1 + i) % slabs)
        return carry

    def greet_source(i, carry):
        other = (slab + i) % slabs

        @pl.when((other != slab) | (source != frame))
        def _():
            greet(source, other)

        return carry

    for i in range(1, frames):
        greet((frame + i) % frames, slab)
    lax.fori_loop(0, slabs - 1, greet_own, 0)
    lax.fori_loop(0, slabs, greet_source, 0)

    data_ref[:, :128] = jnp.zeros((ELEMENTS, 128), data_ref.dtype)
    data_ref[:, -128:] = jnp.zeros((ELEMENTS, 128), data_ref.dtype)
    for copy in loads[:3]:
        copy.wait()
    gains_ref[1, :, :64] = gains_in_ref[...]
    pl.semaphore_wait(barrier, (frames - 1) + (slabs - 1) + slabs - same)

    quarter = width // frames

    def quarter_of(i):
        return data_ref.at[:, pl.ds(pl.multiple_of(i * quarter, 128), quarter + 256)]

    quarter_copies = []
    for i in range(1, frames):
        other = (frame + i) % frames
        copy = pltpu.make_async_remote_copy(
            src_ref=quarter_of(other),
            dst_ref=quarters_ref.at[frame],
            send_sem=quarter_send_sems.at[i - 1],
            recv_sem=quarter_recv_sems.at[i - 1],
            device_id={"frame": other},
            device_id_type=MESH,
        )
        copy.start()
        quarter_copies.append(copy)
    keep_quarter = pltpu.make_async_copy(quarter_of(frame), quarters_ref.at[frame], local_sems.at[7])
    keep_quarter.start()

    pack_own(data_ref, own_send)

    def send_own(i, carry):
        other = (slab + 1 + i) % slabs
        pltpu.make_async_remote_copy(
            src_ref=own_send.at[other],
            dst_ref=own_recv.at[slab],
            send_sem=own_sems.at[0],
            recv_sem=own_sems.at[1],
            device_id={"slab": other},
            device_id_type=MESH,
        ).start()
        return carry

    lax.fori_loop(0, slabs - 1, send_own, 0)
    pltpu.make_async_copy(own_send.at[slab], own_recv.at[slab], own_sems.at[1]).start()

    def gain_copy(way, other):
        return pltpu.make_async_remote_copy(
            src_ref=gains_ref.at[1],
            dst_ref=gains_ref.at[1 - way],
            send_sem=gain_send_sems.at[max(way, 0)],
            recv_sem=gain_recv_sems.at[max(way, 0)],
            device_id={"slab": other},
            device_id_type=MESH,
        )

    to_next = gain_copy(1, (slab + 1) % slabs)
    to_previous = gain_copy(-1, (slab + slabs - 1) % slabs)
    has_next = slab < slabs - 1
    has_previous = slab > 0
    pl.when(has_next)(to_next.start)
    pl.when(has_previous)(to_previous.start)

    for copy in quarter_copies:
        copy.wait_recv()
    keep_quarter.wait()
    pack_reference(quarters_ref, chosen_ref[0], ref_send)

    def send_reference(i, carry):
        place = (slab + i // frames) % share
        to_frame = (frame + i) % frames
        to_slab = frame * share + place
        here = (to_frame == frame) & (to_slab == slab)

        @pl.when(jnp.logical_not(here))
        def _():
            pltpu.make_async_remote_copy(
                src_ref=ref_send.at[place],
                dst_ref=ref_recv.at[slab],
                send_sem=ref_sems.at[0],
                recv_sem=ref_sems.at[1],
                device_id={"frame": to_frame, "slab": to_slab},
                device_id_type=MESH,
            ).start()

        return carry

    lax.fori_loop(0, slabs, send_reference, 0)

    @pl.when(source == frame)
    def _():
        pltpu.make_async_copy(ref_send.at[slab % share], ref_recv.at[slab], ref_sems.at[1]).start()

    for copy in loads[3:]:
        copy.wait()
    expand_gain(column_ref, gain_ref)
    clear(volume_ref)
    pl.when(has_previous)(to_next.wait_recv)
    pl.when(has_next)(to_previous.wait_recv)
    spread_depth(gains_ref, depth_ref)
    pltpu.make_async_copy(own_recv, own_recv, own_sems.at[1]).wait()
    unpack_own(own_recv, samples_ref)
    make_image(migration_ref, samples_ref, gain_ref, depth_ref, image_ref)
    pltpu.make_async_copy(ref_recv, ref_recv, ref_sems.at[1]).wait()
    make_volume(migration_ref, ref_recv, gain_ref, depth_ref, volume_ref)
    correlate(image_ref, volume_ref, shift_ref, parts_ref)
    finish(parts_ref, coarse_ref, scores_ref, moved_ref)

    for copy in quarter_copies:
        copy.wait_send()
    pl.when(has_next)(to_next.wait_send)
    pl.when(has_previous)(to_previous.wait_send)
    most = pl.ds(0, slabs - 1)
    pltpu.make_async_copy(own_recv.at[most], own_recv.at[most], own_sems.at[0]).wait()

    @pl.when(source == frame)
    def _():
        pltpu.make_async_copy(ref_recv.at[most], ref_recv.at[most], ref_sems.at[0]).wait()

    @pl.when(source != frame)
    def _():
        pltpu.make_async_copy(ref_recv, ref_recv, ref_sems.at[0]).wait()


def per_device(slabs, frames, element_data, migration, column_gain, depth_gain, coarse_shift, reference_frame):
    elements, _, depth = element_data.shape
    data = element_data.reshape(elements, depth)
    coarse = coarse_shift[:, 0].transpose(0, 1, 3, 2)
    vmem = pl.BlockSpec(memory_space=pltpu.VMEM)
    hbm = pl.BlockSpec(memory_space=pltpu.HBM)
    bf16, f32 = jnp.bfloat16, jnp.float32
    operands = (coarse, reference_frame, data, migration, column_gain.reshape(16, 128), depth_gain.reshape(1, -1))
    scores, moved = pl.pallas_call(
        functools.partial(fused_kernel, slabs, frames),
        out_shape=(
            jax.ShapeDtypeStruct((7, 4, 4, 8), f32),
            jax.ShapeDtypeStruct((3, 4, 4, 8), f32),
        ),
        in_specs=[hbm] * 6,
        out_specs=(vmem, vmem),
        scratch_shapes=[
            pltpu.SMEM(coarse.shape, jnp.int32),
            pltpu.SMEM(reference_frame.shape, jnp.int32),
            pltpu.VMEM(coarse.shape, jnp.int32),
            pltpu.VMEM((16, 128), f32),
            pltpu.VMEM((1, depth_gain.shape[0]), f32),
            pltpu.VMEM((elements, depth + 256), bf16),
            pltpu.VMEM(migration.shape, bf16),
            pltpu.VMEM((slabs, 8, 128), bf16),
            pltpu.VMEM((slabs, 8, 128), bf16),
            pltpu.VMEM((frames, elements, depth // frames + 256), bf16),
            pltpu.VMEM((slabs // frames, elements, 128), bf16),
            pltpu.VMEM((slabs, elements, 128), bf16),
            pltpu.VMEM((3, 1, 128), f32),
            pltpu.VMEM((LX * LY, 128), f32),
            pltpu.VMEM((8, 128), f32),
            pltpu.VMEM((slabs * elements, 128), bf16),
            pltpu.VMEM((LX * LY, 128), f32),
            pltpu.VMEM((LX + 2 * MARGIN, LY + 2 * YPAD, 128), f32),
            pltpu.VMEM((16 * 32 * 8, 128), f32),
            pltpu.SemaphoreType.DMA((8,)),
            pltpu.SemaphoreType.DMA((2,)),
            pltpu.SemaphoreType.DMA((frames - 1,)),
            pltpu.SemaphoreType.DMA((frames - 1,)),
            pltpu.SemaphoreType.DMA((2,)),
            pltpu.SemaphoreType.DMA((2,)),
            pltpu.SemaphoreType.DMA((2,)),
        ],
        compiler_params=pltpu.CompilerParams(
            collective_id=0, has_side_effects=True, vmem_limit_bytes=48 * 2**20
        ),
    )(*[pltpu.with_memory_space_constraint(x, pltpu.HBM) for x in operands])
    return scores.transpose(0, 1, 3, 2)[:, None], moved.transpose(0, 1, 3, 2)[:, None]


def solution(mesh):
    placed = (
        P("slab", "frame", None),
        P(),
        P(),
        P("slab"),
        P(None, "frame", None, None, "slab"),
        P(),
    )
    return jax.shard_map(
        functools.partial(per_device, mesh.shape["slab"], mesh.shape["frame"]),
        mesh=mesh,
        in_specs=placed,
        out_specs=(P(None, "frame", None, None, "slab"), P(None, "frame", None, None, "slab")),
        check_vma=False,
    )
```

```python
import functools

import jax
import jax.numpy as jnp
from jax import lax
from jax.experimental import pallas as pl
from jax.experimental.pallas import tpu as pltpu
from jax.sharding import PartitionSpec as P

LX, LY = 32, 64
KX, KY, KZ = 8, 8, 16
MARGIN = 9
YPAD = 16
YROWS = LY + 2 * YPAD
PLANES = LX + 2 * MARGIN
GROUP = 32
BLOCKS = 4
EPS = 1e-5
CELLS = KX * KY * KZ
ROWS = 1024
ELEMENTS = 16
MESH = pl.DeviceIdType.MESH


def expand_gain(gain_ref, wide_ref):
    for i in range(gain_ref.shape[0]):
        row = jnp.broadcast_to(gain_ref[i : i + 1, :], (128, 128))
        wide_ref[pl.ds(i * 128, 128), :] = jnp.transpose(row)


def clear(volume_ref):
    def one(i, carry):
        rows = pl.ds(pl.multiple_of(i * YROWS, 8), YROWS)
        volume_ref[rows, :] = jnp.zeros((YROWS, 128), volume_ref.dtype)
        return carry

    lax.fori_loop(0, PLANES, one, 0)


def correlate(image_ref, volume_ref, shift_ref, parts_ref):
    lane = lax.broadcasted_iota(jnp.int32, (8, 128), 1)
    row = lax.broadcasted_iota(jnp.int32, (8, 128), 0)
    inside = lane % GROUP
    first = lane < GROUP
    third = lane < 3 * GROUP
    half = lane < 2 * GROUP
    center_mask = (inside >= 1) & (inside < 1 + KZ)
    before_mask = inside < KZ
    after_mask = (inside >= 2) & (inside < 2 + KZ)

    def one(g, carry):
        bx = g // 8
        by = g % 8
        starts, turns = [], []
        for b in range(BLOCKS):
            plane = bx * KX + shift_ref[0, bx, b, by] + MARGIN
            starts.append(plane * YROWS + by * KY + shift_ref[1, bx, b, by] + YPAD)
            turns.append((GROUP * b + 1 - MARGIN - KZ * b + 128 - shift_ref[2, bx, b, by]) % 128)

        def aligned(rows):
            turned = [pltpu.roll(volume_ref[rows(starts[b]), :], turns[b], 1) for b in range(BLOCKS)]
            return jnp.where(
                half,
                jnp.where(first, turned[0], turned[1]),
                jnp.where(third, turned[2], turned[3]),
            )

        base = bx * (KX * LY) + by * KY

        def kernel_plane(kind, p):
            return image_ref[kind, pl.ds(pl.multiple_of(base + p * LY, 8), 8), :]

        zero = jnp.zeros((8, 128), jnp.float32)
        cross = [zero] * 7
        core, own = zero, zero
        kernels = [kernel_plane(0, p) for p in range(KX)]
        for p in range(-1, KX + 1):
            window = aligned(lambda start: pl.ds(start + p * YROWS, 8))
            power = window * window
            if p == -1:
                ahead = power
            elif p == KX:
                behind = power
            else:
                own = own + kernels[p] * kernels[p]
                cross[0] += kernels[p] * window
                for kind in range(1, 5):
                    cross[2 + kind] += kernel_plane(kind, p) * window
                core = core + power
                if p == 0:
                    low_end = power
                if p == KX - 1:
                    high_end = power
                if 0 < p < KX - 1:
                    middle = power if p == 1 else middle + power
            if p < KX - 1:
                cross[1] += kernels[p + 1] * window
            if p > 0:
                cross[2] += kernels[p - 1] * window
        xm = ahead + low_end + middle
        xp = middle + high_end + behind
        low = aligned(lambda start: pl.ds(start - 1, KX, stride=YROWS))
        high = aligned(lambda start: pl.ds(start + KY, KX, stride=YROWS))
        cross[3] += image_ref[0, pl.ds(base, KX, stride=LY), :] * low
        cross[4] += image_ref[0, pl.ds(base + KY - 1, KX, stride=LY), :] * high
        ym = jnp.where(row < KY - 1, core, 0.0) + low * low
        yp = jnp.where(row > 0, core, 0.0) + high * high
        slots = cross + [own]
        for value, mask in (
            (core, center_mask),
            (xm, center_mask),
            (xp, center_mask),
            (ym, center_mask),
            (yp, center_mask),
            (core, before_mask),
            (core, after_mask),
        ):
            slots.append(jnp.where(mask, value, 0.0))
        slots.append(own)
        for k, value in enumerate(slots):
            parts_ref[pl.ds(pl.multiple_of(k * 256 + g * 8, 8), 8), :] = value
        return carry

    lax.fori_loop(0, 32, one, 0, unroll=4)


def finish(parts_ref, coarse_ref, scores_ref, moved_ref):
    total = parts_ref[pl.ds(0, 512, stride=8), :]
    for s in range(1, 8):
        total = total + parts_ref[pl.ds(s, 512, stride=8), :]
    picked = lax.broadcasted_iota(jnp.int32, (8, 128), 1) // GROUP
    picked = (picked == lax.broadcasted_iota(jnp.int32, (8, 128), 0)).astype(jnp.float32)
    sums = lax.dot_general(
        picked,
        total,
        (((1,), (1,)), ((), ())),
        precision=lax.Precision.HIGHEST,
        preferred_element_type=jnp.float32,
    ) * (1.0 / CELLS)
    tiles = [sums[:, 128 * i : 128 * (i + 1)] for i in range(4)]
    lane = lax.broadcasted_iota(jnp.int32, (8, 128), 1)
    own = jnp.where(lane >= 3 * GROUP, tiles[3], 0.0)
    own = own + pltpu.roll(own, 64, 1)
    own = own + pltpu.roll(own, 32, 1) + EPS
    scored = [
        CELLS**0.5 * tiles[i] / jnp.sqrt(own * (tiles[2 + i] + EPS)) for i in range(2)
    ]
    scores = [
        scored[k // 4] if k % 4 == 0 else pltpu.roll(scored[k // 4], 128 - GROUP * (k % 4), 1)
        for k in range(7)
    ]

    def tile(value, bx):
        value = value if bx == 0 else pltpu.roll(value, 128 - 8 * bx, 1)
        return value[:BLOCKS, :8]

    for k in range(7):
        for bx in range(4):
            scores_ref[k, bx] = tile(scores[k], bx)
    for a in range(3):
        low, high = scores[1 + 2 * a], scores[2 + 2 * a]
        curvature = jnp.maximum(2.0 * scores[0] - low - high, 1.0)
        step = (high - low) / (2.0 * curvature)
        for bx in range(4):
            moved_ref[a, bx] = coarse_ref[a, bx].astype(jnp.float32) + tile(step, bx)


def scaled(migration_ref, samples, gain_ref, depth_row, i):
    rows = pl.ds(pl.multiple_of(i * ROWS, ROWS), ROWS)
    raw = jnp.dot(migration_ref[rows, :], samples, preferred_element_type=jnp.float32)
    return (raw * gain_ref[rows, :] * depth_row).astype(jnp.bfloat16).astype(jnp.float32)


def make_image(migration_ref, samples_ref, gain_ref, depth_ref, image_ref):
    def one(i, carry):
        rows = pl.ds(pl.multiple_of(i * ROWS, ROWS), ROWS)
        image = scaled(migration_ref, samples_ref[...], gain_ref, depth_ref[0:1, :], i)
        tiles = image.reshape(-1, 8, 128)
        row = lax.broadcasted_iota(jnp.int32, tiles.shape, 1)
        image_ref[0, rows, :] = image
        image_ref[1, rows, :] = jnp.where(row < 7, pltpu.roll(tiles, 7, 1), 0.0).reshape(-1, 128)
        image_ref[2, rows, :] = jnp.where(row > 0, pltpu.roll(tiles, 1, 1), 0.0).reshape(-1, 128)
        image_ref[3, rows, :] = pltpu.roll(image, 127, 1)
        image_ref[4, rows, :] = pltpu.roll(image, 1, 1)
        return carry

    lax.fori_loop(0, LX * LY // ROWS, one, 0)


def make_volume(migration_ref, samples_ref, gain_ref, depth_ref, volume_ref):
    planes = ROWS // LY

    def one(i, carry):
        samples = samples_ref[...].reshape(-1, 128)
        ref = scaled(migration_ref, samples, gain_ref, depth_ref[1:2, :], i)
        for j in range(planes):
            place = pl.multiple_of((MARGIN + i * planes + j) * YROWS + YPAD, 8)
            volume_ref[pl.ds(place, LY), :] = ref[j * LY : (j + 1) * LY]
        return carry

    lax.fori_loop(0, LX * LY // ROWS, one, 0)


def place_of(column):
    return GROUP * (column // KZ) + 1 + column % KZ


def spread_depth(gains_ref, depth_ref):
    lane = lax.broadcasted_iota(jnp.int32, (8, 128), 1)
    left, here, right = [jnp.broadcast_to(gains_ref[i], (8, 128)) for i in range(3)]
    row = jnp.zeros((8, 128), jnp.float32)
    for b in range(BLOCKS):
        turned = pltpu.roll(here, (GROUP * b + 1 - KZ * b) % 128, 1)
        start = GROUP * b + 1
        row = jnp.where((lane >= start) & (lane < start + KZ), turned, row)
    sides = jnp.where(lane < MARGIN, pltpu.roll(left, 128 - 64 + MARGIN, 1), 0.0)
    sides = jnp.where((lane >= MARGIN) & (lane < MARGIN + 64), pltpu.roll(here, MARGIN, 1), sides)
    sides = jnp.where(
        (lane >= MARGIN + 64) & (lane < 2 * MARGIN + 64), pltpu.roll(right, MARGIN + 64, 1), sides
    )
    depth_ref[0:1, :] = row[0:1]
    depth_ref[1:2, :] = sides[0:1]


def pack_own(data_ref, send_ref):
    low = lax.broadcasted_iota(jnp.int32, (8, 128), 1) < 64
    for t in range(send_ref.shape[0] // 2):
        tile = data_ref[:, 128 * (t + 1) : 128 * (t + 2)].astype(jnp.float32)
        first, second = tile[:8], tile[8:]
        even = jnp.where(low, first, pltpu.roll(second, 64, 1))
        odd = jnp.where(low, pltpu.roll(first, 64, 1), second)
        send_ref[2 * t] = even.astype(jnp.bfloat16)
        send_ref[2 * t + 1] = odd.astype(jnp.bfloat16)


def unpack_own(recv_ref, samples_ref):
    row = lax.broadcasted_iota(jnp.int32, (128, 128), 0)
    lane = lax.broadcasted_iota(jnp.int32, (128, 128), 1)
    packed = recv_ref[...].astype(jnp.float32).reshape(-1, 128).astype(jnp.bfloat16)
    halves = []
    for start in (0, 64):
        column = row - start
        picked = (lane == place_of(column)) & (column >= 0) & (column < 64)
        picked = picked.astype(jnp.float32).astype(jnp.bfloat16)
        half = jnp.dot(packed, picked, preferred_element_type=jnp.float32)
        halves.append(half.reshape(-1, 8, 128))
    samples = jnp.concatenate(halves, axis=1).reshape(-1, 128)
    samples_ref[...] = samples.astype(jnp.bfloat16)


def pack_reference(quarters_ref, chosen, send_ref):
    lane = lax.broadcasted_iota(jnp.int32, (ELEMENTS, 128), 1)
    tiles = quarters_ref.shape[2] // 128
    parts = [quarters_ref[chosen, :, 128 * t : 128 * (t + 1)].astype(jnp.float32) for t in range(tiles)]
    for m in range(tiles - 2):
        for half in (0, 1):
            turn = MARGIN + 64 * half
            here, after = parts[m + half], parts[m + half + 1]
            window = jnp.where(lane < turn, pltpu.roll(here, turn, 1), pltpu.roll(after, turn, 1))
            send_ref[2 * m + half] = window.astype(jnp.bfloat16)


def fused_kernel(
    slabs, frames,
    shift_hbm, chosen_hbm, data_hbm, migration_hbm, column_hbm, gains_hbm,
    scores_ref, moved_ref,
    shift_ref, chosen_ref, coarse_ref, column_ref, gains_in_ref,
    data_ref, migration_ref, own_send, own_recv, quarters_ref, ref_send, ref_recv,
    gains_ref, gain_ref, depth_ref, samples_ref, image_ref, volume_ref, parts_ref,
    local_sems, own_sems, quarter_send_sems, quarter_recv_sems, ref_sems, gain_send_sems, gain_recv_sems,
):
    frame = lax.axis_index("frame")
    slab = lax.axis_index("slab")
    share = slabs // frames
    source = slab // share
    same = jnp.where(source == frame, 1, 0)

    width = data_hbm.shape[1]
    loads = [
        pltpu.make_async_copy(start, end, local_sems.at[i])
        for i, (start, end) in enumerate(
            (
                (data_hbm, data_ref.at[:, pl.ds(128, width)]),
                (gains_hbm, gains_in_ref),
                (chosen_hbm, chosen_ref),
                (migration_hbm, migration_ref),
                (column_hbm, column_ref),
                (shift_hbm, shift_ref),
                (shift_hbm, coarse_ref),
            )
        )
    ]
    for copy in loads:
        copy.start()
    gains_ref[...] = jnp.zeros(gains_ref.shape, gains_ref.dtype)
    barrier = pltpu.get_barrier_semaphore()

    def greet(target_frame, target_slab):
        pl.semaphore_signal(
            barrier, inc=1, device_id={"frame": target_frame, "slab": target_slab}, device_id_type=MESH
        )

    def greet_own(i, carry):
        greet(frame, (slab + 1 + i) % slabs)
        return carry

    def greet_source(i, carry):
        other = (slab + i) % slabs

        @pl.when((other != slab) | (source != frame))
        def _():
            greet(source, other)

        return carry

    for i in range(1, frames):
        greet((frame + i) % frames, slab)
    lax.fori_loop(0, slabs - 1, greet_own, 0)
    lax.fori_loop(0, slabs, greet_source, 0)

    data_ref[:, :128] = jnp.zeros((ELEMENTS, 128), data_ref.dtype)
    data_ref[:, -128:] = jnp.zeros((ELEMENTS, 128), data_ref.dtype)
    for copy in loads[:3]:
        copy.wait()
    gains_ref[1, :, :64] = gains_in_ref[...]
    pl.semaphore_wait(barrier, (frames - 1) + (slabs - 1) + slabs - same)

    quarter = width // frames

    def quarter_of(i):
        return data_ref.at[:, pl.ds(pl.multiple_of(i * quarter, 128), quarter + 256)]

    quarter_copies = []
    for i in range(1, frames):
        other = (frame + i) % frames
        copy = pltpu.make_async_remote_copy(
            src_ref=quarter_of(other),
            dst_ref=quarters_ref.at[frame],
            send_sem=quarter_send_sems.at[i - 1],
            recv_sem=quarter_recv_sems.at[i - 1],
            device_id={"frame": other},
            device_id_type=MESH,
        )
        copy.start()
        quarter_copies.append(copy)
    keep_quarter = pltpu.make_async_copy(quarter_of(frame), quarters_ref.at[frame], local_sems.at[7])
    keep_quarter.start()

    pack_own(data_ref, own_send)

    def send_own(i, carry):
        other = (slab + 1 + i) % slabs
        pltpu.make_async_remote_copy(
            src_ref=own_send.at[other],
            dst_ref=own_recv.at[slab],
            send_sem=own_sems.at[0],
            recv_sem=own_sems.at[1],
            device_id={"slab": other},
            device_id_type=MESH,
        ).start()
        return carry

    lax.fori_loop(0, slabs - 1, send_own, 0)
    pltpu.make_async_copy(own_send.at[slab], own_recv.at[slab], own_sems.at[1]).start()

    def gain_copy(way, other):
        return pltpu.make_async_remote_copy(
            src_ref=gains_ref.at[1],
            dst_ref=gains_ref.at[1 - way],
            send_sem=gain_send_sems.at[max(way, 0)],
            recv_sem=gain_recv_sems.at[max(way, 0)],
            device_id={"slab": other},
            device_id_type=MESH,
        )

    to_next = gain_copy(1, (slab + 1) % slabs)
    to_previous = gain_copy(-1, (slab + slabs - 1) % slabs)
    has_next = slab < slabs - 1
    has_previous = slab > 0
    pl.when(has_next)(to_next.start)
    pl.when(has_previous)(to_previous.start)

    for copy in quarter_copies:
        copy.wait_recv()
    keep_quarter.wait()
    pack_reference(quarters_ref, chosen_ref[0], ref_send)

    def send_reference(i, carry):
        place = (slab + i // frames) % share
        to_frame = (frame + i) % frames
        to_slab = frame * share + place
        here = (to_frame == frame) & (to_slab == slab)

        @pl.when(jnp.logical_not(here))
        def _():
            pltpu.make_async_remote_copy(
                src_ref=ref_send.at[place],
                dst_ref=ref_recv.at[slab],
                send_sem=ref_sems.at[0],
                recv_sem=ref_sems.at[1],
                device_id={"frame": to_frame, "slab": to_slab},
                device_id_type=MESH,
            ).start()

        return carry

    lax.fori_loop(0, slabs, send_reference, 0)

    @pl.when(source == frame)
    def _():
        pltpu.make_async_copy(ref_send.at[slab % share], ref_recv.at[slab], ref_sems.at[1]).start()

    for copy in loads[3:]:
        copy.wait()
    expand_gain(column_ref, gain_ref)
    clear(volume_ref)
    pl.when(has_previous)(to_next.wait_recv)
    pl.when(has_next)(to_previous.wait_recv)
    spread_depth(gains_ref, depth_ref)
    pltpu.make_async_copy(own_recv, own_recv, own_sems.at[1]).wait()
    unpack_own(own_recv, samples_ref)
    make_image(migration_ref, samples_ref, gain_ref, depth_ref, image_ref)
    pltpu.make_async_copy(ref_recv, ref_recv, ref_sems.at[1]).wait()
    make_volume(migration_ref, ref_recv, gain_ref, depth_ref, volume_ref)
    correlate(image_ref, volume_ref, shift_ref, parts_ref)
    finish(parts_ref, coarse_ref, scores_ref, moved_ref)

    for copy in quarter_copies:
        copy.wait_send()
    pl.when(has_next)(to_next.wait_send)
    pl.when(has_previous)(to_previous.wait_send)
    most = pl.ds(0, slabs - 1)
    pltpu.make_async_copy(own_recv.at[most], own_recv.at[most], own_sems.at[0]).wait()

    @pl.when(source == frame)
    def _():
        pltpu.make_async_copy(ref_recv.at[most], ref_recv.at[most], ref_sems.at[0]).wait()

    @pl.when(source != frame)
    def _():
        pltpu.make_async_copy(ref_recv, ref_recv, ref_sems.at[0]).wait()


def per_device(slabs, frames, element_data, migration, column_gain, depth_gain, coarse_shift, reference_frame):
    elements, _, depth = element_data.shape
    data = element_data.reshape(elements, depth)
    coarse = coarse_shift[:, 0].transpose(0, 1, 3, 2)
    vmem = pl.BlockSpec(memory_space=pltpu.VMEM)
    hbm = pl.BlockSpec(memory_space=pltpu.HBM)
    bf16, f32 = jnp.bfloat16, jnp.float32
    operands = (coarse, reference_frame, data, migration, column_gain.reshape(16, 128), depth_gain.reshape(1, -1))
    scores, moved = pl.pallas_call(
        functools.partial(fused_kernel, slabs, frames),
        out_shape=(
            jax.ShapeDtypeStruct((7, 4, 4, 8), f32),
            jax.ShapeDtypeStruct((3, 4, 4, 8), f32),
        ),
        in_specs=[hbm] * 6,
        out_specs=(vmem, vmem),
        scratch_shapes=[
            pltpu.SMEM(coarse.shape, jnp.int32),
            pltpu.SMEM(reference_frame.shape, jnp.int32),
            pltpu.VMEM(coarse.shape, jnp.int32),
            pltpu.VMEM((16, 128), f32),
            pltpu.VMEM((1, depth_gain.shape[0]), f32),
            pltpu.VMEM((elements, depth + 256), bf16),
            pltpu.VMEM(migration.shape, bf16),
            pltpu.VMEM((slabs, 8, 128), bf16),
            pltpu.VMEM((slabs, 8, 128), bf16),
            pltpu.VMEM((frames, elements, depth // frames + 256), bf16),
            pltpu.VMEM((slabs // frames, elements, 128), bf16),
            pltpu.VMEM((slabs, elements, 128), bf16),
            pltpu.VMEM((3, 1, 128), f32),
            pltpu.VMEM((LX * LY, 128), f32),
            pltpu.VMEM((8, 128), f32),
            pltpu.VMEM((slabs * elements, 128), bf16),
            pltpu.VMEM((5, LX * LY, 128), f32),
            pltpu.VMEM((PLANES * YROWS, 128), f32),
            pltpu.VMEM((16 * 32 * 8, 128), f32),
            pltpu.SemaphoreType.DMA((8,)),
            pltpu.SemaphoreType.DMA((2,)),
            pltpu.SemaphoreType.DMA((frames - 1,)),
            pltpu.SemaphoreType.DMA((frames - 1,)),
            pltpu.SemaphoreType.DMA((2,)),
            pltpu.SemaphoreType.DMA((2,)),
            pltpu.SemaphoreType.DMA((2,)),
        ],
        compiler_params=pltpu.CompilerParams(
            collective_id=0, has_side_effects=True, vmem_limit_bytes=48 * 2**20
        ),
    )(*[pltpu.with_memory_space_constraint(x, pltpu.HBM) for x in operands])
    return scores.transpose(0, 1, 3, 2)[:, None], moved.transpose(0, 1, 3, 2)[:, None]


def solution(mesh):
    placed = (
        P("slab", "frame", None),
        P(),
        P(),
        P("slab"),
        P(None, "frame", None, None, "slab"),
        P(),
    )
    return jax.shard_map(
        functools.partial(per_device, mesh.shape["slab"], mesh.shape["frame"]),
        mesh=mesh,
        in_specs=placed,
        out_specs=(P(None, "frame", None, None, "slab"), P(None, "frame", None, None, "slab")),
        check_vma=False,
    )
```

```python
import functools

import jax
import jax.numpy as jnp
from jax import lax
from jax.experimental import pallas as pl
from jax.experimental.pallas import tpu as pltpu
from jax.sharding import PartitionSpec as P

LX, LY = 32, 64
KX, KY, KZ = 8, 8, 16
MARGIN = 9
YPAD = 16
YROWS = LY + 2 * YPAD
PLANES = LX + 2 * MARGIN
GROUP = 32
BLOCKS = 4
EPS = 1e-5
CELLS = KX * KY * KZ
ROWS = 1024
ELEMENTS = 16
RING = 4
LINE = 8
MESH = pl.DeviceIdType.MESH


def expand_gain(gain_ref, wide_ref):
    for i in range(gain_ref.shape[0]):
        row = jnp.broadcast_to(gain_ref[i : i + 1, :], (128, 128))
        wide_ref[pl.ds(i * 128, 128), :] = jnp.transpose(row)


def clear(volume_ref):
    def one(i, carry):
        rows = pl.ds(pl.multiple_of(i * YROWS, 8), YROWS)
        volume_ref[rows, :] = jnp.zeros((YROWS, 128), volume_ref.dtype)
        return carry

    lax.fori_loop(0, PLANES, one, 0)


def correlate(image_ref, volume_ref, shift_ref, parts_ref):
    lane = lax.broadcasted_iota(jnp.int32, (8, 128), 1)
    row = lax.broadcasted_iota(jnp.int32, (8, 128), 0)
    inside = lane % GROUP
    first = lane < GROUP
    third = lane < 3 * GROUP
    half = lane < 2 * GROUP
    center_mask = (inside >= 1) & (inside < 1 + KZ)
    before_mask = inside < KZ
    after_mask = (inside >= 2) & (inside < 2 + KZ)

    def one(g, carry):
        bx = g // 8
        by = g % 8
        starts, turns = [], []
        for b in range(BLOCKS):
            plane = bx * KX + shift_ref[0, bx, b, by] + MARGIN
            starts.append(plane * YROWS + by * KY + shift_ref[1, bx, b, by] + YPAD)
            turns.append((GROUP * b + 1 - MARGIN - KZ * b + 128 - shift_ref[2, bx, b, by]) % 128)

        def aligned(rows):
            turned = [pltpu.roll(volume_ref[rows(starts[b]), :], turns[b], 1) for b in range(BLOCKS)]
            return jnp.where(
                half,
                jnp.where(first, turned[0], turned[1]),
                jnp.where(third, turned[2], turned[3]),
            )

        base = bx * (KX * LY) + by * KY

        def kernel_plane(kind, p):
            return image_ref[kind, pl.ds(pl.multiple_of(base + p * LY, 8), 8), :]

        zero = jnp.zeros((8, 128), jnp.float32)
        cross = [zero] * 7
        core, own = zero, zero
        kernels = [kernel_plane(0, p) for p in range(KX)]
        for p in range(-1, KX + 1):
            window = aligned(lambda start: pl.ds(start + p * YROWS, 8))
            power = window * window
            if p == -1:
                ahead = power
            elif p == KX:
                behind = power
            else:
                own = own + kernels[p] * kernels[p]
                cross[0] += kernels[p] * window
                for kind in range(1, 5):
                    cross[2 + kind] += kernel_plane(kind, p) * window
                core = core + power
                if p == 0:
                    low_end = power
                if p == KX - 1:
                    high_end = power
                if 0 < p < KX - 1:
                    middle = power if p == 1 else middle + power
            if p < KX - 1:
                cross[1] += kernels[p + 1] * window
            if p > 0:
                cross[2] += kernels[p - 1] * window
        xm = ahead + low_end + middle
        xp = middle + high_end + behind
        low = aligned(lambda start: pl.ds(start - 1, KX, stride=YROWS))
        high = aligned(lambda start: pl.ds(start + KY, KX, stride=YROWS))
        cross[3] += image_ref[0, pl.ds(base, KX, stride=LY), :] * low
        cross[4] += image_ref[0, pl.ds(base + KY - 1, KX, stride=LY), :] * high
        ym = jnp.where(row < KY - 1, core, 0.0) + low * low
        yp = jnp.where(row > 0, core, 0.0) + high * high
        slots = cross + [own]
        for value, mask in (
            (core, center_mask),
            (xm, center_mask),
            (xp, center_mask),
            (ym, center_mask),
            (yp, center_mask),
            (core, before_mask),
            (core, after_mask),
        ):
            slots.append(jnp.where(mask, value, 0.0))
        slots.append(own)
        for k, value in enumerate(slots):
            parts_ref[pl.ds(pl.multiple_of(k * 256 + g * 8, 8), 8), :] = value
        return carry

    lax.fori_loop(0, 32, one, 0, unroll=4)


def finish(parts_ref, coarse_ref, scores_ref, moved_ref):
    total = parts_ref[pl.ds(0, 512, stride=8), :]
    for s in range(1, 8):
        total = total + parts_ref[pl.ds(s, 512, stride=8), :]
    picked = lax.broadcasted_iota(jnp.int32, (8, 128), 1) // GROUP
    picked = (picked == lax.broadcasted_iota(jnp.int32, (8, 128), 0)).astype(jnp.float32)
    sums = lax.dot_general(
        picked,
        total,
        (((1,), (1,)), ((), ())),
        precision=lax.Precision.HIGHEST,
        preferred_element_type=jnp.float32,
    ) * (1.0 / CELLS)
    tiles = [sums[:, 128 * i : 128 * (i + 1)] for i in range(4)]
    lane = lax.broadcasted_iota(jnp.int32, (8, 128), 1)
    own = jnp.where(lane >= 3 * GROUP, tiles[3], 0.0)
    own = own + pltpu.roll(own, 64, 1)
    own = own + pltpu.roll(own, 32, 1) + EPS
    scored = [
        CELLS**0.5 * tiles[i] / jnp.sqrt(own * (tiles[2 + i] + EPS)) for i in range(2)
    ]
    scores = [
        scored[k // 4] if k % 4 == 0 else pltpu.roll(scored[k // 4], 128 - GROUP * (k % 4), 1)
        for k in range(7)
    ]

    def tile(value, bx):
        value = value if bx == 0 else pltpu.roll(value, 128 - 8 * bx, 1)
        return value[:BLOCKS, :8]

    for k in range(7):
        for bx in range(4):
            scores_ref[k, bx] = tile(scores[k], bx)
    for a in range(3):
        low, high = scores[1 + 2 * a], scores[2 + 2 * a]
        curvature = jnp.maximum(2.0 * scores[0] - low - high, 1.0)
        step = (high - low) / (2.0 * curvature)
        for bx in range(4):
            moved_ref[a, bx] = coarse_ref[a, bx].astype(jnp.float32) + tile(step, bx)


def scaled(migration_ref, samples, gain_ref, depth_row, i):
    rows = pl.ds(pl.multiple_of(i * ROWS, ROWS), ROWS)
    raw = jnp.dot(migration_ref[rows, :], samples, preferred_element_type=jnp.float32)
    return (raw * gain_ref[rows, :] * depth_row).astype(jnp.bfloat16).astype(jnp.float32)


def make_image(migration_ref, samples_ref, gain_ref, depth_ref, image_ref):
    def one(i, carry):
        rows = pl.ds(pl.multiple_of(i * ROWS, ROWS), ROWS)
        image = scaled(migration_ref, samples_ref[...], gain_ref, depth_ref[0:1, :], i)
        tiles = image.reshape(-1, 8, 128)
        row = lax.broadcasted_iota(jnp.int32, tiles.shape, 1)
        image_ref[0, rows, :] = image
        image_ref[1, rows, :] = jnp.where(row < 7, pltpu.roll(tiles, 7, 1), 0.0).reshape(-1, 128)
        image_ref[2, rows, :] = jnp.where(row > 0, pltpu.roll(tiles, 1, 1), 0.0).reshape(-1, 128)
        image_ref[3, rows, :] = pltpu.roll(image, 127, 1)
        image_ref[4, rows, :] = pltpu.roll(image, 1, 1)
        return carry

    lax.fori_loop(0, LX * LY // ROWS, one, 0)


def add_reference(migration_ref, recv_ref, piece, gain_ref, depth_ref, total_ref, volume_ref, first, last):
    planes = ROWS // LY
    depth = recv_ref[piece].reshape(-1, 128)
    width = depth.shape[0]
    columns = pl.ds(pl.multiple_of(piece * width, 128), width)

    def one(i, carry):
        rows = pl.ds(pl.multiple_of(i * ROWS, ROWS), ROWS)
        raw = jnp.dot(migration_ref[rows, columns], depth, preferred_element_type=jnp.float32)
        if not first:
            raw = raw + total_ref[rows, :]
        if not last:
            total_ref[rows, :] = raw
            return carry
        ref = (raw * gain_ref[rows, :] * depth_ref[1:2, :]).astype(jnp.bfloat16).astype(jnp.float32)
        for j in range(planes):
            place = pl.multiple_of((MARGIN + i * planes + j) * YROWS + YPAD, 8)
            volume_ref[pl.ds(place, LY), :] = ref[j * LY : (j + 1) * LY]
        return carry

    lax.fori_loop(0, LX * LY // ROWS, one, 0)


def place_of(column):
    return GROUP * (column // KZ) + 1 + column % KZ


def spread_depth(gains_ref, depth_ref):
    lane = lax.broadcasted_iota(jnp.int32, (8, 128), 1)
    left, here, right = [jnp.broadcast_to(gains_ref[i], (8, 128)) for i in range(3)]
    row = jnp.zeros((8, 128), jnp.float32)
    for b in range(BLOCKS):
        turned = pltpu.roll(here, (GROUP * b + 1 - KZ * b) % 128, 1)
        start = GROUP * b + 1
        row = jnp.where((lane >= start) & (lane < start + KZ), turned, row)
    sides = jnp.where(lane < MARGIN, pltpu.roll(left, 128 - 64 + MARGIN, 1), 0.0)
    sides = jnp.where((lane >= MARGIN) & (lane < MARGIN + 64), pltpu.roll(here, MARGIN, 1), sides)
    sides = jnp.where(
        (lane >= MARGIN + 64) & (lane < 2 * MARGIN + 64), pltpu.roll(right, MARGIN + 64, 1), sides
    )
    depth_ref[0:1, :] = row[0:1]
    depth_ref[1:2, :] = sides[0:1]


def pack_own(data_ref, send_ref):
    low = lax.broadcasted_iota(jnp.int32, (8, 128), 1) < 64
    for t in range(data_ref.shape[1] // 128 - 2):
        tile = data_ref[:, 128 * (t + 1) : 128 * (t + 2)].astype(jnp.float32)
        first, second = tile[:8], tile[8:]
        even = jnp.where(low, first, pltpu.roll(second, 64, 1))
        odd = jnp.where(low, pltpu.roll(first, 64, 1), second)
        send_ref[2 * t % LINE, 2 * t // LINE] = even.astype(jnp.bfloat16)
        send_ref[(2 * t + 1) % LINE, 2 * t // LINE] = odd.astype(jnp.bfloat16)


def unpack_own(recv_ref, samples_ref):
    row = lax.broadcasted_iota(jnp.int32, (128, 128), 0)
    lane = lax.broadcasted_iota(jnp.int32, (128, 128), 1)
    packed = recv_ref[...].astype(jnp.float32).reshape(-1, 128).astype(jnp.bfloat16)
    halves = []
    for start in (0, 64):
        column = row - start
        picked = (lane == place_of(column)) & (column >= 0) & (column < 64)
        picked = picked.astype(jnp.float32).astype(jnp.bfloat16)
        half = jnp.dot(packed, picked, preferred_element_type=jnp.float32)
        halves.append(half.reshape(-1, 8, 128))
    samples = jnp.concatenate(halves, axis=1).reshape(-1, 128)
    samples_ref[...] = samples.astype(jnp.bfloat16)


def pack_reference(quarters_ref, chosen, send_ref):
    lane = lax.broadcasted_iota(jnp.int32, (ELEMENTS, 128), 1)
    tiles = quarters_ref.shape[2] // 128
    parts = [quarters_ref[chosen, :, 128 * t : 128 * (t + 1)].astype(jnp.float32) for t in range(tiles)]
    for m in range(tiles - 2):
        for half in (0, 1):
            turn = MARGIN + 64 * half
            here, after = parts[m + half], parts[m + half + 1]
            window = jnp.where(lane < turn, pltpu.roll(here, turn, 1), pltpu.roll(after, turn, 1))
            place = 2 * m + half
            send_ref[place % LINE, place // LINE] = window.astype(jnp.bfloat16)


def remote(source, target, sems, device):
    return pltpu.make_async_remote_copy(
        src_ref=source,
        dst_ref=target,
        send_sem=sems.at[0],
        recv_sem=sems.at[1],
        device_id=device,
        device_id_type=MESH,
    )


def wait_bytes(ref, sem):
    pltpu.make_async_copy(ref, ref, sem).wait()


def fused_kernel(
    slabs, frames,
    shift_hbm, chosen_hbm, data_hbm, migration_hbm, column_hbm, gains_hbm,
    scores_ref, moved_ref,
    shift_ref, chosen_ref, coarse_ref, column_ref, gains_in_ref,
    data_ref, migration_ref, own_send, own_stage, own_recv, quarters_ref, ref_send, ref_stage, ref_recv,
    gains_ref, gain_ref, depth_ref, samples_ref, image_ref, total_ref, volume_ref, parts_ref,
    local_sems, quarter_sems, own_line, own_plane, ref_line, ref_plane_send, ref_plane_recv,
    pair_send, pair_recv, to_next_sems, to_previous_sems,
):
    frame = lax.axis_index("frame")
    slab = lax.axis_index("slab")
    column, depth_place = slab // LINE, slab % LINE
    columns = slabs // LINE
    place_x, place_y, core = column // 2, column % 2, frame % 2
    other_core = frame + 1 - 2 * core
    def distance(of_frame):
        return jnp.where(of_frame == 0, 1, jnp.where(of_frame == 1, 3, jnp.where(of_frame == 2, 0, 2)))

    frame_at = (2, 0, 3, 1)
    target_x = (place_x + distance(frame)) % RING
    keeps = (target_x == place_x) & (core == place_y)
    has_next = slab < slabs - 1
    has_previous = slab > 0
    next_slab, previous_slab = (slab + 1) % slabs, (slab + slabs - 1) % slabs

    def on_line(i):
        return {"frame": frame, "slab": column * LINE + (depth_place + i) % LINE}

    def on_plane(i):
        return {"frame": frame, "slab": (column + i) % columns * LINE + depth_place}

    width = data_hbm.shape[1]
    loads = [
        pltpu.make_async_copy(start, end, local_sems.at[i])
        for i, (start, end) in enumerate(
            (
                (data_hbm, data_ref.at[:, pl.ds(128, width)]),
                (gains_hbm, gains_in_ref),
                (chosen_hbm, chosen_ref),
                (migration_hbm, migration_ref),
                (column_hbm, column_ref),
                (shift_hbm, shift_ref),
                (shift_hbm, coarse_ref),
            )
        )
    ]
    for copy in loads:
        copy.start()
    gains_ref[...] = jnp.zeros(gains_ref.shape, gains_ref.dtype)

    barrier = pltpu.get_barrier_semaphore()

    def greet(device):
        pl.semaphore_signal(barrier, inc=1, device_id=device, device_id_type=MESH)

    for i in range(1, LINE):
        greet(on_line(i))
    for i in range(1, columns):
        greet(on_plane(i))
    for i in range(RING):
        x = (place_x + i) % RING
        device = {"frame": frame_at[-i % RING], "slab": (x * 2 + core) * LINE + depth_place}
        if i == 0:
            pl.when(jnp.logical_not(keeps))(functools.partial(greet, device))
        else:
            greet(device)
    for i in range(1, frames):
        greet({"frame": (frame + i) % frames, "slab": slab})
    pl.when(has_next)(lambda: greet({"frame": frame, "slab": next_slab}))
    pl.when(has_previous)(lambda: greet({"frame": frame, "slab": previous_slab}))

    data_ref[:, :128] = jnp.zeros((ELEMENTS, 128), data_ref.dtype)
    data_ref[:, -128:] = jnp.zeros((ELEMENTS, 128), data_ref.dtype)
    for copy in loads[:3]:
        copy.wait()
    gains_ref[1, :, :64] = gains_in_ref[...]
    pack_own(data_ref, own_send)
    greetings = (LINE - 1) + (columns - 1) + 4 - jnp.where(keeps, 1, 0) + (frames - 1)
    greetings = greetings + jnp.where(has_next, 1, 0) + jnp.where(has_previous, 1, 0)
    pl.semaphore_wait(barrier, greetings)

    quarter = width // frames

    def quarter_of(of_frame):
        place = (place_x + distance(of_frame)) % RING
        return data_ref.at[:, pl.ds(pl.multiple_of(place * quarter, 128), quarter + 256)]

    for i in range(1, frames):
        other = (frame + i) % frames
        remote(
            quarter_of(other), quarters_ref.at[frame], quarter_sems, {"frame": other, "slab": slab}
        ).start()
    pltpu.make_async_copy(quarter_of(frame), quarters_ref.at[frame], quarter_sems.at[1]).start()

    def along_line(send_ref, stage_ref, sems):
        for i in (4, 3, 5, 2, 6, 1, 7):
            there = (depth_place + i) % LINE
            remote(send_ref.at[there], stage_ref.at[depth_place], sems, on_line(i)).start()
        pltpu.make_async_copy(send_ref.at[depth_place], stage_ref.at[depth_place], sems.at[1]).start()

    along_line(own_send, own_stage, own_line)

    to_next = remote(gains_ref.at[1], gains_ref.at[0], to_next_sems, {"frame": frame, "slab": next_slab})
    to_previous = remote(
        gains_ref.at[1], gains_ref.at[2], to_previous_sems, {"frame": frame, "slab": previous_slab}
    )
    pl.when(has_next)(to_next.start)
    pl.when(has_previous)(to_previous.start)

    wait_bytes(quarters_ref, quarter_sems.at[1])
    pack_reference(quarters_ref, chosen_ref[0], ref_send)
    along_line(ref_send, ref_stage, ref_line)

    for copy in loads[3:]:
        copy.wait()
    clear(volume_ref)

    here = pl.ds(column * LINE, LINE)
    wait_bytes(own_stage, own_line.at[1])
    for i in range(1, columns):
        there = (column + i) % columns
        remote(own_stage.at[:, there], own_recv.at[here], own_plane, on_plane(i)).start()
    pltpu.make_async_copy(own_stage.at[:, column], own_recv.at[here], own_plane.at[1]).start()
    expand_gain(column_ref, gain_ref)

    wait_bytes(ref_stage, ref_line.at[1])
    for a, b in ((1, 1), (1, 0), (0, 1), (0, 0)):
        to_y = (place_y + a) % 2
        to_frame = (frame // 2 + b) % 2 * 2 + place_y
        copy = pltpu.make_async_remote_copy(
            src_ref=ref_stage.at[:, to_y],
            dst_ref=ref_recv.at[place_x, place_y],
            send_sem=ref_plane_send.at[0],
            recv_sem=ref_plane_recv.at[place_x],
            device_id={"frame": to_frame, "slab": (target_x * 2 + to_y) * LINE + depth_place},
            device_id_type=MESH,
        )
        if a == 0 and b == 0:
            pl.when(jnp.logical_not(keeps))(copy.start)
        else:
            copy.start()

    @pl.when(keeps)
    def _():
        pltpu.make_async_copy(
            ref_stage.at[:, place_y], ref_recv.at[place_x, place_y], ref_plane_recv.at[place_x]
        ).start()

    pl.when(has_previous)(to_next.wait_recv)
    pl.when(has_next)(to_previous.wait_recv)
    spread_depth(gains_ref, depth_ref)
    wait_bytes(own_recv, own_plane.at[1])
    unpack_own(own_recv, samples_ref)
    make_image(migration_ref, samples_ref, gain_ref, depth_ref, image_ref)
    pieces = [(place_x + i) % RING for i in (0, 1, 3, 2)]
    for x in pieces:
        copy = pltpu.make_async_remote_copy(
            src_ref=ref_recv.at[x, core],
            dst_ref=ref_recv.at[x, core],
            send_sem=pair_send.at[0],
            recv_sem=pair_recv.at[x],
            device_id={"frame": other_core, "slab": slab},
            device_id_type=MESH,
        )
        wait_bytes(ref_recv.at[x, core], ref_plane_recv.at[x])
        copy.start()
    for i, x in enumerate(pieces):
        wait_bytes(ref_recv.at[x, 1 - core], pair_recv.at[x])
        add_reference(
            migration_ref, ref_recv, x, gain_ref, depth_ref, total_ref, volume_ref, i == 0, i == RING - 1
        )
    correlate(image_ref, volume_ref, shift_ref, parts_ref)
    finish(parts_ref, coarse_ref, scores_ref, moved_ref)

    pl.when(has_next)(to_next.wait_send)
    pl.when(has_previous)(to_previous.wait_send)
    wait_bytes(quarters_ref.at[pl.ds(0, frames - 1)], quarter_sems.at[0])
    wait_bytes(own_stage.at[pl.ds(0, LINE - 1)], own_line.at[0])
    wait_bytes(ref_stage.at[pl.ds(0, LINE - 1)], ref_line.at[0])
    wait_bytes(own_recv.at[pl.ds(0, slabs - LINE)], own_plane.at[0])

    wait_bytes(own_recv, pair_send.at[0])

    @pl.when(keeps)
    def _():
        wait_bytes(own_recv.at[pl.ds(0, slabs // 4 * 3)], ref_plane_send.at[0])

    @pl.when(jnp.logical_not(keeps))
    def _():
        wait_bytes(own_recv, ref_plane_send.at[0])


def per_device(slabs, frames, element_data, migration, column_gain, depth_gain, coarse_shift, reference_frame):
    elements, _, depth = element_data.shape
    data = element_data.reshape(elements, depth)
    coarse = coarse_shift[:, 0].transpose(0, 1, 3, 2)
    vmem = pl.BlockSpec(memory_space=pltpu.VMEM)
    hbm = pl.BlockSpec(memory_space=pltpu.HBM)
    bf16, f32 = jnp.bfloat16, jnp.float32
    operands = (coarse, reference_frame, data, migration, column_gain.reshape(16, 128), depth_gain.reshape(1, -1))
    scores, moved = pl.pallas_call(
        functools.partial(fused_kernel, slabs, frames),
        out_shape=(
            jax.ShapeDtypeStruct((7, 4, 4, 8), f32),
            jax.ShapeDtypeStruct((3, 4, 4, 8), f32),
        ),
        in_specs=[hbm] * 6,
        out_specs=(vmem, vmem),
        scratch_shapes=[
            pltpu.SMEM(coarse.shape, jnp.int32),
            pltpu.SMEM(reference_frame.shape, jnp.int32),
            pltpu.VMEM(coarse.shape, jnp.int32),
            pltpu.VMEM((16, 128), f32),
            pltpu.VMEM((1, depth_gain.shape[0]), f32),
            pltpu.VMEM((elements, depth + 256), bf16),
            pltpu.VMEM(migration.shape, bf16),
            pltpu.VMEM((LINE, slabs // LINE, 8, 128), bf16),
            pltpu.VMEM((LINE, slabs // LINE, 8, 128), bf16),
            pltpu.VMEM((slabs, 8, 128), bf16),
            pltpu.VMEM((frames, elements, depth // frames + 256), bf16),
            pltpu.VMEM((LINE, slabs // frames // LINE, elements, 128), bf16),
            pltpu.VMEM((LINE, slabs // frames // LINE, elements, 128), bf16),
            pltpu.VMEM((RING, 2, LINE, elements, 128), bf16),
            pltpu.VMEM((3, 1, 128), f32),
            pltpu.VMEM((LX * LY, 128), f32),
            pltpu.VMEM((8, 128), f32),
            pltpu.VMEM((slabs * elements, 128), bf16),
            pltpu.VMEM((5, LX * LY, 128), f32),
            pltpu.VMEM((LX * LY, 128), f32),
            pltpu.VMEM((PLANES * YROWS, 128), f32),
            pltpu.VMEM((16 * 32 * 8, 128), f32),
            pltpu.SemaphoreType.DMA((7,)),
            pltpu.SemaphoreType.DMA((2,)),
            pltpu.SemaphoreType.DMA((2,)),
            pltpu.SemaphoreType.DMA((2,)),
            pltpu.SemaphoreType.DMA((2,)),
            pltpu.SemaphoreType.DMA((1,)),
            pltpu.SemaphoreType.DMA((RING,)),
            pltpu.SemaphoreType.DMA((1,)),
            pltpu.SemaphoreType.DMA((RING,)),
            pltpu.SemaphoreType.DMA((2,)),
            pltpu.SemaphoreType.DMA((2,)),
        ],
        compiler_params=pltpu.CompilerParams(
            collective_id=0, has_side_effects=True, vmem_limit_bytes=48 * 2**20
        ),
    )(*[pltpu.with_memory_space_constraint(x, pltpu.HBM) for x in operands])
    return scores.transpose(0, 1, 3, 2)[:, None], moved.transpose(0, 1, 3, 2)[:, None]


def solution(mesh):
    placed = (
        P("slab", "frame", None),
        P(),
        P(),
        P("slab"),
        P(None, "frame", None, None, "slab"),
        P(),
    )
    return jax.shard_map(
        functools.partial(per_device, mesh.shape["slab"], mesh.shape["frame"]),
        mesh=mesh,
        in_specs=placed,
        out_specs=(P(None, "frame", None, None, "slab"), P(None, "frame", None, None, "slab")),
        check_vma=False,
    )
```

```python
import functools

import jax
import jax.numpy as jnp
from jax import lax
from jax.experimental import pallas as pl
from jax.experimental.pallas import tpu as pltpu
from jax.sharding import PartitionSpec as P

LX, LY = 32, 64
KX, KY, KZ = 8, 8, 16
MARGIN = 9
YPAD = 16
YROWS = LY + 2 * YPAD
PLANES = LX + 2 * MARGIN
GROUP = 32
BLOCKS = 4
EPS = 1e-5
CELLS = KX * KY * KZ
ROWS = 1024
ELEMENTS = 16
RING = 4
LINE = 8
SEVERAL = 4
MESH = pl.DeviceIdType.MESH


def expand_gain(gain_ref, wide_ref):
    for i in range(gain_ref.shape[0]):
        row = jnp.broadcast_to(gain_ref[i : i + 1, :], (128, 128))
        wide_ref[pl.ds(i * 128, 128), :] = jnp.transpose(row)


def clear(volume_ref):
    def one(i, carry):
        rows = pl.ds(pl.multiple_of(i * YROWS, 8), YROWS)
        volume_ref[rows, :] = jnp.zeros((YROWS, 128), volume_ref.dtype)
        return carry

    lax.fori_loop(0, PLANES, one, 0)


def correlate(image_ref, volume_ref, shift_ref, parts_ref, begin, end, beside=None):
    lane = lax.broadcasted_iota(jnp.int32, (8, 128), 1)
    row = lax.broadcasted_iota(jnp.int32, (8, 128), 0)
    inside = lane % GROUP
    first = lane < GROUP
    third = lane < 3 * GROUP
    half = lane < 2 * GROUP
    center_mask = (inside >= 1) & (inside < 1 + KZ)
    before_mask = inside < KZ
    after_mask = (inside >= 2) & (inside < 2 + KZ)

    def one(g, carry):
        bx = g // 8
        by = g % 8
        starts, turns = [], []
        for b in range(BLOCKS):
            plane = bx * KX + shift_ref[0, bx, b, by] + MARGIN
            starts.append(plane * YROWS + by * KY + shift_ref[1, bx, b, by] + YPAD)
            turns.append((GROUP * b + 1 - MARGIN - KZ * b + 128 - shift_ref[2, bx, b, by]) % 128)

        def aligned(rows):
            turned = [pltpu.roll(volume_ref[rows(starts[b]), :], turns[b], 1) for b in range(BLOCKS)]
            return jnp.where(
                half,
                jnp.where(first, turned[0], turned[1]),
                jnp.where(third, turned[2], turned[3]),
            )

        base = bx * (KX * LY) + by * KY

        def kernel_plane(kind, p):
            return image_ref[kind, pl.ds(pl.multiple_of(base + p * LY, 8), 8), :]

        zero = jnp.zeros((8, 128), jnp.float32)
        cross = [zero] * 7
        core, own = zero, zero
        kernels = [kernel_plane(0, p) for p in range(KX)]
        for p in range(-1, KX + 1):
            window = aligned(lambda start: pl.ds(start + p * YROWS, 8))
            power = window * window
            if p == -1:
                ahead = power
            elif p == KX:
                behind = power
            else:
                own = own + kernels[p] * kernels[p]
                cross[0] += kernels[p] * window
                for kind in range(1, 5):
                    cross[2 + kind] += kernel_plane(kind, p) * window
                core = core + power
                if p == 0:
                    low_end = power
                if p == KX - 1:
                    high_end = power
                if 0 < p < KX - 1:
                    middle = power if p == 1 else middle + power
            if p < KX - 1:
                cross[1] += kernels[p + 1] * window
            if p > 0:
                cross[2] += kernels[p - 1] * window
        xm = ahead + low_end + middle
        xp = middle + high_end + behind
        low = aligned(lambda start: pl.ds(start - 1, KX, stride=YROWS))
        high = aligned(lambda start: pl.ds(start + KY, KX, stride=YROWS))
        cross[3] += image_ref[0, pl.ds(base, KX, stride=LY), :] * low
        cross[4] += image_ref[0, pl.ds(base + KY - 1, KX, stride=LY), :] * high
        ym = jnp.where(row < KY - 1, core, 0.0) + low * low
        yp = jnp.where(row > 0, core, 0.0) + high * high
        slots = cross + [own]
        for value, mask in (
            (core, center_mask),
            (xm, center_mask),
            (xp, center_mask),
            (ym, center_mask),
            (yp, center_mask),
            (core, before_mask),
            (core, after_mask),
        ):
            slots.append(jnp.where(mask, value, 0.0))
        slots.append(own)
        for k, value in enumerate(slots):
            parts_ref[pl.ds(pl.multiple_of(k * 256 + g * 8, 8), 8), :] = value
        return carry

    def several(i, carry):
        if beside is not None:
            beside(i - begin // SEVERAL)
        for j in range(SEVERAL):
            one(i * SEVERAL + j, carry)
        return carry

    lax.fori_loop(begin // SEVERAL, end // SEVERAL, several, 0)


def finish(parts_ref, coarse_ref, scores_ref, moved_ref):
    total = parts_ref[pl.ds(0, 512, stride=8), :]
    for s in range(1, 8):
        total = total + parts_ref[pl.ds(s, 512, stride=8), :]
    picked = lax.broadcasted_iota(jnp.int32, (8, 128), 1) // GROUP
    picked = (picked == lax.broadcasted_iota(jnp.int32, (8, 128), 0)).astype(jnp.float32)
    high = total.astype(jnp.bfloat16)
    low = (total - high.astype(jnp.float32)).astype(jnp.bfloat16)
    sums = [
        lax.dot_general(
            picked.astype(jnp.bfloat16),
            part,
            (((1,), (1,)), ((), ())),
            preferred_element_type=jnp.float32,
        )
        for part in (high, low)
    ]
    sums = (sums[0] + sums[1]) * (1.0 / CELLS)
    tiles = [sums[:, 128 * i : 128 * (i + 1)] for i in range(4)]
    lane = lax.broadcasted_iota(jnp.int32, (8, 128), 1)
    own = jnp.where(lane >= 3 * GROUP, tiles[3], 0.0)
    own = own + pltpu.roll(own, 64, 1)
    own = own + pltpu.roll(own, 32, 1) + EPS
    scored = [
        CELLS**0.5 * tiles[i] / jnp.sqrt(own * (tiles[2 + i] + EPS)) for i in range(2)
    ]
    scores = [
        scored[k // 4] if k % 4 == 0 else pltpu.roll(scored[k // 4], 128 - GROUP * (k % 4), 1)
        for k in range(7)
    ]

    def tile(value, bx):
        value = value if bx == 0 else pltpu.roll(value, 128 - 8 * bx, 1)
        return value[:BLOCKS, :8]

    for k in range(7):
        for bx in range(4):
            scores_ref[k, bx] = tile(scores[k], bx)
    for a in range(3):
        low, high = scores[1 + 2 * a], scores[2 + 2 * a]
        curvature = jnp.maximum(2.0 * scores[0] - low - high, 1.0)
        step = (high - low) / (2.0 * curvature)
        for bx in range(4):
            moved_ref[a, bx] = coarse_ref[a, bx].astype(jnp.float32) + tile(step, bx)


def scaled(migration_ref, samples, gain_ref, depth_row, i):
    rows = pl.ds(pl.multiple_of(i * ROWS, ROWS), ROWS)
    raw = jnp.dot(migration_ref[rows, :], samples, preferred_element_type=jnp.float32)
    return (raw * gain_ref[rows, :] * depth_row).astype(jnp.bfloat16).astype(jnp.float32)


def make_image(migration_ref, samples_ref, gain_ref, depth_ref, image_ref):
    def one(i, carry):
        rows = pl.ds(pl.multiple_of(i * ROWS, ROWS), ROWS)
        image = scaled(migration_ref, samples_ref[...], gain_ref, depth_ref[0:1, :], i)
        tiles = image.reshape(-1, 8, 128)
        row = lax.broadcasted_iota(jnp.int32, tiles.shape, 1)
        image_ref[0, rows, :] = image
        image_ref[1, rows, :] = jnp.where(row < 7, pltpu.roll(tiles, 7, 1), 0.0).reshape(-1, 128)
        image_ref[2, rows, :] = jnp.where(row > 0, pltpu.roll(tiles, 1, 1), 0.0).reshape(-1, 128)
        image_ref[3, rows, :] = pltpu.roll(image, 127, 1)
        image_ref[4, rows, :] = pltpu.roll(image, 1, 1)
        return carry

    lax.fori_loop(0, LX * LY // ROWS, one, 0)


def reference_raw(migration_ref, recv_ref, total_ref, start, count):
    samples = recv_ref[...].reshape(-1, 128)
    rows = pl.ds(start, count)
    total_ref[rows, :] = jnp.dot(migration_ref[rows, :], samples, preferred_element_type=jnp.float32)


def reference_planes(total_ref, gain_ref, depth_ref, volume_ref, start, count):
    for plane in range(start, start + count):
        rows = pl.ds(plane * LY, LY)
        ref = (total_ref[rows, :] * gain_ref[rows, :] * depth_ref[1:2, :]).astype(jnp.bfloat16)
        volume_ref[pl.ds((MARGIN + plane) * YROWS + YPAD, LY), :] = ref.astype(jnp.float32)


def place_of(column):
    return GROUP * (column // KZ) + 1 + column % KZ


def spread_depth(gains_ref, depth_ref):
    lane = lax.broadcasted_iota(jnp.int32, (8, 128), 1)
    left, here, right = [jnp.broadcast_to(gains_ref[i], (8, 128)) for i in range(3)]
    row = jnp.zeros((8, 128), jnp.float32)
    for b in range(BLOCKS):
        turned = pltpu.roll(here, (GROUP * b + 1 - KZ * b) % 128, 1)
        start = GROUP * b + 1
        row = jnp.where((lane >= start) & (lane < start + KZ), turned, row)
    sides = jnp.where(lane < MARGIN, pltpu.roll(left, 128 - 64 + MARGIN, 1), 0.0)
    sides = jnp.where((lane >= MARGIN) & (lane < MARGIN + 64), pltpu.roll(here, MARGIN, 1), sides)
    sides = jnp.where(
        (lane >= MARGIN + 64) & (lane < 2 * MARGIN + 64), pltpu.roll(right, MARGIN + 64, 1), sides
    )
    depth_ref[0:1, :] = row[0:1]
    depth_ref[1:2, :] = sides[0:1]


def pack_own(data_ref, send_ref):
    low = lax.broadcasted_iota(jnp.int32, (8, 128), 1) < 64
    for t in range(data_ref.shape[1] // 128 - 2):
        tile = data_ref[:, 128 * (t + 1) : 128 * (t + 2)].astype(jnp.float32)
        first, second = tile[:8], tile[8:]
        even = jnp.where(low, first, pltpu.roll(second, 64, 1))
        odd = jnp.where(low, pltpu.roll(first, 64, 1), second)
        send_ref[2 * t % LINE, 2 * t // LINE] = even.astype(jnp.bfloat16)
        send_ref[(2 * t + 1) % LINE, 2 * t // LINE] = odd.astype(jnp.bfloat16)


def unpack_own(recv_ref, samples_ref):
    row = lax.broadcasted_iota(jnp.int32, (128, 128), 0)
    lane = lax.broadcasted_iota(jnp.int32, (128, 128), 1)
    packed = recv_ref[...].astype(jnp.float32).reshape(-1, 128).astype(jnp.bfloat16)
    halves = []
    for start in (0, 64):
        column = row - start
        picked = (lane == place_of(column)) & (column >= 0) & (column < 64)
        picked = picked.astype(jnp.float32).astype(jnp.bfloat16)
        half = jnp.dot(packed, picked, preferred_element_type=jnp.float32)
        halves.append(half.reshape(-1, 8, 128))
    samples = jnp.concatenate(halves, axis=1).reshape(-1, 128)
    samples_ref[...] = samples.astype(jnp.bfloat16)


def pack_reference(quarters_ref, chosen, send_ref):
    lane = lax.broadcasted_iota(jnp.int32, (ELEMENTS, 128), 1)
    tiles = quarters_ref.shape[2] // 128
    parts = [quarters_ref[chosen, :, 128 * t : 128 * (t + 1)].astype(jnp.float32) for t in range(tiles)]
    for m in range(tiles - 2):
        for half in (0, 1):
            turn = MARGIN + 64 * half
            here, after = parts[m + half], parts[m + half + 1]
            window = jnp.where(lane < turn, pltpu.roll(here, turn, 1), pltpu.roll(after, turn, 1))
            place = 2 * m + half
            send_ref[place % LINE, place // LINE] = window.astype(jnp.bfloat16)


def remote(source, target, sems, device):
    return pltpu.make_async_remote_copy(
        src_ref=source,
        dst_ref=target,
        send_sem=sems.at[0],
        recv_sem=sems.at[1],
        device_id=device,
        device_id_type=MESH,
    )


def wait_bytes(ref, sem):
    pltpu.make_async_copy(ref, ref, sem).wait()


def fused_kernel(
    slabs, frames,
    shift_hbm, chosen_hbm, data_hbm, migration_hbm, column_hbm, gains_hbm,
    scores_ref, moved_ref,
    shift_ref, chosen_ref, coarse_ref, column_ref, gains_in_ref,
    data_ref, migration_ref, own_send, own_stage, own_recv, quarters_ref, ref_send, ref_stage, ref_recv,
    gains_ref, gain_ref, depth_ref, samples_ref, image_ref, total_ref, volume_ref, parts_ref,
    local_sems, quarter_sems, own_line, own_plane, ref_line, ref_plane_send, ref_plane_recv,
    pair_send, pair_recv, to_next_sems, to_previous_sems,
):
    frame = lax.axis_index("frame")
    slab = lax.axis_index("slab")
    column, depth_place = slab // LINE, slab % LINE
    columns = slabs // LINE
    place_x, place_y, core = column // 2, column % 2, frame % 2
    other_core = frame + 1 - 2 * core
    def distance(of_frame):
        return jnp.where(of_frame == 0, 1, jnp.where(of_frame == 1, 3, jnp.where(of_frame == 2, 0, 2)))

    frame_at = (2, 0, 3, 1)
    target_x = (place_x + distance(frame)) % RING
    keeps = (target_x == place_x) & (core == place_y)
    has_next = slab < slabs - 1
    has_previous = slab > 0
    next_slab, previous_slab = (slab + 1) % slabs, (slab + slabs - 1) % slabs

    def on_line(i):
        return {"frame": frame, "slab": column * LINE + (depth_place + i) % LINE}

    def on_plane(i):
        return {"frame": frame, "slab": (column + i) % columns * LINE + depth_place}

    width = data_hbm.shape[1]
    loads = [
        pltpu.make_async_copy(start, end, local_sems.at[i])
        for i, (start, end) in enumerate(
            (
                (data_hbm, data_ref.at[:, pl.ds(128, width)]),
                (gains_hbm, gains_in_ref),
                (chosen_hbm, chosen_ref),
                (migration_hbm, migration_ref),
                (column_hbm, column_ref),
                (shift_hbm, shift_ref),
                (shift_hbm, coarse_ref),
            )
        )
    ]
    for copy in loads:
        copy.start()
    gains_ref[...] = jnp.zeros(gains_ref.shape, gains_ref.dtype)

    barrier = pltpu.get_barrier_semaphore()

    def greet(device):
        pl.semaphore_signal(barrier, inc=1, device_id=device, device_id_type=MESH)

    for i in range(1, LINE):
        greet(on_line(i))
    for i in range(1, columns):
        greet(on_plane(i))
    for i in range(RING):
        x = (place_x + i) % RING
        device = {"frame": frame_at[-i % RING], "slab": (x * 2 + core) * LINE + depth_place}
        if i == 0:
            pl.when(jnp.logical_not(keeps))(functools.partial(greet, device))
        else:
            greet(device)
    for i in range(1, frames):
        greet({"frame": (frame + i) % frames, "slab": slab})
    pl.when(has_next)(lambda: greet({"frame": frame, "slab": next_slab}))
    pl.when(has_previous)(lambda: greet({"frame": frame, "slab": previous_slab}))

    data_ref[:, :128] = jnp.zeros((ELEMENTS, 128), data_ref.dtype)
    data_ref[:, -128:] = jnp.zeros((ELEMENTS, 128), data_ref.dtype)
    for copy in loads[:3]:
        copy.wait()
    gains_ref[1, :, :64] = gains_in_ref[...]
    pack_own(data_ref, own_send)
    greetings = (LINE - 1) + (columns - 1) + 4 - jnp.where(keeps, 1, 0) + (frames - 1)
    greetings = greetings + jnp.where(has_next, 1, 0) + jnp.where(has_previous, 1, 0)
    pl.semaphore_wait(barrier, greetings)

    quarter = width // frames

    def quarter_of(of_frame):
        place = (place_x + distance(of_frame)) % RING
        return data_ref.at[:, pl.ds(pl.multiple_of(place * quarter, 128), quarter + 256)]

    for i in range(1, frames):
        other = (frame + i) % frames
        remote(
            quarter_of(other), quarters_ref.at[frame], quarter_sems, {"frame": other, "slab": slab}
        ).start()
    pltpu.make_async_copy(quarter_of(frame), quarters_ref.at[frame], quarter_sems.at[1]).start()

    def along_line(send_ref, stage_ref, sems):
        for i in (4, 3, 5, 2, 6, 1, 7):
            there = (depth_place + i) % LINE
            remote(send_ref.at[there], stage_ref.at[depth_place], sems, on_line(i)).start()
        pltpu.make_async_copy(send_ref.at[depth_place], stage_ref.at[depth_place], sems.at[1]).start()

    along_line(own_send, own_stage, own_line)

    to_next = remote(gains_ref.at[1], gains_ref.at[0], to_next_sems, {"frame": frame, "slab": next_slab})
    to_previous = remote(
        gains_ref.at[1], gains_ref.at[2], to_previous_sems, {"frame": frame, "slab": previous_slab}
    )
    pl.when(has_next)(to_next.start)
    pl.when(has_previous)(to_previous.start)

    wait_bytes(quarters_ref, quarter_sems.at[1])
    pack_reference(quarters_ref, chosen_ref[0], ref_send)
    along_line(ref_send, ref_stage, ref_line)

    for copy in loads[3:]:
        copy.wait()
    clear(volume_ref)

    here = pl.ds(column * LINE, LINE)
    wait_bytes(own_stage, own_line.at[1])
    for i in range(1, columns):
        there = (column + i) % columns
        remote(own_stage.at[:, there], own_recv.at[here], own_plane, on_plane(i)).start()
    pltpu.make_async_copy(own_stage.at[:, column], own_recv.at[here], own_plane.at[1]).start()
    expand_gain(column_ref, gain_ref)

    wait_bytes(ref_stage, ref_line.at[1])
    for a, b in ((1, 1), (1, 0), (0, 1), (0, 0)):
        to_y = (place_y + a) % 2
        to_frame = (frame // 2 + b) % 2 * 2 + place_y
        copy = pltpu.make_async_remote_copy(
            src_ref=ref_stage.at[:, to_y],
            dst_ref=ref_recv.at[place_x, place_y],
            send_sem=ref_plane_send.at[0],
            recv_sem=ref_plane_recv.at[place_x],
            device_id={"frame": to_frame, "slab": (target_x * 2 + to_y) * LINE + depth_place},
            device_id_type=MESH,
        )
        if a == 0 and b == 0:
            pl.when(jnp.logical_not(keeps))(copy.start)
        else:
            copy.start()

    @pl.when(keeps)
    def _():
        pltpu.make_async_copy(
            ref_stage.at[:, place_y], ref_recv.at[place_x, place_y], ref_plane_recv.at[place_x]
        ).start()

    pl.when(has_previous)(to_next.wait_recv)
    pl.when(has_next)(to_previous.wait_recv)
    spread_depth(gains_ref, depth_ref)
    wait_bytes(own_recv, own_plane.at[1])
    unpack_own(own_recv, samples_ref)
    make_image(migration_ref, samples_ref, gain_ref, depth_ref, image_ref)
    pieces = [(place_x + i) % RING for i in (0, 1, 3, 2)]
    for x in pieces:
        copy = pltpu.make_async_remote_copy(
            src_ref=ref_recv.at[x, core],
            dst_ref=ref_recv.at[x, core],
            send_sem=pair_send.at[0],
            recv_sem=pair_recv.at[x],
            device_id={"frame": other_core, "slab": slab},
            device_id_type=MESH,
        )
        wait_bytes(ref_recv.at[x, core], ref_plane_recv.at[x])
        copy.start()
    for x in pieces:
        wait_bytes(ref_recv.at[x, 1 - core], pair_recv.at[x])
    reach = 2 * KX + 1
    reference_raw(migration_ref, ref_recv, total_ref, 0, reach * LY)
    reference_planes(total_ref, gain_ref, depth_ref, volume_ref, 0, reach)
    for bx in range(LX // KX):
        planes = min(KX, LX - reach)
        beside = None
        if planes:
            count = planes * LY * SEVERAL // 8

            def beside(i, reach=reach, count=count):
                start = pl.multiple_of(reach * LY + i * count, 32)
                reference_raw(migration_ref, ref_recv, total_ref, start, count)

        correlate(image_ref, volume_ref, shift_ref, parts_ref, bx * 8, bx * 8 + 8, beside)
        reference_planes(total_ref, gain_ref, depth_ref, volume_ref, reach, planes)
        reach += planes
    finish(parts_ref, coarse_ref, scores_ref, moved_ref)

    pl.when(has_next)(to_next.wait_send)
    pl.when(has_previous)(to_previous.wait_send)
    wait_bytes(quarters_ref.at[pl.ds(0, frames - 1)], quarter_sems.at[0])
    wait_bytes(own_stage.at[pl.ds(0, LINE - 1)], own_line.at[0])
    wait_bytes(ref_stage.at[pl.ds(0, LINE - 1)], ref_line.at[0])
    wait_bytes(own_recv.at[pl.ds(0, slabs - LINE)], own_plane.at[0])

    wait_bytes(own_recv, pair_send.at[0])

    @pl.when(keeps)
    def _():
        wait_bytes(own_recv.at[pl.ds(0, slabs // 4 * 3)], ref_plane_send.at[0])

    @pl.when(jnp.logical_not(keeps))
    def _():
        wait_bytes(own_recv, ref_plane_send.at[0])


def per_device(slabs, frames, element_data, migration, column_gain, depth_gain, coarse_shift, reference_frame):
    elements, _, depth = element_data.shape
    data = element_data.reshape(elements, depth)
    coarse = coarse_shift[:, 0].transpose(0, 1, 3, 2)
    vmem = pl.BlockSpec(memory_space=pltpu.VMEM)
    hbm = pl.BlockSpec(memory_space=pltpu.HBM)
    bf16, f32 = jnp.bfloat16, jnp.float32
    operands = (coarse, reference_frame, data, migration, column_gain.reshape(16, 128), depth_gain.reshape(1, -1))
    scores, moved = pl.pallas_call(
        functools.partial(fused_kernel, slabs, frames),
        out_shape=(
            jax.ShapeDtypeStruct((7, 4, 4, 8), f32),
            jax.ShapeDtypeStruct((3, 4, 4, 8), f32),
        ),
        in_specs=[hbm] * 6,
        out_specs=(vmem, vmem),
        scratch_shapes=[
            pltpu.SMEM(coarse.shape, jnp.int32),
            pltpu.SMEM(reference_frame.shape, jnp.int32),
            pltpu.VMEM(coarse.shape, jnp.int32),
            pltpu.VMEM((16, 128), f32),
            pltpu.VMEM((1, depth_gain.shape[0]), f32),
            pltpu.VMEM((elements, depth + 256), bf16),
            pltpu.VMEM(migration.shape, bf16),
            pltpu.VMEM((LINE, slabs // LINE, 8, 128), bf16),
            pltpu.VMEM((LINE, slabs // LINE, 8, 128), bf16),
            pltpu.VMEM((slabs, 8, 128), bf16),
            pltpu.VMEM((frames, elements, depth // frames + 256), bf16),
            pltpu.VMEM((LINE, slabs // frames // LINE, elements, 128), bf16),
            pltpu.VMEM((LINE, slabs // frames // LINE, elements, 128), bf16),
            pltpu.VMEM((RING, 2, LINE, elements, 128), bf16),
            pltpu.VMEM((3, 1, 128), f32),
            pltpu.VMEM((LX * LY, 128), f32),
            pltpu.VMEM((8, 128), f32),
            pltpu.VMEM((slabs * elements, 128), bf16),
            pltpu.VMEM((5, LX * LY, 128), f32),
            pltpu.VMEM((LX * LY, 128), f32),
            pltpu.VMEM((PLANES * YROWS, 128), f32),
            pltpu.VMEM((16 * 32 * 8, 128), f32),
            pltpu.SemaphoreType.DMA((7,)),
            pltpu.SemaphoreType.DMA((2,)),
            pltpu.SemaphoreType.DMA((2,)),
            pltpu.SemaphoreType.DMA((2,)),
            pltpu.SemaphoreType.DMA((2,)),
            pltpu.SemaphoreType.DMA((1,)),
            pltpu.SemaphoreType.DMA((RING,)),
            pltpu.SemaphoreType.DMA((1,)),
            pltpu.SemaphoreType.DMA((RING,)),
            pltpu.SemaphoreType.DMA((2,)),
            pltpu.SemaphoreType.DMA((2,)),
        ],
        compiler_params=pltpu.CompilerParams(
            collective_id=0, has_side_effects=True, vmem_limit_bytes=48 * 2**20
        ),
    )(*[pltpu.with_memory_space_constraint(x, pltpu.HBM) for x in operands])
    return scores.transpose(0, 1, 3, 2)[:, None], moved.transpose(0, 1, 3, 2)[:, None]


def solution(mesh):
    placed = (
        P("slab", "frame", None),
        P(),
        P(),
        P("slab"),
        P(None, "frame", None, None, "slab"),
        P(),
    )
    return jax.shard_map(
        functools.partial(per_device, mesh.shape["slab"], mesh.shape["frame"]),
        mesh=mesh,
        in_specs=placed,
        out_specs=(P(None, "frame", None, None, "slab"), P(None, "frame", None, None, "slab")),
        check_vma=False,
    )
```

```python
import functools

import jax
import jax.numpy as jnp
from jax import lax
from jax.experimental import pallas as pl
from jax.experimental.pallas import tpu as pltpu
from jax.sharding import PartitionSpec as P

LX, LY = 32, 64
KX, KY, KZ = 8, 8, 16
MARGIN = 9
YPAD = 16
YROWS = LY + 2 * YPAD
PLANES = LX + 2 * MARGIN
GROUP = 32
BLOCKS = 4
EPS = 1e-5
CELLS = KX * KY * KZ
ROWS = 1024
ELEMENTS = 16
RING = 4
LINE = 8
SEVERAL = 4
MESH = pl.DeviceIdType.MESH


def expand_gain(gain_ref, wide_ref):
    for i in range(gain_ref.shape[0]):
        row = jnp.broadcast_to(gain_ref[i : i + 1, :], (128, 128))
        wide_ref[pl.ds(i * 128, 128), :] = jnp.transpose(row)


def clear(volume_ref):
    def one(i, carry):
        rows = pl.ds(pl.multiple_of(i * YROWS, 8), YROWS)
        volume_ref[rows, :] = jnp.zeros((YROWS, 128), volume_ref.dtype)
        return carry

    lax.fori_loop(0, PLANES, one, 0)


def correlate(image_ref, volume_ref, shift_ref, parts_ref, begin, end, beside=None):
    lane = lax.broadcasted_iota(jnp.int32, (8, 128), 1)
    row = lax.broadcasted_iota(jnp.int32, (8, 128), 0)
    inside = lane % GROUP
    first = lane < GROUP
    third = lane < 3 * GROUP
    half = lane < 2 * GROUP
    center_mask = (inside >= 1) & (inside < 1 + KZ)
    before_mask = inside < KZ
    after_mask = (inside >= 2) & (inside < 2 + KZ)

    def one(g, carry):
        bx = g // 8
        by = g % 8
        starts, turns = [], []
        for b in range(BLOCKS):
            plane = bx * KX + shift_ref[0, bx, b, by] + MARGIN
            starts.append(plane * YROWS + by * KY + shift_ref[1, bx, b, by] + YPAD)
            turns.append((GROUP * b + 1 - MARGIN - KZ * b + 128 - shift_ref[2, bx, b, by]) % 128)

        def aligned(rows):
            turned = [pltpu.roll(volume_ref[rows(starts[b]), :], turns[b], 1) for b in range(BLOCKS)]
            return jnp.where(
                half,
                jnp.where(first, turned[0], turned[1]),
                jnp.where(third, turned[2], turned[3]),
            )

        base = bx * (KX * LY) + by * KY

        def kernel_plane(kind, p):
            return image_ref[kind, pl.ds(pl.multiple_of(base + p * LY, 8), 8), :]

        zero = jnp.zeros((8, 128), jnp.float32)
        cross = [zero] * 7
        core, own = zero, zero
        kernels = [kernel_plane(0, p) for p in range(KX)]
        for p in range(-1, KX + 1):
            window = aligned(lambda start: pl.ds(start + p * YROWS, 8))
            power = window * window
            if p == -1:
                ahead = power
            elif p == KX:
                behind = power
            else:
                own = own + kernels[p] * kernels[p]
                cross[0] += kernels[p] * window
                for kind in range(1, 5):
                    cross[2 + kind] += kernel_plane(kind, p) * window
                core = core + power
                if p == 0:
                    low_end = power
                if p == KX - 1:
                    high_end = power
                if 0 < p < KX - 1:
                    middle = power if p == 1 else middle + power
            if p < KX - 1:
                cross[1] += kernels[p + 1] * window
            if p > 0:
                cross[2] += kernels[p - 1] * window
        xm = ahead + low_end + middle
        xp = middle + high_end + behind
        low = aligned(lambda start: pl.ds(start - 1, KX, stride=YROWS))
        high = aligned(lambda start: pl.ds(start + KY, KX, stride=YROWS))
        cross[3] += image_ref[0, pl.ds(base, KX, stride=LY), :] * low
        cross[4] += image_ref[0, pl.ds(base + KY - 1, KX, stride=LY), :] * high
        ym = jnp.where(row < KY - 1, core, 0.0) + low * low
        yp = jnp.where(row > 0, core, 0.0) + high * high
        slots = cross + [own]
        for value, mask in (
            (core, center_mask),
            (xm, center_mask),
            (xp, center_mask),
            (ym, center_mask),
            (yp, center_mask),
            (core, before_mask),
            (core, after_mask),
        ):
            slots.append(jnp.where(mask, value, 0.0))
        slots.append(own)
        for k, value in enumerate(slots):
            parts_ref[pl.ds(pl.multiple_of(k * 256 + g * 8, 8), 8), :] = value
        return carry

    def several(i, carry):
        if beside is not None:
            beside(i - begin // SEVERAL)
        for j in range(SEVERAL):
            one(i * SEVERAL + j, carry)
        return carry

    lax.fori_loop(begin // SEVERAL, end // SEVERAL, several, 0)


def finish(parts_ref, coarse_ref, scores_ref, moved_ref):
    total = parts_ref[pl.ds(0, 512, stride=8), :]
    for s in range(1, 8):
        total = total + parts_ref[pl.ds(s, 512, stride=8), :]
    picked = lax.broadcasted_iota(jnp.int32, (8, 128), 1) // GROUP
    picked = (picked == lax.broadcasted_iota(jnp.int32, (8, 128), 0)).astype(jnp.float32)
    high = total.astype(jnp.bfloat16)
    low = (total - high.astype(jnp.float32)).astype(jnp.bfloat16)
    sums = [
        lax.dot_general(
            picked.astype(jnp.bfloat16),
            part,
            (((1,), (1,)), ((), ())),
            preferred_element_type=jnp.float32,
        )
        for part in (high, low)
    ]
    sums = (sums[0] + sums[1]) * (1.0 / CELLS)
    tiles = [sums[:, 128 * i : 128 * (i + 1)] for i in range(4)]
    lane = lax.broadcasted_iota(jnp.int32, (8, 128), 1)
    own = jnp.where(lane >= 3 * GROUP, tiles[3], 0.0)
    own = own + pltpu.roll(own, 64, 1)
    own = own + pltpu.roll(own, 32, 1) + EPS
    scored = [
        CELLS**0.5 * tiles[i] / jnp.sqrt(own * (tiles[2 + i] + EPS)) for i in range(2)
    ]
    scores = [
        scored[k // 4] if k % 4 == 0 else pltpu.roll(scored[k // 4], 128 - GROUP * (k % 4), 1)
        for k in range(7)
    ]

    def tile(value, bx):
        value = value if bx == 0 else pltpu.roll(value, 128 - 8 * bx, 1)
        return value[:BLOCKS, :8]

    for k in range(7):
        for bx in range(4):
            scores_ref[k, bx] = tile(scores[k], bx)
    for a in range(3):
        low, high = scores[1 + 2 * a], scores[2 + 2 * a]
        curvature = jnp.maximum(2.0 * scores[0] - low - high, 1.0)
        step = (high - low) / (2.0 * curvature)
        for bx in range(4):
            moved_ref[a, bx] = coarse_ref[a, bx].astype(jnp.float32) + tile(step, bx)


def scaled(migration_ref, samples, gain_ref, depth_row, i):
    rows = pl.ds(pl.multiple_of(i * ROWS, ROWS), ROWS)
    raw = jnp.dot(migration_ref[rows, :], samples, preferred_element_type=jnp.float32)
    return (raw * gain_ref[rows, :] * depth_row).astype(jnp.bfloat16).astype(jnp.float32)


def make_image(migration_ref, samples_ref, gain_ref, depth_ref, image_ref):
    def one(i, carry):
        rows = pl.ds(pl.multiple_of(i * ROWS, ROWS), ROWS)
        image = scaled(migration_ref, samples_ref[...], gain_ref, depth_ref[0:1, :], i)
        tiles = image.reshape(-1, 8, 128)
        row = lax.broadcasted_iota(jnp.int32, tiles.shape, 1)
        image_ref[0, rows, :] = image
        image_ref[1, rows, :] = jnp.where(row < 7, pltpu.roll(tiles, 7, 1), 0.0).reshape(-1, 128)
        image_ref[2, rows, :] = jnp.where(row > 0, pltpu.roll(tiles, 1, 1), 0.0).reshape(-1, 128)
        image_ref[3, rows, :] = pltpu.roll(image, 127, 1)
        image_ref[4, rows, :] = pltpu.roll(image, 1, 1)
        return carry

    lax.fori_loop(0, LX * LY // ROWS, one, 0)


def reference_raw(migration_ref, recv_ref, total_ref, start, count):
    samples = recv_ref[...].reshape(-1, 128)
    rows = pl.ds(start, count)
    total_ref[rows, :] = jnp.dot(migration_ref[rows, :], samples, preferred_element_type=jnp.float32)


def reference_planes(total_ref, gain_ref, depth_ref, volume_ref, start, count):
    for plane in range(start, start + count):
        rows = pl.ds(plane * LY, LY)
        ref = (total_ref[rows, :] * gain_ref[rows, :] * depth_ref[1:2, :]).astype(jnp.bfloat16)
        volume_ref[pl.ds((MARGIN + plane) * YROWS + YPAD, LY), :] = ref.astype(jnp.float32)


def place_of(column):
    return GROUP * (column // KZ) + 1 + column % KZ


def spread_depth(gains_ref, depth_ref):
    lane = lax.broadcasted_iota(jnp.int32, (8, 128), 1)
    left, here, right = [jnp.broadcast_to(gains_ref[i], (8, 128)) for i in range(3)]
    row = jnp.zeros((8, 128), jnp.float32)
    for b in range(BLOCKS):
        turned = pltpu.roll(here, (GROUP * b + 1 - KZ * b) % 128, 1)
        start = GROUP * b + 1
        row = jnp.where((lane >= start) & (lane < start + KZ), turned, row)
    sides = jnp.where(lane < MARGIN, pltpu.roll(left, 128 - 64 + MARGIN, 1), 0.0)
    sides = jnp.where((lane >= MARGIN) & (lane < MARGIN + 64), pltpu.roll(here, MARGIN, 1), sides)
    sides = jnp.where(
        (lane >= MARGIN + 64) & (lane < 2 * MARGIN + 64), pltpu.roll(right, MARGIN + 64, 1), sides
    )
    depth_ref[0:1, :] = row[0:1]
    depth_ref[1:2, :] = sides[0:1]


def pack_own(data_ref, send_ref):
    low = lax.broadcasted_iota(jnp.int32, (8, 128), 1) < 64
    for t in range(data_ref.shape[1] // 128 - 2):
        tile = data_ref[:, 128 * (t + 1) : 128 * (t + 2)].astype(jnp.float32)
        first, second = tile[:8], tile[8:]
        even = jnp.where(low, first, pltpu.roll(second, 64, 1))
        odd = jnp.where(low, pltpu.roll(first, 64, 1), second)
        send_ref[2 * t % LINE, 2 * t // LINE] = even.astype(jnp.bfloat16)
        send_ref[(2 * t + 1) % LINE, 2 * t // LINE] = odd.astype(jnp.bfloat16)


def unpack_own(recv_ref, samples_ref):
    row = lax.broadcasted_iota(jnp.int32, (128, 128), 0)
    lane = lax.broadcasted_iota(jnp.int32, (128, 128), 1)
    packed = recv_ref[...].astype(jnp.float32).reshape(-1, 128).astype(jnp.bfloat16)
    halves = []
    for start in (0, 64):
        column = row - start
        picked = (lane == place_of(column)) & (column >= 0) & (column < 64)
        picked = picked.astype(jnp.float32).astype(jnp.bfloat16)
        half = jnp.dot(packed, picked, preferred_element_type=jnp.float32)
        halves.append(half.reshape(-1, 8, 128))
    samples = jnp.concatenate(halves, axis=1).reshape(-1, 128)
    samples_ref[...] = samples.astype(jnp.bfloat16)


def pack_reference(quarters_ref, chosen, send_ref):
    lane = lax.broadcasted_iota(jnp.int32, (ELEMENTS, 128), 1)
    tiles = quarters_ref.shape[2] // 128
    parts = [quarters_ref[chosen, :, 128 * t : 128 * (t + 1)].astype(jnp.float32) for t in range(tiles)]
    for m in range(tiles - 2):
        for half in (0, 1):
            turn = MARGIN + 64 * half
            here, after = parts[m + half], parts[m + half + 1]
            window = jnp.where(lane < turn, pltpu.roll(here, turn, 1), pltpu.roll(after, turn, 1))
            place = 2 * m + half
            send_ref[place % LINE, place // LINE] = window.astype(jnp.bfloat16)


def remote(source, target, sems, device):
    return pltpu.make_async_remote_copy(
        src_ref=source,
        dst_ref=target,
        send_sem=sems.at[0],
        recv_sem=sems.at[1],
        device_id=device,
        device_id_type=MESH,
    )


def wait_bytes(ref, sem):
    pltpu.make_async_copy(ref, ref, sem).wait()


def fused_kernel(
    slabs, frames,
    shift_hbm, chosen_hbm, data_hbm, migration_hbm, column_hbm, gains_hbm,
    parts_ref,
    shift_ref, chosen_ref, column_ref, gains_in_ref,
    data_ref, migration_ref, own_send, own_stage, own_recv, quarters_ref, ref_send, ref_stage, ref_recv,
    gains_ref, gain_ref, depth_ref, samples_ref, image_ref, total_ref, volume_ref,
    local_sems, quarter_sems, own_line, own_plane, ref_line, ref_plane_send, ref_plane_recv,
    pair_send, pair_recv, to_next_sems, to_previous_sems,
):
    frame = lax.axis_index("frame")
    slab = lax.axis_index("slab")
    column, depth_place = slab // LINE, slab % LINE
    columns = slabs // LINE
    place_x, place_y, core = column // 2, column % 2, frame % 2
    other_core = frame + 1 - 2 * core
    def distance(of_frame):
        return jnp.where(of_frame == 0, 1, jnp.where(of_frame == 1, 3, jnp.where(of_frame == 2, 0, 2)))

    frame_at = (2, 0, 3, 1)
    target_x = (place_x + distance(frame)) % RING
    keeps = (target_x == place_x) & (core == place_y)
    has_next = slab < slabs - 1
    has_previous = slab > 0
    next_slab, previous_slab = (slab + 1) % slabs, (slab + slabs - 1) % slabs

    def on_line(i):
        return {"frame": frame, "slab": column * LINE + (depth_place + i) % LINE}

    def on_plane(i):
        return {"frame": frame, "slab": (column + i) % columns * LINE + depth_place}

    width = data_hbm.shape[1]
    loads = [
        pltpu.make_async_copy(start, end, local_sems.at[i])
        for i, (start, end) in enumerate(
            (
                (data_hbm, data_ref.at[:, pl.ds(128, width)]),
                (gains_hbm, gains_in_ref),
                (chosen_hbm, chosen_ref),
                (migration_hbm, migration_ref),
                (column_hbm, column_ref),
                (shift_hbm, shift_ref),
            )
        )
    ]
    for copy in loads:
        copy.start()
    gains_ref[...] = jnp.zeros(gains_ref.shape, gains_ref.dtype)

    barrier = pltpu.get_barrier_semaphore()

    def greet(device):
        pl.semaphore_signal(barrier, inc=1, device_id=device, device_id_type=MESH)

    for i in range(1, LINE):
        greet(on_line(i))
    for i in range(1, columns):
        greet(on_plane(i))
    for i in range(RING):
        x = (place_x + i) % RING
        device = {"frame": frame_at[-i % RING], "slab": (x * 2 + core) * LINE + depth_place}
        if i == 0:
            pl.when(jnp.logical_not(keeps))(functools.partial(greet, device))
        else:
            greet(device)
    for i in range(1, frames):
        greet({"frame": (frame + i) % frames, "slab": slab})
    pl.when(has_next)(lambda: greet({"frame": frame, "slab": next_slab}))
    pl.when(has_previous)(lambda: greet({"frame": frame, "slab": previous_slab}))

    data_ref[:, :128] = jnp.zeros((ELEMENTS, 128), data_ref.dtype)
    data_ref[:, -128:] = jnp.zeros((ELEMENTS, 128), data_ref.dtype)
    for copy in loads[:3]:
        copy.wait()
    gains_ref[1, :, :64] = gains_in_ref[...]
    pack_own(data_ref, own_send)
    greetings = (LINE - 1) + (columns - 1) + 4 - jnp.where(keeps, 1, 0) + (frames - 1)
    greetings = greetings + jnp.where(has_next, 1, 0) + jnp.where(has_previous, 1, 0)
    pl.semaphore_wait(barrier, greetings)

    quarter = width // frames

    def quarter_of(of_frame):
        place = (place_x + distance(of_frame)) % RING
        return data_ref.at[:, pl.ds(pl.multiple_of(place * quarter, 128), quarter + 256)]

    for i in range(1, frames):
        other = (frame + i) % frames
        remote(
            quarter_of(other), quarters_ref.at[frame], quarter_sems, {"frame": other, "slab": slab}
        ).start()
    pltpu.make_async_copy(quarter_of(frame), quarters_ref.at[frame], quarter_sems.at[1]).start()

    def along_line(send_ref, stage_ref, sems):
        for i in (4, 3, 5, 2, 6, 1, 7):
            there = (depth_place + i) % LINE
            remote(send_ref.at[there], stage_ref.at[depth_place], sems, on_line(i)).start()
        pltpu.make_async_copy(send_ref.at[depth_place], stage_ref.at[depth_place], sems.at[1]).start()

    along_line(own_send, own_stage, own_line)

    to_next = remote(gains_ref.at[1], gains_ref.at[0], to_next_sems, {"frame": frame, "slab": next_slab})
    to_previous = remote(
        gains_ref.at[1], gains_ref.at[2], to_previous_sems, {"frame": frame, "slab": previous_slab}
    )
    pl.when(has_next)(to_next.start)
    pl.when(has_previous)(to_previous.start)

    wait_bytes(quarters_ref, quarter_sems.at[1])
    pack_reference(quarters_ref, chosen_ref[0], ref_send)
    along_line(ref_send, ref_stage, ref_line)

    for copy in loads[3:]:
        copy.wait()
    clear(volume_ref)

    here = pl.ds(column * LINE, LINE)
    wait_bytes(own_stage, own_line.at[1])
    for i in range(1, columns):
        there = (column + i) % columns
        remote(own_stage.at[:, there], own_recv.at[here], own_plane, on_plane(i)).start()
    pltpu.make_async_copy(own_stage.at[:, column], own_recv.at[here], own_plane.at[1]).start()
    expand_gain(column_ref, gain_ref)

    wait_bytes(ref_stage, ref_line.at[1])
    for a, b in ((1, 1), (1, 0), (0, 1), (0, 0)):
        to_y = (place_y + a) % 2
        to_frame = (frame // 2 + b) % 2 * 2 + place_y
        copy = pltpu.make_async_remote_copy(
            src_ref=ref_stage.at[:, to_y],
            dst_ref=ref_recv.at[place_x, place_y],
            send_sem=ref_plane_send.at[0],
            recv_sem=ref_plane_recv.at[place_x],
            device_id={"frame": to_frame, "slab": (target_x * 2 + to_y) * LINE + depth_place},
            device_id_type=MESH,
        )
        if a == 0 and b == 0:
            pl.when(jnp.logical_not(keeps))(copy.start)
        else:
            copy.start()

    @pl.when(keeps)
    def _():
        pltpu.make_async_copy(
            ref_stage.at[:, place_y], ref_recv.at[place_x, place_y], ref_plane_recv.at[place_x]
        ).start()

    pl.when(has_previous)(to_next.wait_recv)
    pl.when(has_next)(to_previous.wait_recv)
    spread_depth(gains_ref, depth_ref)
    wait_bytes(own_recv, own_plane.at[1])
    unpack_own(own_recv, samples_ref)
    make_image(migration_ref, samples_ref, gain_ref, depth_ref, image_ref)
    pieces = [(place_x + i) % RING for i in (0, 1, 3, 2)]
    for x in pieces:
        copy = pltpu.make_async_remote_copy(
            src_ref=ref_recv.at[x, core],
            dst_ref=ref_recv.at[x, core],
            send_sem=pair_send.at[0],
            recv_sem=pair_recv.at[x],
            device_id={"frame": other_core, "slab": slab},
            device_id_type=MESH,
        )
        wait_bytes(ref_recv.at[x, core], ref_plane_recv.at[x])
        copy.start()
    for x in pieces:
        wait_bytes(ref_recv.at[x, 1 - core], pair_recv.at[x])
    reach = 2 * KX + 1
    reference_raw(migration_ref, ref_recv, total_ref, 0, reach * LY)
    reference_planes(total_ref, gain_ref, depth_ref, volume_ref, 0, reach)
    for bx in range(LX // KX):
        planes = min(KX, LX - reach)
        beside = None
        if planes:
            count = planes * LY * SEVERAL // 8

            def beside(i, reach=reach, count=count):
                start = pl.multiple_of(reach * LY + i * count, 32)
                reference_raw(migration_ref, ref_recv, total_ref, start, count)

        correlate(image_ref, volume_ref, shift_ref, parts_ref, bx * 8, bx * 8 + 8, beside)
        reference_planes(total_ref, gain_ref, depth_ref, volume_ref, reach, planes)
        reach += planes

    pl.when(has_next)(to_next.wait_send)
    pl.when(has_previous)(to_previous.wait_send)
    wait_bytes(quarters_ref.at[pl.ds(0, frames - 1)], quarter_sems.at[0])
    wait_bytes(own_stage.at[pl.ds(0, LINE - 1)], own_line.at[0])
    wait_bytes(ref_stage.at[pl.ds(0, LINE - 1)], ref_line.at[0])
    wait_bytes(own_recv.at[pl.ds(0, slabs - LINE)], own_plane.at[0])

    wait_bytes(own_recv, pair_send.at[0])

    @pl.when(keeps)
    def _():
        wait_bytes(own_recv.at[pl.ds(0, slabs // 4 * 3)], ref_plane_send.at[0])

    @pl.when(jnp.logical_not(keeps))
    def _():
        wait_bytes(own_recv, ref_plane_send.at[0])


def per_device(slabs, frames, element_data, migration, column_gain, depth_gain, coarse_shift, reference_frame):
    elements, _, depth = element_data.shape
    data = element_data.reshape(elements, depth)
    coarse = coarse_shift[:, 0].transpose(0, 1, 3, 2)
    vmem = pl.BlockSpec(memory_space=pltpu.VMEM)
    hbm = pl.BlockSpec(memory_space=pltpu.HBM)
    bf16, f32 = jnp.bfloat16, jnp.float32
    operands = (coarse, reference_frame, data, migration, column_gain.reshape(16, 128), depth_gain.reshape(1, -1))
    parts = pl.pallas_call(
        functools.partial(fused_kernel, slabs, frames),
        out_shape=jax.ShapeDtypeStruct((16 * 32 * 8, 128), f32),
        in_specs=[hbm] * 6,
        out_specs=vmem,
        scratch_shapes=[
            pltpu.SMEM(coarse.shape, jnp.int32),
            pltpu.SMEM(reference_frame.shape, jnp.int32),
            pltpu.VMEM((16, 128), f32),
            pltpu.VMEM((1, depth_gain.shape[0]), f32),
            pltpu.VMEM((elements, depth + 256), bf16),
            pltpu.VMEM(migration.shape, bf16),
            pltpu.VMEM((LINE, slabs // LINE, 8, 128), bf16),
            pltpu.VMEM((LINE, slabs // LINE, 8, 128), bf16),
            pltpu.VMEM((slabs, 8, 128), bf16),
            pltpu.VMEM((frames, elements, depth // frames + 256), bf16),
            pltpu.VMEM((LINE, slabs // frames // LINE, elements, 128), bf16),
            pltpu.VMEM((LINE, slabs // frames // LINE, elements, 128), bf16),
            pltpu.VMEM((RING, 2, LINE, elements, 128), bf16),
            pltpu.VMEM((3, 1, 128), f32),
            pltpu.VMEM((LX * LY, 128), f32),
            pltpu.VMEM((8, 128), f32),
            pltpu.VMEM((slabs * elements, 128), bf16),
            pltpu.VMEM((5, LX * LY, 128), f32),
            pltpu.VMEM((LX * LY, 128), f32),
            pltpu.VMEM((PLANES * YROWS, 128), f32),
            pltpu.SemaphoreType.DMA((6,)),
            pltpu.SemaphoreType.DMA((2,)),
            pltpu.SemaphoreType.DMA((2,)),
            pltpu.SemaphoreType.DMA((2,)),
            pltpu.SemaphoreType.DMA((2,)),
            pltpu.SemaphoreType.DMA((1,)),
            pltpu.SemaphoreType.DMA((RING,)),
            pltpu.SemaphoreType.DMA((1,)),
            pltpu.SemaphoreType.DMA((RING,)),
            pltpu.SemaphoreType.DMA((2,)),
            pltpu.SemaphoreType.DMA((2,)),
        ],
        compiler_params=pltpu.CompilerParams(
            collective_id=0, has_side_effects=True, vmem_limit_bytes=48 * 2**20
        ),
    )(*[pltpu.with_memory_space_constraint(x, pltpu.HBM) for x in operands])
    scores, moved = pl.pallas_call(
        finish,
        out_shape=(
            jax.ShapeDtypeStruct((7, 4, 4, 8), f32),
            jax.ShapeDtypeStruct((3, 4, 4, 8), f32),
        ),
        in_specs=[vmem, vmem],
        out_specs=(vmem, vmem),
        compiler_params=pltpu.CompilerParams(vmem_limit_bytes=8 * 2**20),
    )(parts, coarse)
    return scores.transpose(0, 1, 3, 2)[:, None], moved.transpose(0, 1, 3, 2)[:, None]


def solution(mesh):
    placed = (
        P("slab", "frame", None),
        P(),
        P(),
        P("slab"),
        P(None, "frame", None, None, "slab"),
        P(),
    )
    return jax.shard_map(
        functools.partial(per_device, mesh.shape["slab"], mesh.shape["frame"]),
        mesh=mesh,
        in_specs=placed,
        out_specs=(P(None, "frame", None, None, "slab"), P(None, "frame", None, None, "slab")),
        check_vma=False,
    )
```

```python
import functools

import jax
import jax.numpy as jnp
from jax import lax
from jax.experimental import pallas as pl
from jax.experimental.pallas import tpu as pltpu
from jax.sharding import PartitionSpec as P

LX, LY = 32, 64
KX, KY, KZ = 8, 8, 16
MARGIN = 9
YPAD = 16
YROWS = LY + 2 * YPAD
PLANES = LX + 2 * MARGIN
GROUP = 32
BLOCKS = 4
EPS = 1e-5
CELLS = KX * KY * KZ
ROWS = 1024
ELEMENTS = 16
RING = 4
LINE = 8
SEVERAL = 4
MESH = pl.DeviceIdType.MESH


def expand_gain(gain_ref, wide_ref):
    for i in range(gain_ref.shape[0]):
        row = jnp.broadcast_to(gain_ref[i : i + 1, :], (128, 128))
        wide_ref[pl.ds(i * 128, 128), :] = jnp.transpose(row)


def clear(volume_ref):
    def one(i, carry):
        rows = pl.ds(pl.multiple_of(i * YROWS, 8), YROWS)
        volume_ref[rows, :] = jnp.zeros((YROWS, 128), volume_ref.dtype)
        return carry

    lax.fori_loop(0, PLANES, one, 0)


def correlate(image_ref, volume_ref, shift_ref, parts_ref, begin, end, beside=None):
    lane = lax.broadcasted_iota(jnp.int32, (8, 128), 1)
    row = lax.broadcasted_iota(jnp.int32, (8, 128), 0)
    inside = lane % GROUP
    first = lane < GROUP
    third = lane < 3 * GROUP
    half = lane < 2 * GROUP
    center_mask = (inside >= 1) & (inside < 1 + KZ)
    before_mask = inside < KZ
    after_mask = (inside >= 2) & (inside < 2 + KZ)

    def one(g, carry):
        bx = g // 8
        by = g % 8
        starts, turns = [], []
        for b in range(BLOCKS):
            plane = bx * KX + shift_ref[0, bx, b, by] + MARGIN
            starts.append(plane * YROWS + by * KY + shift_ref[1, bx, b, by] + YPAD)
            turns.append((GROUP * b + 1 - MARGIN - KZ * b + 128 - shift_ref[2, bx, b, by]) % 128)

        def aligned(rows):
            turned = [pltpu.roll(volume_ref[rows(starts[b]), :], turns[b], 1) for b in range(BLOCKS)]
            return jnp.where(
                half,
                jnp.where(first, turned[0], turned[1]),
                jnp.where(third, turned[2], turned[3]),
            )

        base = bx * (KX * LY) + by * KY

        def kernel_plane(kind, p):
            return image_ref[kind, pl.ds(pl.multiple_of(base + p * LY, 8), 8), :]

        zero = jnp.zeros((8, 128), jnp.float32)
        cross = [zero] * 7
        core, own = zero, zero
        kernels = [kernel_plane(0, p) for p in range(KX)]
        for p in range(-1, KX + 1):
            window = aligned(lambda start: pl.ds(start + p * YROWS, 8))
            power = window * window
            if p == -1:
                ahead = power
            elif p == KX:
                behind = power
            else:
                own = own + kernels[p] * kernels[p]
                cross[0] += kernels[p] * window
                for kind in range(1, 5):
                    cross[2 + kind] += kernel_plane(kind, p) * window
                core = core + power
                if p == 0:
                    low_end = power
                if p == KX - 1:
                    high_end = power
                if 0 < p < KX - 1:
                    middle = power if p == 1 else middle + power
            if p < KX - 1:
                cross[1] += kernels[p + 1] * window
            if p > 0:
                cross[2] += kernels[p - 1] * window
        xm = ahead + low_end + middle
        xp = middle + high_end + behind
        low = aligned(lambda start: pl.ds(start - 1, KX, stride=YROWS))
        high = aligned(lambda start: pl.ds(start + KY, KX, stride=YROWS))
        cross[3] += image_ref[0, pl.ds(base, KX, stride=LY), :] * low
        cross[4] += image_ref[0, pl.ds(base + KY - 1, KX, stride=LY), :] * high
        ym = jnp.where(row < KY - 1, core, 0.0) + low * low
        yp = jnp.where(row > 0, core, 0.0) + high * high
        slots = cross + [own]
        for value, mask in (
            (core, center_mask),
            (xm, center_mask),
            (xp, center_mask),
            (ym, center_mask),
            (yp, center_mask),
            (core, before_mask),
            (core, after_mask),
        ):
            slots.append(jnp.where(mask, value, 0.0))
        slots.append(own)
        for k, value in enumerate(slots):
            parts_ref[pl.ds(pl.multiple_of(k * 256 + g * 8, 8), 8), :] = value
        return carry

    def several(i, carry):
        if beside is not None:
            beside(i - begin // SEVERAL)
        for j in range(SEVERAL):
            one(i * SEVERAL + j, carry)
        return carry

    lax.fori_loop(begin // SEVERAL, end // SEVERAL, several, 0)


def finish(parts_ref, coarse_ref, scores_ref, moved_ref):
    total = parts_ref[pl.ds(0, 512, stride=8), :]
    for s in range(1, 8):
        total = total + parts_ref[pl.ds(s, 512, stride=8), :]
    picked = lax.broadcasted_iota(jnp.int32, (8, 128), 1) // GROUP
    picked = (picked == lax.broadcasted_iota(jnp.int32, (8, 128), 0)).astype(jnp.float32)
    high = total.astype(jnp.bfloat16)
    low = (total - high.astype(jnp.float32)).astype(jnp.bfloat16)
    sums = [
        lax.dot_general(
            picked.astype(jnp.bfloat16),
            part,
            (((1,), (1,)), ((), ())),
            preferred_element_type=jnp.float32,
        )
        for part in (high, low)
    ]
    sums = (sums[0] + sums[1]) * (1.0 / CELLS)
    tiles = [sums[:, 128 * i : 128 * (i + 1)] for i in range(4)]
    lane = lax.broadcasted_iota(jnp.int32, (8, 128), 1)
    own = jnp.where(lane >= 3 * GROUP, tiles[3], 0.0)
    own = own + pltpu.roll(own, 64, 1)
    own = own + pltpu.roll(own, 32, 1) + EPS
    scored = [
        CELLS**0.5 * tiles[i] / jnp.sqrt(own * (tiles[2 + i] + EPS)) for i in range(2)
    ]
    scores = [
        scored[k // 4] if k % 4 == 0 else pltpu.roll(scored[k // 4], 128 - GROUP * (k % 4), 1)
        for k in range(7)
    ]

    def tile(value, bx):
        value = value if bx == 0 else pltpu.roll(value, 128 - 8 * bx, 1)
        return value[:BLOCKS, :8]

    for k in range(7):
        for bx in range(4):
            scores_ref[k, bx] = tile(scores[k], bx)
    for a in range(3):
        low, high = scores[1 + 2 * a], scores[2 + 2 * a]
        curvature = jnp.maximum(2.0 * scores[0] - low - high, 1.0)
        step = (high - low) / (2.0 * curvature)
        for bx in range(4):
            moved_ref[a, bx] = coarse_ref[a, bx].astype(jnp.float32) + tile(step, bx)


def scaled(migration_ref, samples, gain_ref, depth_row, i):
    rows = pl.ds(pl.multiple_of(i * ROWS, ROWS), ROWS)
    raw = jnp.dot(migration_ref[rows, :], samples, preferred_element_type=jnp.float32)
    return (raw * gain_ref[rows, :] * depth_row).astype(jnp.bfloat16).astype(jnp.float32)


def make_image(migration_ref, samples_ref, gain_ref, depth_ref, image_ref):
    def one(i, carry):
        rows = pl.ds(pl.multiple_of(i * ROWS, ROWS), ROWS)
        image = scaled(migration_ref, samples_ref[...], gain_ref, depth_ref[0:1, :], i)
        tiles = image.reshape(-1, 8, 128)
        row = lax.broadcasted_iota(jnp.int32, tiles.shape, 1)
        image_ref[0, rows, :] = image
        image_ref[1, rows, :] = jnp.where(row < 7, pltpu.roll(tiles, 7, 1), 0.0).reshape(-1, 128)
        image_ref[2, rows, :] = jnp.where(row > 0, pltpu.roll(tiles, 1, 1), 0.0).reshape(-1, 128)
        image_ref[3, rows, :] = pltpu.roll(image, 127, 1)
        image_ref[4, rows, :] = pltpu.roll(image, 1, 1)
        return carry

    lax.fori_loop(0, LX * LY // ROWS, one, 0)


def reference_raw(migration_ref, recv_ref, total_ref, start, count):
    samples = recv_ref[...].reshape(-1, 128)
    rows = pl.ds(start, count)
    total_ref[rows, :] = jnp.dot(migration_ref[rows, :], samples, preferred_element_type=jnp.float32)


def reference_planes(total_ref, gain_ref, depth_ref, volume_ref, start, count):
    for plane in range(start, start + count):
        rows = pl.ds(plane * LY, LY)
        ref = (total_ref[rows, :] * gain_ref[rows, :] * depth_ref[1:2, :]).astype(jnp.bfloat16)
        volume_ref[pl.ds((MARGIN + plane) * YROWS + YPAD, LY), :] = ref.astype(jnp.float32)


def place_of(column):
    return GROUP * (column // KZ) + 1 + column % KZ


def spread_depth(gains_ref, depth_ref):
    lane = lax.broadcasted_iota(jnp.int32, (8, 128), 1)
    left, here, right = [jnp.broadcast_to(gains_ref[i], (8, 128)) for i in range(3)]
    row = jnp.zeros((8, 128), jnp.float32)
    for b in range(BLOCKS):
        turned = pltpu.roll(here, (GROUP * b + 1 - KZ * b) % 128, 1)
        start = GROUP * b + 1
        row = jnp.where((lane >= start) & (lane < start + KZ), turned, row)
    sides = jnp.where(lane < MARGIN, pltpu.roll(left, 128 - 64 + MARGIN, 1), 0.0)
    sides = jnp.where((lane >= MARGIN) & (lane < MARGIN + 64), pltpu.roll(here, MARGIN, 1), sides)
    sides = jnp.where(
        (lane >= MARGIN + 64) & (lane < 2 * MARGIN + 64), pltpu.roll(right, MARGIN + 64, 1), sides
    )
    depth_ref[0:1, :] = row[0:1]
    depth_ref[1:2, :] = sides[0:1]


def pack_own(data_ref, send_ref):
    low = lax.broadcasted_iota(jnp.int32, (8, 128), 1) < 64
    for t in range(data_ref.shape[1] // 128 - 2):
        tile = data_ref[:, 128 * (t + 1) : 128 * (t + 2)].astype(jnp.float32)
        first, second = tile[:8], tile[8:]
        even = jnp.where(low, first, pltpu.roll(second, 64, 1))
        odd = jnp.where(low, pltpu.roll(first, 64, 1), second)
        send_ref[2 * t % LINE, 2 * t // LINE] = even.astype(jnp.bfloat16)
        send_ref[(2 * t + 1) % LINE, 2 * t // LINE] = odd.astype(jnp.bfloat16)


def unpack_own(recv_ref, samples_ref):
    row = lax.broadcasted_iota(jnp.int32, (128, 128), 0)
    lane = lax.broadcasted_iota(jnp.int32, (128, 128), 1)
    packed = recv_ref[...].astype(jnp.float32).reshape(-1, 128).astype(jnp.bfloat16)
    halves = []
    for start in (0, 64):
        column = row - start
        picked = (lane == place_of(column)) & (column >= 0) & (column < 64)
        picked = picked.astype(jnp.float32).astype(jnp.bfloat16)
        half = jnp.dot(packed, picked, preferred_element_type=jnp.float32)
        halves.append(half.reshape(-1, 8, 128))
    samples = jnp.concatenate(halves, axis=1).reshape(-1, 128)
    samples_ref[...] = samples.astype(jnp.bfloat16)


def pack_reference(quarters_ref, chosen, send_ref):
    lane = lax.broadcasted_iota(jnp.int32, (ELEMENTS, 128), 1)
    tiles = quarters_ref.shape[2] // 128
    parts = [quarters_ref[chosen, :, 128 * t : 128 * (t + 1)].astype(jnp.float32) for t in range(tiles)]
    for m in range(tiles - 2):
        for half in (0, 1):
            turn = MARGIN + 64 * half
            here, after = parts[m + half], parts[m + half + 1]
            window = jnp.where(lane < turn, pltpu.roll(here, turn, 1), pltpu.roll(after, turn, 1))
            place = 2 * m + half
            send_ref[place % LINE, place // LINE] = window.astype(jnp.bfloat16)


def remote(source, target, sems, device):
    return pltpu.make_async_remote_copy(
        src_ref=source,
        dst_ref=target,
        send_sem=sems.at[0],
        recv_sem=sems.at[1],
        device_id=device,
        device_id_type=MESH,
    )


def wait_bytes(ref, sem):
    pltpu.make_async_copy(ref, ref, sem).wait()


def fused_kernel(
    slabs, frames,
    shift_hbm, chosen_hbm, data_hbm, migration_hbm, column_hbm, gains_hbm,
    parts_ref,
    shift_ref, chosen_ref, column_ref, gains_in_ref,
    data_ref, migration_ref, own_send, own_stage, own_recv, quarters_ref, ref_send, ref_stage, ref_recv,
    gains_ref, gain_ref, depth_ref, samples_ref, image_ref, total_ref, volume_ref,
    local_sems, quarter_sems, own_line, own_plane, ref_line, ref_plane_send, ref_plane_recv,
    pair_send, pair_recv, to_next_sems, to_previous_sems,
):
    frame = lax.axis_index("frame")
    slab = lax.axis_index("slab")
    column, depth_place = slab // LINE, slab % LINE
    columns = slabs // LINE
    place_x, place_y, core = column // 2, column % 2, frame % 2
    other_core = frame + 1 - 2 * core
    def distance(of_frame):
        return jnp.where(of_frame == 0, 1, jnp.where(of_frame == 1, 3, jnp.where(of_frame == 2, 0, 2)))

    frame_at = (2, 0, 3, 1)
    target_x = (place_x + distance(frame)) % RING
    keeps = (target_x == place_x) & (core == place_y)
    has_next = slab < slabs - 1
    has_previous = slab > 0
    next_slab, previous_slab = (slab + 1) % slabs, (slab + slabs - 1) % slabs

    def on_line(i):
        return {"frame": frame, "slab": column * LINE + (depth_place + i) % LINE}

    def on_plane(i):
        return {"frame": frame, "slab": (column + i) % columns * LINE + depth_place}

    width = data_hbm.shape[1]
    loads = [
        pltpu.make_async_copy(start, end, local_sems.at[i])
        for i, (start, end) in enumerate(
            (
                (data_hbm, data_ref.at[:, pl.ds(128, width)]),
                (gains_hbm, gains_in_ref),
                (chosen_hbm, chosen_ref),
                (migration_hbm, migration_ref),
                (column_hbm, column_ref),
                (shift_hbm, shift_ref),
            )
        )
    ]
    for copy in loads:
        copy.start()
    gains_ref[...] = jnp.zeros(gains_ref.shape, gains_ref.dtype)

    barrier = pltpu.get_barrier_semaphore()

    def greet(device):
        pl.semaphore_signal(barrier, inc=1, device_id=device, device_id_type=MESH)

    for i in range(1, LINE):
        greet(on_line(i))
    for i in range(1, columns):
        greet(on_plane(i))
    for i in range(RING):
        x = (place_x + i) % RING
        device = {"frame": frame_at[-i % RING], "slab": (x * 2 + core) * LINE + depth_place}
        if i == 0:
            pl.when(jnp.logical_not(keeps))(functools.partial(greet, device))
        else:
            greet(device)
    for i in range(1, frames):
        greet({"frame": (frame + i) % frames, "slab": slab})
    pl.when(has_next)(lambda: greet({"frame": frame, "slab": next_slab}))
    pl.when(has_previous)(lambda: greet({"frame": frame, "slab": previous_slab}))

    data_ref[:, :128] = jnp.zeros((ELEMENTS, 128), data_ref.dtype)
    data_ref[:, -128:] = jnp.zeros((ELEMENTS, 128), data_ref.dtype)
    for copy in loads[:3]:
        copy.wait()
    gains_ref[1, :, :64] = gains_in_ref[...]
    pack_own(data_ref, own_send)
    greetings = (LINE - 1) + (columns - 1) + 4 - jnp.where(keeps, 1, 0) + (frames - 1)
    greetings = greetings + jnp.where(has_next, 1, 0) + jnp.where(has_previous, 1, 0)
    pl.semaphore_wait(barrier, greetings)

    quarter = width // frames

    def quarter_of(of_frame):
        place = (place_x + distance(of_frame)) % RING
        return data_ref.at[:, pl.ds(pl.multiple_of(place * quarter, 128), quarter + 256)]

    for i in range(1, frames):
        other = (frame + i) % frames
        remote(
            quarter_of(other), quarters_ref.at[frame], quarter_sems, {"frame": other, "slab": slab}
        ).start()
    pltpu.make_async_copy(quarter_of(frame), quarters_ref.at[frame], quarter_sems.at[1]).start()

    def along_line(send_ref, stage_ref, sems):
        for i in (4, 3, 5, 2, 6, 1, 7):
            there = (depth_place + i) % LINE
            remote(send_ref.at[there], stage_ref.at[depth_place], sems, on_line(i)).start()
        pltpu.make_async_copy(send_ref.at[depth_place], stage_ref.at[depth_place], sems.at[1]).start()

    along_line(own_send, own_stage, own_line)

    to_next = remote(gains_ref.at[1], gains_ref.at[0], to_next_sems, {"frame": frame, "slab": next_slab})
    to_previous = remote(
        gains_ref.at[1], gains_ref.at[2], to_previous_sems, {"frame": frame, "slab": previous_slab}
    )
    pl.when(has_next)(to_next.start)
    pl.when(has_previous)(to_previous.start)

    wait_bytes(quarters_ref, quarter_sems.at[1])
    pack_reference(quarters_ref, chosen_ref[0], ref_send)
    along_line(ref_send, ref_stage, ref_line)

    for copy in loads[3:]:
        copy.wait()
    clear(volume_ref)

    here = pl.ds(column * LINE, LINE)
    wait_bytes(own_stage, own_line.at[1])
    for i in range(1, columns):
        there = (column + i) % columns
        remote(own_stage.at[:, there], own_recv.at[here], own_plane, on_plane(i)).start()
    pltpu.make_async_copy(own_stage.at[:, column], own_recv.at[here], own_plane.at[1]).start()
    expand_gain(column_ref, gain_ref)

    wait_bytes(ref_stage, ref_line.at[1])
    for a, b in ((1, 1), (1, 0), (0, 1), (0, 0)):
        to_y = (place_y + a) % 2
        to_frame = (frame // 2 + b) % 2 * 2 + place_y
        copy = pltpu.make_async_remote_copy(
            src_ref=ref_stage.at[:, to_y],
            dst_ref=ref_recv.at[place_x, place_y],
            send_sem=ref_plane_send.at[0],
            recv_sem=ref_plane_recv.at[place_x],
            device_id={"frame": to_frame, "slab": (target_x * 2 + to_y) * LINE + depth_place},
            device_id_type=MESH,
        )
        if a == 0 and b == 0:
            pl.when(jnp.logical_not(keeps))(copy.start)
        else:
            copy.start()

    @pl.when(keeps)
    def _():
        pltpu.make_async_copy(
            ref_stage.at[:, place_y], ref_recv.at[place_x, place_y], ref_plane_recv.at[place_x]
        ).start()

    pl.when(has_previous)(to_next.wait_recv)
    pl.when(has_next)(to_previous.wait_recv)
    spread_depth(gains_ref, depth_ref)
    wait_bytes(own_recv, own_plane.at[1])
    unpack_own(own_recv, samples_ref)
    make_image(migration_ref, samples_ref, gain_ref, depth_ref, image_ref)
    pieces = [(place_x + i) % RING for i in (0, 1, 3, 2)]
    for x in pieces:
        copy = pltpu.make_async_remote_copy(
            src_ref=ref_recv.at[x, core],
            dst_ref=ref_recv.at[x, core],
            send_sem=pair_send.at[0],
            recv_sem=pair_recv.at[x],
            device_id={"frame": other_core, "slab": slab},
            device_id_type=MESH,
        )
        wait_bytes(ref_recv.at[x, core], ref_plane_recv.at[x])
        copy.start()
    for x in pieces:
        wait_bytes(ref_recv.at[x, 1 - core], pair_recv.at[x])
    reach = 2 * KX + 1
    reference_raw(migration_ref, ref_recv, total_ref, 0, reach * LY)
    reference_planes(total_ref, gain_ref, depth_ref, volume_ref, 0, reach)
    for bx in range(LX // KX):
        planes = min(KX, LX - reach)
        beside = None
        if planes:
            count = planes * LY * SEVERAL // 8

            def beside(i, reach=reach, count=count):
                start = pl.multiple_of(reach * LY + i * count, 32)
                reference_raw(migration_ref, ref_recv, total_ref, start, count)

        if beside is None:
            correlate(image_ref, volume_ref, shift_ref, parts_ref, bx * 8, 32)
            break
        correlate(image_ref, volume_ref, shift_ref, parts_ref, bx * 8, bx * 8 + 8, beside)
        reference_planes(total_ref, gain_ref, depth_ref, volume_ref, reach, planes)
        reach += planes

    pl.when(has_next)(to_next.wait_send)
    pl.when(has_previous)(to_previous.wait_send)
    wait_bytes(quarters_ref.at[pl.ds(0, frames - 1)], quarter_sems.at[0])
    wait_bytes(own_stage.at[pl.ds(0, LINE - 1)], own_line.at[0])
    wait_bytes(ref_stage.at[pl.ds(0, LINE - 1)], ref_line.at[0])
    wait_bytes(own_recv.at[pl.ds(0, slabs - LINE)], own_plane.at[0])

    wait_bytes(own_recv, pair_send.at[0])

    @pl.when(keeps)
    def _():
        wait_bytes(own_recv.at[pl.ds(0, slabs // 4 * 3)], ref_plane_send.at[0])

    @pl.when(jnp.logical_not(keeps))
    def _():
        wait_bytes(own_recv, ref_plane_send.at[0])


def per_device(slabs, frames, element_data, migration, column_gain, depth_gain, coarse_shift, reference_frame):
    elements, _, depth = element_data.shape
    data = element_data.reshape(elements, depth)
    coarse = coarse_shift[:, 0].transpose(0, 1, 3, 2)
    vmem = pl.BlockSpec(memory_space=pltpu.VMEM)
    hbm = pl.BlockSpec(memory_space=pltpu.HBM)
    bf16, f32 = jnp.bfloat16, jnp.float32
    operands = (coarse, reference_frame, data, migration, column_gain.reshape(16, 128), depth_gain.reshape(1, -1))
    parts = pl.pallas_call(
        functools.partial(fused_kernel, slabs, frames),
        out_shape=jax.ShapeDtypeStruct((16 * 32 * 8, 128), f32),
        in_specs=[hbm] * 6,
        out_specs=vmem,
        scratch_shapes=[
            pltpu.SMEM(coarse.shape, jnp.int32),
            pltpu.SMEM(reference_frame.shape, jnp.int32),
            pltpu.VMEM((16, 128), f32),
            pltpu.VMEM((1, depth_gain.shape[0]), f32),
            pltpu.VMEM((elements, depth + 256), bf16),
            pltpu.VMEM(migration.shape, bf16),
            pltpu.VMEM((LINE, slabs // LINE, 8, 128), bf16),
            pltpu.VMEM((LINE, slabs // LINE, 8, 128), bf16),
            pltpu.VMEM((slabs, 8, 128), bf16),
            pltpu.VMEM((frames, elements, depth // frames + 256), bf16),
            pltpu.VMEM((LINE, slabs // frames // LINE, elements, 128), bf16),
            pltpu.VMEM((LINE, slabs // frames // LINE, elements, 128), bf16),
            pltpu.VMEM((RING, 2, LINE, elements, 128), bf16),
            pltpu.VMEM((3, 1, 128), f32),
            pltpu.VMEM((LX * LY, 128), f32),
            pltpu.VMEM((8, 128), f32),
            pltpu.VMEM((slabs * elements, 128), bf16),
            pltpu.VMEM((5, LX * LY, 128), f32),
            pltpu.VMEM((LX * LY, 128), f32),
            pltpu.VMEM((PLANES * YROWS, 128), f32),
            pltpu.SemaphoreType.DMA((6,)),
            pltpu.SemaphoreType.DMA((2,)),
            pltpu.SemaphoreType.DMA((2,)),
            pltpu.SemaphoreType.DMA((2,)),
            pltpu.SemaphoreType.DMA((2,)),
            pltpu.SemaphoreType.DMA((1,)),
            pltpu.SemaphoreType.DMA((RING,)),
            pltpu.SemaphoreType.DMA((1,)),
            pltpu.SemaphoreType.DMA((RING,)),
            pltpu.SemaphoreType.DMA((2,)),
            pltpu.SemaphoreType.DMA((2,)),
        ],
        compiler_params=pltpu.CompilerParams(
            collective_id=0, has_side_effects=True, vmem_limit_bytes=48 * 2**20
        ),
    )(*[pltpu.with_memory_space_constraint(x, pltpu.HBM) for x in operands])
    scores, moved = pl.pallas_call(
        finish,
        out_shape=(
            jax.ShapeDtypeStruct((7, 4, 4, 8), f32),
            jax.ShapeDtypeStruct((3, 4, 4, 8), f32),
        ),
        in_specs=[vmem, vmem],
        out_specs=(vmem, vmem),
        compiler_params=pltpu.CompilerParams(vmem_limit_bytes=8 * 2**20),
    )(parts, coarse)
    return scores.transpose(0, 1, 3, 2)[:, None], moved.transpose(0, 1, 3, 2)[:, None]


def solution(mesh):
    placed = (
        P("slab", "frame", None),
        P(),
        P(),
        P("slab"),
        P(None, "frame", None, None, "slab"),
        P(),
    )
    return jax.shard_map(
        functools.partial(per_device, mesh.shape["slab"], mesh.shape["frame"]),
        mesh=mesh,
        in_specs=placed,
        out_specs=(P(None, "frame", None, None, "slab"), P(None, "frame", None, None, "slab")),
        check_vma=False,
    )
```

```python
import functools

import jax
import jax.numpy as jnp
from jax import lax
from jax.experimental import pallas as pl
from jax.experimental.pallas import tpu as pltpu
from jax.sharding import PartitionSpec as P

LX, LY = 32, 64
KX, KY, KZ = 8, 8, 16
MARGIN = 9
YPAD = 16
YROWS = LY + 2 * YPAD
PLANES = LX + 2 * MARGIN
GROUP = 32
BLOCKS = 4
EPS = 1e-5
CELLS = KX * KY * KZ
ROWS = 1024
ELEMENTS = 16
RING = 4
LINE = 8
SEVERAL = 4
MESH = pl.DeviceIdType.MESH


def expand_gain(gain_ref, wide_ref):
    for i in range(gain_ref.shape[0]):
        row = jnp.broadcast_to(gain_ref[i : i + 1, :], (128, 128))
        wide_ref[pl.ds(i * 128, 128), :] = jnp.transpose(row)


def clear(volume_ref):
    def one(i, carry):
        rows = pl.ds(pl.multiple_of(i * YROWS, 8), YROWS)
        volume_ref[rows, :] = jnp.zeros((YROWS, 128), volume_ref.dtype)
        return carry

    lax.fori_loop(0, PLANES, one, 0)


def correlate(image_ref, volume_ref, shift_ref, parts_ref, begin, end, beside=None):
    lane = lax.broadcasted_iota(jnp.int32, (8, 128), 1)
    row = lax.broadcasted_iota(jnp.int32, (8, 128), 0)
    inside = lane % GROUP
    first = lane < GROUP
    third = lane < 3 * GROUP
    half = lane < 2 * GROUP
    center_mask = (inside >= 1) & (inside < 1 + KZ)
    before_mask = inside < KZ
    after_mask = (inside >= 2) & (inside < 2 + KZ)

    def one(g, carry):
        bx = g // 8
        by = g % 8
        starts, turns = [], []
        for b in range(BLOCKS):
            plane = bx * KX + shift_ref[0, bx, b, by] + MARGIN
            starts.append(plane * YROWS + by * KY + shift_ref[1, bx, b, by] + YPAD)
            turns.append((GROUP * b + 1 - MARGIN - KZ * b + 128 - shift_ref[2, bx, b, by]) % 128)

        def aligned(rows):
            turned = [pltpu.roll(volume_ref[rows(starts[b]), :], turns[b], 1) for b in range(BLOCKS)]
            return jnp.where(
                half,
                jnp.where(first, turned[0], turned[1]),
                jnp.where(third, turned[2], turned[3]),
            )

        base = bx * (KX * LY) + by * KY

        def kernel_plane(kind, p):
            return image_ref[kind, pl.ds(pl.multiple_of(base + p * LY, 8), 8), :]

        zero = jnp.zeros((8, 128), jnp.float32)
        cross = [zero] * 7
        core, own = zero, zero
        kernels = [kernel_plane(0, p) for p in range(KX)]
        for p in range(-1, KX + 1):
            window = aligned(lambda start: pl.ds(start + p * YROWS, 8))
            power = window * window
            if p == -1:
                ahead = power
            elif p == KX:
                behind = power
            else:
                own = own + kernels[p] * kernels[p]
                cross[0] += kernels[p] * window
                for kind in range(1, 5):
                    cross[2 + kind] += kernel_plane(kind, p) * window
                core = core + power
                if p == 0:
                    low_end = power
                if p == KX - 1:
                    high_end = power
                if 0 < p < KX - 1:
                    middle = power if p == 1 else middle + power
            if p < KX - 1:
                cross[1] += kernels[p + 1] * window
            if p > 0:
                cross[2] += kernels[p - 1] * window
        xm = ahead + low_end + middle
        xp = middle + high_end + behind
        low = aligned(lambda start: pl.ds(start - 1, KX, stride=YROWS))
        high = aligned(lambda start: pl.ds(start + KY, KX, stride=YROWS))
        cross[3] += image_ref[0, pl.ds(base, KX, stride=LY), :] * low
        cross[4] += image_ref[0, pl.ds(base + KY - 1, KX, stride=LY), :] * high
        ym = jnp.where(row < KY - 1, core, 0.0) + low * low
        yp = jnp.where(row > 0, core, 0.0) + high * high
        slots = cross + [own]
        for value, mask in (
            (core, center_mask),
            (xm, center_mask),
            (xp, center_mask),
            (ym, center_mask),
            (yp, center_mask),
            (core, before_mask),
            (core, after_mask),
        ):
            slots.append(jnp.where(mask, value, 0.0))
        slots.append(own)
        for k, value in enumerate(slots):
            parts_ref[pl.ds(pl.multiple_of(k * 256 + g * 8, 8), 8), :] = value
        return carry

    def several(i, carry):
        if beside is not None:
            beside(i - begin // SEVERAL)
        for j in range(SEVERAL):
            one(i * SEVERAL + j, carry)
        return carry

    lax.fori_loop(begin // SEVERAL, end // SEVERAL, several, 0)


def finish(parts_ref, coarse_ref, scores_ref, moved_ref):
    total = parts_ref[pl.ds(0, 512, stride=8), :]
    for s in range(1, 8):
        total = total + parts_ref[pl.ds(s, 512, stride=8), :]
    picked = lax.broadcasted_iota(jnp.int32, (8, 128), 1) // GROUP
    picked = (picked == lax.broadcasted_iota(jnp.int32, (8, 128), 0)).astype(jnp.float32)
    high = total.astype(jnp.bfloat16)
    low = (total - high.astype(jnp.float32)).astype(jnp.bfloat16)
    sums = [
        lax.dot_general(
            picked.astype(jnp.bfloat16),
            part,
            (((1,), (1,)), ((), ())),
            preferred_element_type=jnp.float32,
        )
        for part in (high, low)
    ]
    sums = (sums[0] + sums[1]) * (1.0 / CELLS)
    tiles = [sums[:, 128 * i : 128 * (i + 1)] for i in range(4)]
    lane = lax.broadcasted_iota(jnp.int32, (8, 128), 1)
    own = jnp.where(lane >= 3 * GROUP, tiles[3], 0.0)
    own = own + pltpu.roll(own, 64, 1)
    own = own + pltpu.roll(own, 32, 1) + EPS
    scored = [
        CELLS**0.5 * tiles[i] / jnp.sqrt(own * (tiles[2 + i] + EPS)) for i in range(2)
    ]
    scores = [
        scored[k // 4] if k % 4 == 0 else pltpu.roll(scored[k // 4], 128 - GROUP * (k % 4), 1)
        for k in range(7)
    ]

    def tile(value, bx):
        value = value if bx == 0 else pltpu.roll(value, 128 - 8 * bx, 1)
        return value[:BLOCKS, :8]

    for k in range(7):
        for bx in range(4):
            scores_ref[k, bx] = tile(scores[k], bx)
    for a in range(3):
        low, high = scores[1 + 2 * a], scores[2 + 2 * a]
        curvature = jnp.maximum(2.0 * scores[0] - low - high, 1.0)
        step = (high - low) / (2.0 * curvature)
        for bx in range(4):
            moved_ref[a, bx] = coarse_ref[a, bx].astype(jnp.float32) + tile(step, bx)


def scaled(migration_ref, samples, gain_ref, depth_row, i):
    rows = pl.ds(pl.multiple_of(i * ROWS, ROWS), ROWS)
    raw = jnp.dot(migration_ref[rows, :], samples, preferred_element_type=jnp.float32)
    return (raw * gain_ref[rows, :] * depth_row).astype(jnp.bfloat16).astype(jnp.float32)


def make_image(migration_ref, samples_ref, gain_ref, depth_ref, image_ref):
    def one(i, carry):
        rows = pl.ds(pl.multiple_of(i * ROWS, ROWS), ROWS)
        image = scaled(migration_ref, samples_ref[...], gain_ref, depth_ref[0:1, :], i)
        tiles = image.reshape(-1, 8, 128)
        row = lax.broadcasted_iota(jnp.int32, tiles.shape, 1)
        image_ref[0, rows, :] = image
        image_ref[1, rows, :] = jnp.where(row < 7, pltpu.roll(tiles, 7, 1), 0.0).reshape(-1, 128)
        image_ref[2, rows, :] = jnp.where(row > 0, pltpu.roll(tiles, 1, 1), 0.0).reshape(-1, 128)
        image_ref[3, rows, :] = pltpu.roll(image, 127, 1)
        image_ref[4, rows, :] = pltpu.roll(image, 1, 1)
        return carry

    lax.fori_loop(0, LX * LY // ROWS, one, 0)


def reference_raw(migration_ref, recv_ref, total_ref, start, count):
    samples = recv_ref[...].reshape(-1, 128)
    rows = pl.ds(start, count)
    total_ref[rows, :] = jnp.dot(migration_ref[rows, :], samples, preferred_element_type=jnp.float32)


def reference_planes(total_ref, gain_ref, depth_ref, volume_ref, start, count):
    for plane in range(start, start + count):
        rows = pl.ds(plane * LY, LY)
        ref = (total_ref[rows, :] * gain_ref[rows, :] * depth_ref[1:2, :]).astype(jnp.bfloat16)
        volume_ref[pl.ds((MARGIN + plane) * YROWS + YPAD, LY), :] = ref.astype(jnp.float32)


def place_of(column):
    return GROUP * (column // KZ) + 1 + column % KZ


def spread_depth(gains_ref, depth_ref):
    lane = lax.broadcasted_iota(jnp.int32, (8, 128), 1)
    left, here, right = [jnp.broadcast_to(gains_ref[i], (8, 128)) for i in range(3)]
    row = jnp.zeros((8, 128), jnp.float32)
    for b in range(BLOCKS):
        turned = pltpu.roll(here, (GROUP * b + 1 - KZ * b) % 128, 1)
        start = GROUP * b + 1
        row = jnp.where((lane >= start) & (lane < start + KZ), turned, row)
    sides = jnp.where(lane < MARGIN, pltpu.roll(left, 128 - 64 + MARGIN, 1), 0.0)
    sides = jnp.where((lane >= MARGIN) & (lane < MARGIN + 64), pltpu.roll(here, MARGIN, 1), sides)
    sides = jnp.where(
        (lane >= MARGIN + 64) & (lane < 2 * MARGIN + 64), pltpu.roll(right, MARGIN + 64, 1), sides
    )
    depth_ref[0:1, :] = row[0:1]
    depth_ref[1:2, :] = sides[0:1]


def pack_own(data_ref, send_ref):
    low = lax.broadcasted_iota(jnp.int32, (8, 128), 1) < 64
    for t in range(data_ref.shape[1] // 128 - 2):
        tile = data_ref[:, 128 * (t + 1) : 128 * (t + 2)].astype(jnp.float32)
        first, second = tile[:8], tile[8:]
        even = jnp.where(low, first, pltpu.roll(second, 64, 1))
        odd = jnp.where(low, pltpu.roll(first, 64, 1), second)
        send_ref[2 * t % LINE, 2 * t // LINE] = even.astype(jnp.bfloat16)
        send_ref[(2 * t + 1) % LINE, 2 * t // LINE] = odd.astype(jnp.bfloat16)


def unpack_own(recv_ref, samples_ref):
    row = lax.broadcasted_iota(jnp.int32, (128, 128), 0)
    lane = lax.broadcasted_iota(jnp.int32, (128, 128), 1)
    packed = recv_ref[...].astype(jnp.float32).reshape(-1, 128).astype(jnp.bfloat16)
    halves = []
    for start in (0, 64):
        column = row - start
        picked = (lane == place_of(column)) & (column >= 0) & (column < 64)
        picked = picked.astype(jnp.float32).astype(jnp.bfloat16)
        half = jnp.dot(packed, picked, preferred_element_type=jnp.float32)
        halves.append(half.reshape(-1, 8, 128))
    samples = jnp.concatenate(halves, axis=1).reshape(-1, 128)
    samples_ref[...] = samples.astype(jnp.bfloat16)


def pack_reference(quarters_ref, chosen, send_ref):
    lane = lax.broadcasted_iota(jnp.int32, (ELEMENTS, 128), 1)
    tiles = quarters_ref.shape[2] // 128
    parts = [quarters_ref[chosen, :, 128 * t : 128 * (t + 1)].astype(jnp.float32) for t in range(tiles)]
    for m in range(tiles - 2):
        for half in (0, 1):
            turn = MARGIN + 64 * half
            here, after = parts[m + half], parts[m + half + 1]
            window = jnp.where(lane < turn, pltpu.roll(here, turn, 1), pltpu.roll(after, turn, 1))
            place = 2 * m + half
            send_ref[place % LINE, place // LINE] = window.astype(jnp.bfloat16)


def remote(source, target, sems, device):
    return pltpu.make_async_remote_copy(
        src_ref=source,
        dst_ref=target,
        send_sem=sems.at[0],
        recv_sem=sems.at[1],
        device_id=device,
        device_id_type=MESH,
    )


def wait_bytes(ref, sem):
    pltpu.make_async_copy(ref, ref, sem).wait()


def fused_kernel(
    slabs, frames,
    shift_hbm, chosen_hbm, data_hbm, migration_hbm, column_hbm, gains_hbm,
    parts_ref,
    shift_ref, chosen_ref, column_ref, gains_in_ref,
    data_ref, migration_ref, own_send, own_stage, own_recv, quarters_ref, ref_send, ref_stage, ref_recv,
    gains_ref, gain_ref, depth_ref, samples_ref, image_ref, total_ref, volume_ref,
    local_sems, quarter_sems, own_line, own_plane, ref_line, ref_plane_send, ref_plane_recv,
    to_next_sems, to_previous_sems,
):
    frame = lax.axis_index("frame")
    slab = lax.axis_index("slab")
    column, depth_place = slab // LINE, slab % LINE
    columns = slabs // LINE
    place_x, place_y, core = column // 2, column % 2, frame % 2
    def distance(of_frame):
        return jnp.where(of_frame == 0, 1, jnp.where(of_frame == 1, 3, jnp.where(of_frame == 2, 0, 2)))

    frame_at = (2, 0, 3, 1)
    target_x = (place_x + distance(frame)) % RING
    keeps = target_x == place_x
    has_next = slab < slabs - 1
    has_previous = slab > 0
    next_slab, previous_slab = (slab + 1) % slabs, (slab + slabs - 1) % slabs

    def on_line(i):
        return {"frame": frame, "slab": column * LINE + (depth_place + i) % LINE}

    def on_plane(i):
        return {"frame": frame, "slab": (column + i) % columns * LINE + depth_place}

    width = data_hbm.shape[1]
    loads = [
        pltpu.make_async_copy(start, end, local_sems.at[i])
        for i, (start, end) in enumerate(
            (
                (data_hbm, data_ref.at[:, pl.ds(128, width)]),
                (gains_hbm, gains_in_ref),
                (chosen_hbm, chosen_ref),
                (migration_hbm, migration_ref),
                (column_hbm, column_ref),
                (shift_hbm, shift_ref),
            )
        )
    ]
    for copy in loads:
        copy.start()
    gains_ref[...] = jnp.zeros(gains_ref.shape, gains_ref.dtype)

    barrier = pltpu.get_barrier_semaphore()

    def greet(device):
        pl.semaphore_signal(barrier, inc=1, device_id=device, device_id_type=MESH)

    for i in range(1, LINE):
        greet(on_line(i))
    for i in range(1, columns):
        greet(on_plane(i))
    for i in range(RING):
        for c in (1, 0):
            from_column = (place_x + i) % RING * 2 + (place_y + c) % 2
            device = {"frame": frame_at[-i % RING], "slab": from_column * LINE + depth_place}
            if i == 0 and c == 0:
                pl.when(jnp.logical_not(keeps))(functools.partial(greet, device))
            else:
                greet(device)
    for i in range(1, frames):
        greet({"frame": (frame + i) % frames, "slab": slab})
    pl.when(has_next)(lambda: greet({"frame": frame, "slab": next_slab}))
    pl.when(has_previous)(lambda: greet({"frame": frame, "slab": previous_slab}))

    data_ref[:, :128] = jnp.zeros((ELEMENTS, 128), data_ref.dtype)
    data_ref[:, -128:] = jnp.zeros((ELEMENTS, 128), data_ref.dtype)
    for copy in loads[:3]:
        copy.wait()
    gains_ref[1, :, :64] = gains_in_ref[...]
    pack_own(data_ref, own_send)
    greetings = (LINE - 1) + (columns - 1) + 8 - jnp.where(keeps, 1, 0) + (frames - 1)
    greetings = greetings + jnp.where(has_next, 1, 0) + jnp.where(has_previous, 1, 0)
    pl.semaphore_wait(barrier, greetings)

    quarter = width // frames

    def quarter_of(of_frame):
        place = (place_x + distance(of_frame)) % RING
        return data_ref.at[:, pl.ds(pl.multiple_of(place * quarter, 128), quarter + 256)]

    for i in range(1, frames):
        other = (frame + i) % frames
        remote(
            quarter_of(other), quarters_ref.at[frame], quarter_sems, {"frame": other, "slab": slab}
        ).start()
    pltpu.make_async_copy(quarter_of(frame), quarters_ref.at[frame], quarter_sems.at[1]).start()

    def along_line(send_ref, stage_ref, sems):
        for i in (4, 3, 5, 2, 6, 1, 7):
            there = (depth_place + i) % LINE
            remote(send_ref.at[there], stage_ref.at[depth_place], sems, on_line(i)).start()
        pltpu.make_async_copy(send_ref.at[depth_place], stage_ref.at[depth_place], sems.at[1]).start()

    along_line(own_send, own_stage, own_line)

    to_next = remote(gains_ref.at[1], gains_ref.at[0], to_next_sems, {"frame": frame, "slab": next_slab})
    to_previous = remote(
        gains_ref.at[1], gains_ref.at[2], to_previous_sems, {"frame": frame, "slab": previous_slab}
    )
    pl.when(has_next)(to_next.start)
    pl.when(has_previous)(to_previous.start)

    wait_bytes(quarters_ref, quarter_sems.at[1])
    pack_reference(quarters_ref, chosen_ref[0], ref_send)
    along_line(ref_send, ref_stage, ref_line)

    for copy in loads[3:]:
        copy.wait()
    clear(volume_ref)

    here = pl.ds(column * LINE, LINE)
    wait_bytes(own_stage, own_line.at[1])
    for i in range(1, columns):
        there = (column + i) % columns
        remote(own_stage.at[:, there], own_recv.at[here], own_plane, on_plane(i)).start()
    pltpu.make_async_copy(own_stage.at[:, column], own_recv.at[here], own_plane.at[1]).start()
    expand_gain(column_ref, gain_ref)

    wait_bytes(ref_stage, ref_line.at[1])
    for i in range(7, -1, -1):
        a, b, c = i // 4, i // 2 % 2, i % 2
        to_y = (place_y + a) % 2
        to_frame = (frame // 2 + b) % 2 * 2 + (core + c) % 2
        copy = pltpu.make_async_remote_copy(
            src_ref=ref_stage.at[:, to_y],
            dst_ref=ref_recv.at[place_x, place_y],
            send_sem=ref_plane_send.at[0],
            recv_sem=ref_plane_recv.at[place_x],
            device_id={"frame": to_frame, "slab": (target_x * 2 + to_y) * LINE + depth_place},
            device_id_type=MESH,
        )
        if i == 0:
            pl.when(jnp.logical_not(keeps))(copy.start)
        else:
            copy.start()

    @pl.when(keeps)
    def _():
        pltpu.make_async_copy(
            ref_stage.at[:, place_y], ref_recv.at[place_x, place_y], ref_plane_recv.at[place_x]
        ).start()

    pl.when(has_previous)(to_next.wait_recv)
    pl.when(has_next)(to_previous.wait_recv)
    spread_depth(gains_ref, depth_ref)
    wait_bytes(own_recv, own_plane.at[1])
    unpack_own(own_recv, samples_ref)
    make_image(migration_ref, samples_ref, gain_ref, depth_ref, image_ref)
    for x in range(RING):
        wait_bytes(ref_recv.at[x], ref_plane_recv.at[x])
    reach = 2 * KX + 1
    reference_raw(migration_ref, ref_recv, total_ref, 0, reach * LY)
    reference_planes(total_ref, gain_ref, depth_ref, volume_ref, 0, reach)
    for bx in range(LX // KX):
        planes = min(KX, LX - reach)
        beside = None
        if planes:
            count = planes * LY * SEVERAL // 8

            def beside(i, reach=reach, count=count):
                start = pl.multiple_of(reach * LY + i * count, 32)
                reference_raw(migration_ref, ref_recv, total_ref, start, count)

        if beside is None:
            correlate(image_ref, volume_ref, shift_ref, parts_ref, bx * 8, 32)
            break
        correlate(image_ref, volume_ref, shift_ref, parts_ref, bx * 8, bx * 8 + 8, beside)
        reference_planes(total_ref, gain_ref, depth_ref, volume_ref, reach, planes)
        reach += planes

    pl.when(has_next)(to_next.wait_send)
    pl.when(has_previous)(to_previous.wait_send)
    wait_bytes(quarters_ref.at[pl.ds(0, frames - 1)], quarter_sems.at[0])
    wait_bytes(own_stage.at[pl.ds(0, LINE - 1)], own_line.at[0])
    wait_bytes(ref_stage.at[pl.ds(0, LINE - 1)], ref_line.at[0])
    wait_bytes(own_recv.at[pl.ds(0, slabs - LINE)], own_plane.at[0])


    @pl.when(keeps)
    def _():
        wait_bytes(migration_ref.at[pl.ds(0, 112)], ref_plane_send.at[0])

    @pl.when(jnp.logical_not(keeps))
    def _():
        wait_bytes(ref_recv, ref_plane_send.at[0])


def per_device(slabs, frames, element_data, migration, column_gain, depth_gain, coarse_shift, reference_frame):
    elements, _, depth = element_data.shape
    data = element_data.reshape(elements, depth)
    coarse = coarse_shift[:, 0].transpose(0, 1, 3, 2)
    vmem = pl.BlockSpec(memory_space=pltpu.VMEM)
    hbm = pl.BlockSpec(memory_space=pltpu.HBM)
    bf16, f32 = jnp.bfloat16, jnp.float32
    operands = (coarse, reference_frame, data, migration, column_gain.reshape(16, 128), depth_gain.reshape(1, -1))
    parts = pl.pallas_call(
        functools.partial(fused_kernel, slabs, frames),
        out_shape=jax.ShapeDtypeStruct((16 * 32 * 8, 128), f32),
        in_specs=[hbm] * 6,
        out_specs=vmem,
        scratch_shapes=[
            pltpu.SMEM(coarse.shape, jnp.int32),
            pltpu.SMEM(reference_frame.shape, jnp.int32),
            pltpu.VMEM((16, 128), f32),
            pltpu.VMEM((1, depth_gain.shape[0]), f32),
            pltpu.VMEM((elements, depth + 256), bf16),
            pltpu.VMEM(migration.shape, bf16),
            pltpu.VMEM((LINE, slabs // LINE, 8, 128), bf16),
            pltpu.VMEM((LINE, slabs // LINE, 8, 128), bf16),
            pltpu.VMEM((slabs, 8, 128), bf16),
            pltpu.VMEM((frames, elements, depth // frames + 256), bf16),
            pltpu.VMEM((LINE, slabs // frames // LINE, elements, 128), bf16),
            pltpu.VMEM((LINE, slabs // frames // LINE, elements, 128), bf16),
            pltpu.VMEM((RING, 2, LINE, elements, 128), bf16),
            pltpu.VMEM((3, 1, 128), f32),
            pltpu.VMEM((LX * LY, 128), f32),
            pltpu.VMEM((8, 128), f32),
            pltpu.VMEM((slabs * elements, 128), bf16),
            pltpu.VMEM((5, LX * LY, 128), f32),
            pltpu.VMEM((LX * LY, 128), f32),
            pltpu.VMEM((PLANES * YROWS, 128), f32),
            pltpu.SemaphoreType.DMA((6,)),
            pltpu.SemaphoreType.DMA((2,)),
            pltpu.SemaphoreType.DMA((2,)),
            pltpu.SemaphoreType.DMA((2,)),
            pltpu.SemaphoreType.DMA((2,)),
            pltpu.SemaphoreType.DMA((1,)),
            pltpu.SemaphoreType.DMA((RING,)),
            pltpu.SemaphoreType.DMA((2,)),
            pltpu.SemaphoreType.DMA((2,)),
        ],
        compiler_params=pltpu.CompilerParams(
            collective_id=0, has_side_effects=True, vmem_limit_bytes=48 * 2**20
        ),
    )(*[pltpu.with_memory_space_constraint(x, pltpu.HBM) for x in operands])
    scores, moved = pl.pallas_call(
        finish,
        out_shape=(
            jax.ShapeDtypeStruct((7, 4, 4, 8), f32),
            jax.ShapeDtypeStruct((3, 4, 4, 8), f32),
        ),
        in_specs=[vmem, vmem],
        out_specs=(vmem, vmem),
        compiler_params=pltpu.CompilerParams(vmem_limit_bytes=8 * 2**20),
    )(parts, coarse)
    return scores.transpose(0, 1, 3, 2)[:, None], moved.transpose(0, 1, 3, 2)[:, None]


def solution(mesh):
    placed = (
        P("slab", "frame", None),
        P(),
        P(),
        P("slab"),
        P(None, "frame", None, None, "slab"),
        P(),
    )
    return jax.shard_map(
        functools.partial(per_device, mesh.shape["slab"], mesh.shape["frame"]),
        mesh=mesh,
        in_specs=placed,
        out_specs=(P(None, "frame", None, None, "slab"), P(None, "frame", None, None, "slab")),
        check_vma=False,
    )
```
